512 devices in a mesh: ctx: 32 (over y, x), tp: 8 (over z_hi, core), dp: 2 (over z_lo).
Axes of the slice: x: 4, y: 8, z: 8 (z_hi: 4, z_lo: 2; z = z_hi * 2 + z_lo), core: 2. Of those that a mesh axis runs over, the one named last changes fastest.
Arguments:
- q_light: bfloat16 [8192, 4096], P(('dp', 'ctx'), 'tp'), parts along dimension 0, may hold values from -1.4 to 1.4
- k_light: bfloat16 [8192, 4096], P(('dp', 'ctx'), 'tp'), parts along dimension 0, may hold values from -1.35 to 1.35
- v_light: bfloat16 [8192, 4096], P(('dp', 'ctx'), 'tp'), parts along dimension 0, may hold values from -6.2 to 6.2
- g_light: bfloat16 [8192, 4096], P(('dp', 'ctx'), 'tp'), parts along dimension 0, may hold values from -6 to 6
- log_decay: float32 [8192, 32], P(('dp', 'ctx'), 'tp'), parts along dimension 0, may hold values from -0.6 to 0
- q_soft: bfloat16 [8192, 4096], P(('dp', 'ctx'), 'tp'), parts along dimension 0, may hold values from -125 to 125
- k_soft: bfloat16 [8192, 1024], P(('dp', 'ctx'), 'tp'), parts along dimension 0, may hold values from -5 to 5
- v_soft: bfloat16 [8192, 1024], P(('dp', 'ctx'), 'tp'), parts along dimension 0, may hold values from -6 to 6
- g_soft: bfloat16 [8192, 4096], P(('dp', 'ctx'), 'tp'), parts along dimension 0, may hold values from -6 to 6
Outputs:
- o_light: bfloat16 [8192, 4096], P(('dp', 'ctx'), 'tp'), parts along dimension 0
- dq_light: bfloat16 [8192, 4096], P(('dp', 'ctx'), 'tp'), parts along dimension 0
- dk_light: bfloat16 [8192, 4096], P(('dp', 'ctx'), 'tp'), parts along dimension 0
- dv_light: bfloat16 [8192, 4096], P(('dp', 'ctx'), 'tp'), parts along dimension 0
- o_soft: bfloat16 [8192, 4096], P(('dp', 'ctx'), 'tp'), parts along dimension 0
- dq_soft: bfloat16 [8192, 4096], P(('dp', 'ctx'), 'tp'), parts along dimension 0
- dk_soft: bfloat16 [8192, 1024], P(('dp', 'ctx'), 'tp'), parts along dimension 0
- dv_soft: bfloat16 [8192, 1024], P(('dp', 'ctx'), 'tp'), parts along dimension 0
The draws below stay inside these ranges and needn't reach their ends.
There are 2 independent parts, one for each index of `dp`. The reference program is written for one: setup_inputs(seed, part) draws one part's arguments, and reference() takes and returns one part's arrays. A program takes and returns all parts, laid end to end along the dimension named above; each array names one. Nothing has to cross between parts.
All inputs are finite; a program needn't handle non-finite values.
Results may differ from the reference program's by a relative error of at most 0.015.
Values may be sent and summed in bfloat16 or wider, within the bound.
A program may use at most 128 MiB of HBM per device.

```python
import jax
import jax.numpy as jnp
from jax import lax

DH = 128
TOK_DEV = 128
SEQUENCE_TOKENS = 4096
HQ = 32
KVH = 8
LIGHTNING_HEADS = 32
GROUP = 4


def common_direction(key):
    return jnp.where(jax.random.uniform(jax.random.fold_in(key, 103), (KVH, DH)) < 0.5, -1.0, 1.0).astype(jnp.float32)


def keys_base(key):
    base = jnp.clip(jax.random.normal(jax.random.fold_in(key, 101), (SEQUENCE_TOKENS, KVH, DH), jnp.float32), -5.0, 5.0)
    row_index_list = jnp.arange(SEQUENCE_TOKENS)[:, None, None]
    return jnp.where(row_index_list == 0, 2.0 * common_direction(key)[None, :, :], base)


def light_layout(key):
    head_order = jax.random.permutation(jax.random.fold_in(key, 211), LIGHTNING_HEADS)
    gated_heads = head_order < max(1, LIGHTNING_HEADS // 4)
    block_total = SEQUENCE_TOKENS // TOK_DEV
    segment_span = max(1, block_total // 4)
    block_offset = jax.random.randint(jax.random.fold_in(key, 213), (), 0, segment_span)
    positions = jnp.arange(SEQUENCE_TOKENS)
    shifted_block = positions // TOK_DEV - block_offset
    closing_rows = (shifted_block % segment_span == 0) & (positions % TOK_DEV < min(6, TOK_DEV))
    segment_parity = shifted_block // segment_span % 2
    return (head_order, gated_heads, closing_rows, segment_parity)


def light_directions(key):
    signs = jnp.where(jax.random.uniform(jax.random.fold_in(key, 217), (2, LIGHTNING_HEADS, DH)) < 0.5, -1.0, 1.0).astype(jnp.float32)
    lower_half = jnp.arange(DH) < DH // 2
    first_direction = jnp.where(lower_half[None, :], signs[0], 0.0)
    second_direction = jnp.where(lower_half[None, :], 0.0, signs[0])
    return (first_direction, second_direction, signs[1])


def light_rows(noise, gated_heads, direction, strength):
    return noise + jnp.where(gated_heads[None, :, None], strength * direction, 0.0)


def draw_q_light(key, part):
    head_order, gated_heads, closing_rows, segment_parity = light_layout(key)
    first_direction, second_direction, value_direction = light_directions(key)
    key = jax.random.fold_in(key, 11)
    noise = jnp.clip(0.2 * jax.random.normal(key, (SEQUENCE_TOKENS, LIGHTNING_HEADS, DH), jnp.float32), -1.2, 1.2)
    direction = jnp.where(segment_parity[:, None, None] == 0, second_direction[None], first_direction[None])
    rows = light_rows(noise, gated_heads, direction, 0.2)
    return rows.reshape(SEQUENCE_TOKENS, LIGHTNING_HEADS * DH).astype(jnp.bfloat16)


def draw_k_light(key, part):
    head_order, gated_heads, closing_rows, segment_parity = light_layout(key)
    first_direction, second_direction, value_direction = light_directions(key)
    key = jax.random.fold_in(key, 13)
    noise = jnp.clip(0.2 * jax.random.normal(key, (SEQUENCE_TOKENS, LIGHTNING_HEADS, DH), jnp.float32), -1.2, 1.2)
    direction = jnp.where(segment_parity[:, None, None] == 0, first_direction[None], second_direction[None])
    rows = light_rows(noise, gated_heads, direction, 0.15)
    return rows.reshape(SEQUENCE_TOKENS, LIGHTNING_HEADS * DH).astype(jnp.bfloat16)


def draw_v_light(key, part):
    head_order, gated_heads, closing_rows, segment_parity = light_layout(key)
    first_direction, second_direction, value_direction = light_directions(key)
    key = jax.random.fold_in(key, 17)
    noise = jnp.clip(jax.random.normal(key, (SEQUENCE_TOKENS, LIGHTNING_HEADS, DH), jnp.float32), -6.0, 6.0)
    rows = light_rows(noise, gated_heads, value_direction[None], 0.2)
    return rows.reshape(SEQUENCE_TOKENS, LIGHTNING_HEADS * DH).astype(jnp.bfloat16)


def draw_k_soft(key, part):
    key_base = keys_base(key)
    return key_base.reshape(SEQUENCE_TOKENS, KVH * DH).astype(jnp.bfloat16)


def draw_q_soft(key, part):
    shared = jnp.repeat(common_direction(key), HQ // KVH, axis=0)[None, :, :] * (3.5 / DH ** 0.5)
    key = jax.random.fold_in(key, 5)
    first = jax.random.fold_in(key, 0)
    queries = jnp.clip(jax.random.normal(first, (SEQUENCE_TOKENS, HQ, DH), jnp.float32), -5.0, 5.0)
    queries = queries + shared
    return queries.reshape(SEQUENCE_TOKENS, HQ * DH).astype(jnp.bfloat16)


def draw_log_decay(key, part):
    head_order, gated_heads, closing_rows, segment_parity = light_layout(key)
    key = jax.random.fold_in(key, 7)
    context_shards = jax.random.split(key, 7)
    gated_count = max(1, LIGHTNING_HEADS // 4)
    fast_count = max(1, LIGHTNING_HEADS // 4)
    fast_heads = (head_order >= gated_count) & (head_order < gated_count + fast_count)
    slow_rate = jnp.exp(jax.random.uniform(context_shards[1], (LIGHTNING_HEADS,), jnp.float32, jnp.log(0.05), jnp.log(0.5))) / SEQUENCE_TOKENS
    fast_rate = 1.0 / jax.random.uniform(context_shards[2], (LIGHTNING_HEADS,), jnp.float32, 30.0, 50.0)
    decay_rate_floor = jnp.where(fast_heads, fast_rate, slow_rate)
    pieces = SEQUENCE_TOKENS // 16 + 1
    multiplier = jnp.exp(jax.random.uniform(context_shards[3], (pieces, LIGHTNING_HEADS), jnp.float32, -0.693, 0.693))
    row_index_list = jnp.arange(SEQUENCE_TOKENS)
    multiplier = multiplier[row_index_list // 16]
    spike_row_list = jax.random.randint(context_shards[4], (3,), 0, SEQUENCE_TOKENS)
    spike_loss_value = jnp.log(jax.random.uniform(context_shards[5], (3, LIGHTNING_HEADS), jnp.float32, 0.6, 0.8))
    spike_hit_count = (row_index_list[:, None] == spike_row_list[None, :]).astype(jnp.float32)
    spike_events = jnp.sum(spike_hit_count[:, :, None] * spike_loss_value[None, :, :], axis=1)
    closure_value = jax.random.uniform(context_shards[6], (SEQUENCE_TOKENS, LIGHTNING_HEADS), jnp.float32, -0.6, -0.52)
    drawn = -decay_rate_floor[None, :] * multiplier + spike_events
    closing_cells = closing_rows[:, None] & gated_heads[None, :]
    values = jnp.where(closing_cells, closure_value + spike_events, drawn)
    return jnp.maximum(values, -0.6)


def levels(key, shape, shards, low, largest):
    level = 1.0
    for position, shards_of in shards:
        steps = jax.random.uniform(jax.random.fold_in(jax.random.fold_in(key, 6), position), (shards_of,), jnp.float32, low / len(shards), largest / len(shards))
        level = level * jnp.repeat(jnp.exp(steps), shape[position] // shards_of).reshape((-1,) + (1,) * (len(shape) - 1 - position))
    return level


def centred(stream_key, dims, spread, limit, cuts=(), kind=jnp.bfloat16):
    values = spread * jax.random.normal(stream_key, dims, jnp.float32)
    if cuts:
        values = values * levels(stream_key, dims, cuts, -0.22, 0.18)
    return jnp.clip(values, -limit, limit).astype(kind)


def setup_inputs(seed: int = 0, part: int = 0) -> dict:
    key_list = jax.random.split(jax.random.key(seed), 10)
    part_keys = jax.random.split(jax.random.fold_in(key_list[9], part), 10)
    return {
        "q_light": draw_q_light(jax.random.fold_in(jax.random.fold_in(key_list[9], part), 71), part),
        "k_light": draw_k_light(jax.random.fold_in(jax.random.fold_in(key_list[9], part), 71), part),
        "v_light": draw_v_light(jax.random.fold_in(jax.random.fold_in(key_list[9], part), 71), part),
        "g_light": centred(part_keys[3], (SEQUENCE_TOKENS, LIGHTNING_HEADS * DH), 1.0, 6.0, ((0, 32), (1, 8))),
        "log_decay": draw_log_decay(jax.random.fold_in(jax.random.fold_in(key_list[9], part), 71), part),
        "q_soft": draw_q_soft(jax.random.fold_in(jax.random.fold_in(key_list[9], part), 71), part),
        "k_soft": draw_k_soft(jax.random.fold_in(jax.random.fold_in(key_list[9], part), 71), part),
        "v_soft": centred(part_keys[7], (SEQUENCE_TOKENS, KVH * DH), 1.0, 6.0, ((0, 32), (1, 8))),
        "g_soft": centred(part_keys[8], (SEQUENCE_TOKENS, HQ * DH), 1.0, 6.0, ((0, 32), (1, 8))),
    }


HIGHEST_PRECISION = lax.Precision.HIGHEST


def narrowed(values_in):
    return lax.optimization_barrier(values_in.astype(jnp.bfloat16)).astype(jnp.float32)


def light_local(queries, key_rows, value_rows, out_grad, log_gaps_in):
    row_count = queries.shape[0]
    scaling = queries.shape[2] ** -0.5
    cumulative = jnp.cumsum(log_gaps_in, axis=0)
    log_gaps = cumulative[:, None, :] - cumulative[None, :, :]
    causal = (jnp.arange(row_count)[:, None] >= jnp.arange(row_count)[None, :])[:, :, None]
    weights = jnp.where(causal, jnp.exp(jnp.where(causal, log_gaps, 0.0)), 0.0) * scaling
    weights = jnp.transpose(weights, (2, 0, 1))
    scores = jnp.einsum('thd,ihd->hti', queries, key_rows, precision=HIGHEST_PRECISION)
    mixing = narrowed(scores * weights)
    back_scores = jnp.einsum('thd,ihd->hti', out_grad, value_rows, precision=HIGHEST_PRECISION)
    back_mix = narrowed(back_scores * weights)
    out_intra = jnp.einsum('hti,ihd->thd', mixing, value_rows, precision=HIGHEST_PRECISION)
    value_intra = jnp.einsum('hti,thd->ihd', mixing, out_grad, precision=HIGHEST_PRECISION)
    query_intra = jnp.einsum('hti,ihd->thd', back_mix, key_rows, precision=HIGHEST_PRECISION)
    key_intra = jnp.einsum('hti,thd->ihd', back_mix, queries, precision=HIGHEST_PRECISION)
    decay_in = jnp.exp(cumulative)
    decay_out = jnp.exp(cumulative[-1][None, :] - cumulative)
    block_decay = decay_in[-1]
    state_local = jnp.einsum('ih,ihd,ihe->hde', decay_out, key_rows, value_rows, precision=HIGHEST_PRECISION)
    grad_local = jnp.einsum('th,thd,the->hde', decay_in, queries, out_grad, precision=HIGHEST_PRECISION)
    return out_intra, query_intra, key_intra, value_intra, decay_in, decay_out, block_decay, state_local, grad_local


def state_chain(block_decay, locals_in, backward):
    def advance(carried, item):
        return item[0][:, None, None] * carried + item[1], carried

    _, before = lax.scan(advance, jnp.zeros_like(locals_in[0]), (block_decay, locals_in), reverse=backward)
    return before


def lightning(q_light, k_light, v_light, g_light, log_decay):
    blocks = SEQUENCE_TOKENS // TOK_DEV
    shaped = (blocks, TOK_DEV, LIGHTNING_HEADS, DH)
    queries = q_light.astype(jnp.float32).reshape(shaped)
    key_rows = k_light.astype(jnp.float32).reshape(shaped)
    value_rows = v_light.astype(jnp.float32).reshape(shaped)
    out_grad = g_light.astype(jnp.float32).reshape(shaped)
    decays = log_decay.reshape(blocks, TOK_DEV, LIGHTNING_HEADS)
    parts = jax.vmap(light_local)(queries, key_rows, value_rows, out_grad, decays)
    out_intra, query_intra, key_intra, value_intra, decay_in, decay_out, block_decay, state_local, grad_local = parts
    prior_state = state_chain(block_decay, state_local, False)
    later_grad = state_chain(block_decay, grad_local, True)
    scaling = DH ** -0.5
    out_full = out_intra + scaling * decay_in[..., None] * jnp.einsum('bthd,bhde->bthe', queries, prior_state, precision=HIGHEST_PRECISION)
    query_grad = query_intra + scaling * decay_in[..., None] * jnp.einsum('bthe,bhde->bthd', out_grad, prior_state, precision=HIGHEST_PRECISION)
    key_grad = key_intra + scaling * decay_out[..., None] * jnp.einsum('bihe,bhde->bihd', value_rows, later_grad, precision=HIGHEST_PRECISION)
    value_grad = value_intra + scaling * decay_out[..., None] * jnp.einsum('bihd,bhde->bihe', key_rows, later_grad, precision=HIGHEST_PRECISION)
    flat = (SEQUENCE_TOKENS, LIGHTNING_HEADS * DH)
    return tuple(item.reshape(flat).astype(jnp.bfloat16) for item in (out_full, query_grad, key_grad, value_grad))


def soft_head(queries, key_rows, value_rows, out_grad):
    row_count = queries.shape[0]
    scaling = DH ** -0.5
    causal = jnp.arange(row_count)[:, None] >= jnp.arange(row_count)[None, :]
    scores = jnp.dot(queries, key_rows.T, preferred_element_type=jnp.float32) * scaling
    scores = jnp.where(causal, scores, -jnp.inf)
    maxima = jnp.max(scores, axis=1, keepdims=True)
    log_totals = maxima + jnp.log(jnp.sum(jnp.exp(scores - maxima), axis=1, keepdims=True))
    soft_weights = jnp.exp(scores - log_totals)
    soft_rounded = soft_weights.astype(jnp.bfloat16)
    out_full = jnp.dot(soft_rounded, value_rows, preferred_element_type=jnp.float32)
    row_dots = jnp.sum(out_grad.astype(jnp.float32) * out_full, axis=1, keepdims=True)
    weight_grad = jnp.dot(out_grad, value_rows.T, preferred_element_type=jnp.float32)
    score_grad = (scaling * soft_weights * (weight_grad - row_dots)).astype(jnp.bfloat16)
    query_grad = jnp.dot(score_grad, key_rows, preferred_element_type=jnp.float32)
    key_grad = jnp.dot(score_grad.T, queries, preferred_element_type=jnp.float32)
    value_grad = jnp.dot(soft_rounded.T, out_grad, preferred_element_type=jnp.float32)
    return out_full, query_grad, key_grad, value_grad


def soft_group(members):
    queries, key_rows, value_rows, out_grad = members
    outputs = []
    query_grads = []
    key_grad = jnp.zeros(key_rows.shape, jnp.float32)
    value_grad = jnp.zeros(value_rows.shape, jnp.float32)
    for member in range(queries.shape[0]):
        out_full, query_grad, key_part, value_part = soft_head(queries[member], key_rows, value_rows, out_grad[member])
        outputs.append(out_full)
        query_grads.append(query_grad)
        key_grad = key_grad + key_part
        value_grad = value_grad + value_part
    return jnp.stack(outputs), jnp.stack(query_grads), key_grad, value_grad


def reference(q_light, k_light, v_light, g_light, log_decay, q_soft, k_soft, v_soft, g_soft):
    o_light, dq_light, dk_light, dv_light = lightning(q_light, k_light, v_light, g_light, log_decay)
    queries = q_soft.reshape(SEQUENCE_TOKENS, KVH, GROUP, DH).transpose(1, 2, 0, 3)
    out_grad = g_soft.reshape(SEQUENCE_TOKENS, KVH, GROUP, DH).transpose(1, 2, 0, 3)
    key_rows = k_soft.reshape(SEQUENCE_TOKENS, KVH, DH).transpose(1, 0, 2)
    value_rows = v_soft.reshape(SEQUENCE_TOKENS, KVH, DH).transpose(1, 0, 2)
    outputs, query_grads, key_grads, value_grads = lax.map(soft_group, (queries, key_rows, value_rows, out_grad))
    o_soft = outputs.transpose(2, 0, 1, 3).reshape(SEQUENCE_TOKENS, HQ * DH).astype(jnp.bfloat16)
    dq_soft = query_grads.transpose(2, 0, 1, 3).reshape(SEQUENCE_TOKENS, HQ * DH).astype(jnp.bfloat16)
    dk_soft = key_grads.transpose(1, 0, 2).reshape(SEQUENCE_TOKENS, KVH * DH).astype(jnp.bfloat16)
    dv_soft = value_grads.transpose(1, 0, 2).reshape(SEQUENCE_TOKENS, KVH * DH).astype(jnp.bfloat16)
    return (o_light, dq_light, dk_light, dv_light, o_soft, dq_soft, dk_soft, dv_soft)
```

```python
import jax
import jax.numpy as jnp
from jax import lax
from jax.experimental import pallas as pl
from jax.experimental.pallas import tpu as pltpu
from jax.sharding import PartitionSpec as P

DH = 128
ROWS = 128
NX = 4
NY = 8
HEADS = 4
WIDE = HEADS * DH
SPAN = NX * ROWS
CHUNK = 64
SCALE = DH**-0.5
LOG2E = 1.4426950408889634
MASKED = -1e30
F32 = jnp.float32
BF16 = jnp.bfloat16


def mm(a, b):
    return jnp.dot(a, b, preferred_element_type=F32)


def mm_nt(a, b):
    return lax.dot_general(a, b, (((1,), (1,)), ((), ())), preferred_element_type=F32)


def mm_tn(a, b):
    return lax.dot_general(a, b, (((0,), (0,)), ((), ())), preferred_element_type=F32)


def push(src, dst, send, recv, target):
    return pltpu.make_async_remote_copy(
        src_ref=src,
        dst_ref=dst,
        send_sem=send,
        recv_sem=recv,
        device_id={"ctx": target},
        device_id_type=pl.DeviceIdType.MESH,
    )


def split_log(total):
    high = total.astype(BF16)
    rest = total - high.astype(F32)
    middle = rest.astype(BF16)
    low = (rest - middle.astype(F32)).astype(BF16)
    return high, middle, low


def join_log(ref, first):
    return (
        ref[first : first + 16, :].astype(F32)
        + ref[first + 16 : first + 32, :].astype(F32)
        + ref[first + 32 : first + 48, :].astype(F32)
    )[0:1, :]


def kernel(
    q_l, k_l, v_l, g_l, ld, q_s, k_s, v_s, g_s,
    o_l, dq_l, dk_l, dv_l, o_s, dq_s, dk_s, dv_s,
    qs, gs, kg, vg, e_ref, dp_ref, stat_m, stat_l, stat_t, dot_ref, wb_ref, ds_ref,
    out_t, dq_t, dkf, dkp, rbuf, dvp, vr, vsum, vfin, kfin, dks,
    lall, intra, lmsg, lin, ymsg, yin, cp, cg, lout, fin,
    kx_s, kx_r, kr_s, kr_r, vy_s, vy_r, vx_s, vx_r,
    l1_s, l1_r, y_s, y_r, l3_s, l3_r,
    dr_s, dr_r, du_s, du_r, dw_s, dw_r, kf_s, kf_r,
):
    me = lax.axis_index("ctx")
    y = lax.div(me, NX)
    x = lax.rem(me, NX)
    sigma = 1 - 2 * lax.rem(lax.axis_index("tp"), 2)

    def ring(value):
        return lax.rem(value + 2 * NY, NY)

    def at(yy, xx):
        return yy * NX + xx

    def col(step):
        return lax.rem(x + step + NX, NX)

    barrier = pltpu.get_barrier_semaphore()
    for dx in range(1, NX):
        pl.semaphore_signal(
            barrier, inc=1, device_id={"ctx": at(y, col(dx))},
            device_id_type=pl.DeviceIdType.MESH,
        )
    for dy in range(1, NY):
        pl.semaphore_signal(
            barrier, inc=1, device_id={"ctx": at(ring(y + dy), x)},
            device_id_type=pl.DeviceIdType.MESH,
        )
    pl.semaphore_wait(barrier, NX + NY - 2)

    def key_across(dx, owner):
        return push(k_s, kg.at[y, owner], kx_s.at[dx - 1], kx_r.at[dx - 1], at(y, col(dx)))

    def value_along(dy, owner):
        return push(
            v_s, vg.at[owner, x], vy_s.at[dy - 1], vy_r.at[dy - 1],
            at(jnp.minimum(y + dy, NY - 1), x),
        )

    def value_across(dy, dx, row, owner):
        return push(
            vg.at[row, x], vg.at[row, owner], vx_s.at[dy, dx - 1], vx_r.at[dy, dx - 1],
            at(y, col(dx)),
        )

    def key_ring(place, row, turn):
        return push(kg.at[row], kg.at[row], kr_s.at[place], kr_r.at[place], at(ring(y + turn), x))

    for dx in range(1, NX):
        key_across(dx, x).start()
    for dy in range(1, NY):
        @pl.when(y + dy < NY)
        def _():
            value_along(dy, y).start()
    kg[y, x] = k_s[...]
    vg[y, x] = v_s[...]
    for dx in range(1, NX):
        value_across(0, dx, y, x).start()

    for h in range(HEADS):
        part = slice(h * DH, (h + 1) * DH)
        qs[part, :] = q_s[:, part]
        gs[part, :] = g_s[:, part]
    for r in range(NY):
        stat_m[r] = jnp.full((8, WIDE), MASKED, F32)
        stat_l[r] = jnp.zeros((8, WIDE), F32)
        stat_t[r] = jnp.zeros((8, WIDE), F32)
    out_t[...] = jnp.zeros_like(out_t)
    dq_t[...] = jnp.zeros_like(dq_t)
    cp[...] = jnp.zeros_like(cp)
    cg[...] = jnp.zeros_like(cg)

    def soft_row(r, masked):
        top = jnp.full((8, WIDE), MASKED, F32)
        for b in range(NX):
            scores = mm_nt(kg[r, b], qs[...])
            if masked:
                key_at = lax.broadcasted_iota(jnp.int32, (ROWS, WIDE), 0) + b * ROWS
                query_at = lax.rem(lax.broadcasted_iota(jnp.int32, (ROWS, WIDE), 1), ROWS)
                scores = jnp.where(key_at <= query_at + x * ROWS, scores, MASKED)
            e_ref[r, b * ROWS : (b + 1) * ROWS, :] = scores
            top = jnp.maximum(top, jnp.max(scores.reshape(ROWS // 8, 8, WIDE), axis=0))
        top = jnp.max(top, axis=0, keepdims=True)
        stat_m[r] = jnp.broadcast_to(top, (8, WIDE))
        shift = top * (SCALE * LOG2E)

        def turn(i, total):
            rows = pl.ds(pl.multiple_of(i * CHUNK, CHUNK), CHUNK)
            grown = jnp.exp2(e_ref[r, rows, :] * (SCALE * LOG2E) - shift)
            e_ref[r, rows, :] = grown
            return total + jnp.sum(grown.reshape(CHUNK // 8, 8, WIDE), axis=0)

        total = lax.fori_loop(0, SPAN // CHUNK, turn, jnp.zeros((8, WIDE), F32))
        stat_l[r] = jnp.broadcast_to(jnp.sum(total, axis=0, keepdims=True), (8, WIDE))

    def light_head(h):
        cols = pl.ds(pl.multiple_of(h * DH, DH), DH)
        qh, kh, vh, gh = q_l[:, cols], k_l[:, cols], v_l[:, cols], g_l[:, cols]
        level = lall[:, cols]
        row_at = lax.broadcasted_iota(jnp.int32, (ROWS, ROWS), 0)
        causal = row_at >= lax.broadcasted_iota(jnp.int32, (ROWS, ROWS), 1)
        gaps = jnp.where(causal, level - level.T, 0.0)
        weights = jnp.where(causal, jnp.exp(gaps), 0.0) * SCALE
        mixing = (mm_nt(qh, kh) * weights).astype(BF16)
        back_mix = (mm_nt(gh, vh) * weights).astype(BF16)
        intra[0, :, cols] = mm(mixing, vh)
        intra[1, :, cols] = mm(back_mix, kh)
        intra[2, :, cols] = mm_tn(back_mix, qh)
        intra[3, :, cols] = mm_tn(mixing, gh)
        last = level[ROWS - 1 : ROWS, :]
        fading = (kh.astype(F32) * jnp.exp(last - level)).astype(BF16)
        entering = (qh.astype(F32) * jnp.exp(level)).astype(BF16)
        lmsg[h, 0:DH, :] = mm_tn(fading, vh).astype(BF16)
        lmsg[h, DH : 2 * DH, :] = mm_tn(entering, gh).astype(BF16)
        for n, term in enumerate(split_log(jnp.broadcast_to(last, (16, DH)))):
            lmsg[h, 2 * DH + 16 * n : 2 * DH + 16 * (n + 1), :] = term

    def light_send(h, owner):
        return push(lmsg.at[h], lin.at[owner], l1_s.at[h], l1_r.at[owner], at(y, h))

    for dx in range(1, NX):
        key_across(dx, col(-dx)).wait_recv()
    key_ring(1, y, sigma).start()
    key_ring(2, y, -sigma).start()
    soft_row(y, True)

    spread = jnp.concatenate(
        [jnp.broadcast_to(ld[:, h : h + 1], (ROWS, DH)) for h in range(HEADS)], axis=1
    )
    lower = (
        lax.broadcasted_iota(jnp.int32, (ROWS, ROWS), 0)
        >= lax.broadcasted_iota(jnp.int32, (ROWS, ROWS), 1)
    ).astype(F32)
    lall[...] = jnp.dot(
        lower, spread, precision=lax.Precision.HIGHEST, preferred_element_type=F32
    )

    def gather_turn(place, _):
        turn = sigma * (2 * lax.rem(place, 2) - 1)
        row = ring(y - turn * lax.div(place + 1, 2))
        key_ring(place, row, turn).wait_recv()

        @pl.when(place <= NY - 3)
        def _():
            key_ring(place + 2, row, turn).start()

        @pl.when(y - place >= 0)
        def _():
            push(
                v_s, vg.at[y - place, x], vy_s.at[place - 1], vy_r.at[place - 1], at(y - place, x)
            ).wait_recv()
            for dx in range(1, NX):
                value_across(place, dx, y - place, x).start()

        @pl.when(place <= HEADS)
        def _():
            h = place - 1
            light_head(h)

            @pl.when(h != x)
            def _():
                light_send(h, x).start()

            @pl.when(h == x)
            def _():
                lin[x] = lmsg[h]

        @pl.when(row < y)
        def _():
            soft_row(row, False)

        return 0

    lax.fori_loop(1, NY, gather_turn, 0)

    for h in range(NX):
        @pl.when(h != x)
        def _():
            push(lmsg.at[h], lin.at[h], l1_s.at[h], l1_r.at[h], at(y, h)).wait_recv()
    levels = [join_log(lin.at[b], 2 * DH) for b in range(NX)]
    row_state = lin[0, 0:DH, :].astype(F32)
    for b in range(1, NX):
        row_state = jnp.exp(levels[b]) * row_state + lin[b, 0:DH, :].astype(F32)
    row_grad = lin[NX - 1, DH : 2 * DH, :].astype(F32)
    for b in range(NX - 2, -1, -1):
        row_grad = jnp.exp(levels[b]) * row_grad + lin[b, DH : 2 * DH, :].astype(F32)
    row_level = jnp.broadcast_to(levels[0] + levels[1] + levels[2] + levels[3], (16, DH))
    ymsg[0, 0:DH, :] = row_state.astype(BF16)
    ymsg[1, 0:DH, :] = row_grad.astype(BF16)
    for n, term in enumerate(split_log(row_level)):
        ymsg[0, DH + 16 * n : DH + 16 * (n + 1), :] = term
        ymsg[1, DH + 16 * n : DH + 16 * (n + 1), :] = term

    def state_along(dy, owner):
        kind = jnp.where(y + dy < NY, 0, 1)
        return push(
            ymsg.at[kind], yin.at[owner], y_s.at[dy - 1], y_r.at[dy - 1], at(ring(y + dy), x)
        )

    for dy in range(1, NY):
        state_along(dy, y).start()

    def value_turn(dy, _):
        row = y - dy
        for dx in range(1, NX):
            value_across(dy, dx, row, col(-dx)).wait_recv()
        total = jnp.zeros((8, WIDE), F32)
        for b in range(NX):
            grads = mm_nt(vg[row, b], gs[...])
            dp_ref[row, b * ROWS : (b + 1) * ROWS, :] = grads
            weighed = grads * e_ref[row, b * ROWS : (b + 1) * ROWS, :]
            total = total + jnp.sum(weighed.reshape(ROWS // 8, 8, WIDE), axis=0)
        stat_t[row] = jnp.broadcast_to(jnp.sum(total, axis=0, keepdims=True), (8, WIDE))
        return 0

    lax.fori_loop(0, y + 1, value_turn, 0)

    top = stat_m[0]
    for r in range(1, NY):
        top = jnp.maximum(top, stat_m[r])
    total = jnp.zeros((8, WIDE), F32)
    dots = jnp.zeros((8, WIDE), F32)
    for r in range(NY):
        factor = jnp.exp2((stat_m[r] - top) * (SCALE * LOG2E))
        total = total + factor * stat_l[r]
        dots = dots + factor * stat_t[r]
        stat_m[r] = factor
    inverse = 1.0 / total
    dot_ref[...] = dots * inverse
    for r in range(NY):
        stat_l[r] = stat_m[r] * inverse

    for dy in range(1, NY):
        state_along(dy, ring(y - dy)).wait_recv()
    for yy in range(NY):
        @pl.when(yy < y)
        def _():
            cp[...] = jnp.exp(join_log(yin.at[yy], DH)) * cp[...] + yin[yy, 0:DH, :].astype(F32)
    for yy in range(NY - 1, -1, -1):
        @pl.when(yy > y)
        def _():
            cg[...] = jnp.exp(join_log(yin.at[yy], DH)) * cg[...] + yin[yy, 0:DH, :].astype(F32)
    carried = cp[...]
    for b in range(NX):
        lout[b, 0:DH, :] = carried.astype(BF16)
        carried = jnp.exp(join_log(lin.at[b], 2 * DH)) * carried + lin[b, 0:DH, :].astype(F32)
    carried = cg[...]
    for b in range(NX - 1, -1, -1):
        lout[b, DH : 2 * DH, :] = carried.astype(BF16)
        carried = jnp.exp(join_log(lin.at[b], 2 * DH)) * carried + lin[b, DH : 2 * DH, :].astype(F32)

    def state_back(b, owner):
        return push(lout.at[b], fin.at[owner], l3_s.at[b], l3_r.at[owner], at(y, b))

    for b in range(NX):
        @pl.when(b != x)
        def _():
            state_back(b, x).start()
    fin[x] = lout[x]

    def grad_ring(place, turn):
        return push(
            dkp.at[place], rbuf.at[place], dr_s.at[place], dr_r.at[place], at(ring(y + turn), x)
        )

    def dv_across(row, dx):
        return push(
            dvp.at[row, col(dx)], vr.at[row, dx - 1], du_s.at[row, dx - 1], du_r.at[row, dx - 1],
            at(y, col(dx)),
        )

    def dv_along(row, owner):
        return push(vsum.at[row], vfin.at[owner], dw_s.at[row], dw_r.at[owner], at(row, x))

    def dv_sum(row):
        for dx in range(1, NX):
            dv_across(row, dx).wait_recv()
        return (
            dvp[row, x].astype(F32)
            + vr[row, 0].astype(F32)
            + vr[row, 1].astype(F32)
            + vr[row, 2].astype(F32)
        )

    def place_row(place):
        forth = (lax.rem(place, 2) == 1) | (place == 0)
        turn = jnp.where(forth, sigma, -sigma)
        return turn, ring(y + turn * (4 - lax.div(place + 1, 2)))

    def back_turn(place, _):
        turn, row = place_row(place)

        @pl.when(row <= y)
        def _():
            def weigh(i, _):
                rows = pl.ds(pl.multiple_of(i * CHUNK, CHUNK), CHUNK)
                weights = e_ref[row, rows, :] * stat_l[row, 0:1, :]
                wb_ref[rows, :] = weights.astype(BF16)
                ds_ref[rows, :] = (weights * (dp_ref[row, rows, :] - dot_ref[0:1, :])).astype(BF16)
                return 0

            lax.fori_loop(0, SPAN // CHUNK, weigh, 0)
            dvp[row] = mm(wb_ref[...], gs[...]).astype(BF16).reshape(NX, ROWS, DH)
            for dx in range(1, NX):
                dv_across(row, dx).start()
            dkf[...] = (mm(ds_ref[...], qs[...]) * SCALE).reshape(NX, ROWS, DH)

        @pl.when(row > y)
        def _():
            dkf[...] = jnp.zeros_like(dkf)

        @pl.when((place != 0) & (place != 2) & (place != NY - 1))
        def _():
            before = jnp.where(place == 1, 0, place - 2)
            grad_ring(before, turn).wait_recv()
            dkf[...] += rbuf[before].astype(F32)

        @pl.when(place < NY - 1)
        def _():
            dkp[place] = dkf[...].astype(BF16)
            grad_ring(place, turn).start()

        @pl.when(row <= y)
        def _():
            out_t[...] += mm_tn(vg[row].reshape(SPAN, DH), wb_ref[...])
            dq_t[...] += mm_tn(kg[row].reshape(SPAN, DH), ds_ref[...])

        @pl.when(place >= 1)
        def _():
            _, before_row = place_row(place - 1)

            @pl.when(before_row < y)
            def _():
                vsum[before_row] = dv_sum(before_row).astype(BF16)
                dv_along(before_row, y).start()

        return 0

    lax.fori_loop(0, NY, back_turn, 0)

    for b in range(NX):
        @pl.when(b != x)
        def _():
            push(lout.at[b], fin.at[b], l3_s.at[b], l3_r.at[b], at(y, b)).wait_recv()

    def light_out(h, _):
        cols = pl.ds(pl.multiple_of(h * DH, DH), DH)
        qh, kh, vh, gh = q_l[:, cols], k_l[:, cols], v_l[:, cols], g_l[:, cols]
        level = lall[:, cols]
        entering = jnp.exp(level) * SCALE
        fading = jnp.exp(level[ROWS - 1 : ROWS, :] - level) * SCALE
        prior = fin[h, 0:DH, :]
        later = fin[h, DH : 2 * DH, :]
        o_l[:, cols] = (intra[0, :, cols] + entering * mm(qh, prior)).astype(BF16)
        dq_l[:, cols] = (intra[1, :, cols] + entering * mm_nt(gh, prior)).astype(BF16)
        dk_l[:, cols] = (intra[2, :, cols] + fading * mm_nt(vh, later)).astype(BF16)
        dv_l[:, cols] = (intra[3, :, cols] + fading * mm(kh, later)).astype(BF16)
        return 0

    lax.fori_loop(0, HEADS, light_out, 0)

    grad_ring(NY - 3, sigma).wait_recv()
    grad_ring(NY - 2, sigma).wait_recv()
    dkf[...] += rbuf[NY - 3].astype(F32) + rbuf[NY - 2].astype(F32)
    dks[...] = dkf[...].astype(BF16)

    def dk_across(dx):
        return push(
            dks.at[col(dx)], kfin.at[dx - 1], kf_s.at[dx - 1], kf_r.at[dx - 1], at(y, col(dx))
        )

    for dx in range(1, NX):
        dk_across(dx).start()

    for h in range(HEADS):
        part = slice(h * DH, (h + 1) * DH)
        o_s[:, part] = out_t[:, part].T.astype(BF16)
        dq_s[:, part] = (dq_t[:, part].T * SCALE).astype(BF16)

    cp[...] = dv_sum(y)
    for yy in range(1, NY):
        @pl.when(yy > y)
        def _():
            push(vsum.at[yy], vfin.at[yy], dw_s.at[yy], dw_r.at[yy], at(yy, x)).wait_recv()
            cp[...] += vfin[yy].astype(F32)
    dv_s[...] = cp[...].astype(BF16)

    for dx in range(1, NX):
        dk_across(dx).wait_recv()
    dk_s[...] = (
        dkf[x] + kfin[0].astype(F32) + kfin[1].astype(F32) + kfin[2].astype(F32)
    ).astype(BF16)

    for dx in range(1, NX):
        key_across(dx, x).wait_send()
        dk_across(dx).wait_send()
    for dy in range(1, NY):
        state_along(dy, y).wait_send()
        key_ring(dy, y, sigma).wait_send()
        grad_ring(dy - 1, sigma).wait_send()

        @pl.when(y + dy < NY)
        def _():
            value_along(dy, y).wait_send()

        @pl.when(dy - 1 < y)
        def _():
            dv_along(dy - 1, y).wait_send()
    for b in range(NX):
        @pl.when(b != x)
        def _():
            light_send(b, x).wait_send()
            state_back(b, x).wait_send()
    for dy in range(NY):
        @pl.when(dy <= y)
        def _():
            for dx in range(1, NX):
                value_across(dy, dx, y, x).wait_send()
                dv_across(dy, dx).wait_send()


def shards(q_light, k_light, v_light, g_light, log_decay, q_soft, k_soft, v_soft, g_soft):
    dma = pltpu.SemaphoreType.DMA
    wide = jax.ShapeDtypeStruct((ROWS, WIDE), BF16)
    narrow = jax.ShapeDtypeStruct((ROWS, DH), BF16)
    scratch = [
        pltpu.VMEM((WIDE, DH), BF16),
        pltpu.VMEM((WIDE, DH), BF16),
        pltpu.VMEM((NY, NX, ROWS, DH), BF16),
        pltpu.VMEM((NY, NX, ROWS, DH), BF16),
        pltpu.VMEM((NY, SPAN, WIDE), F32),
        pltpu.VMEM((NY, SPAN, WIDE), F32),
        pltpu.VMEM((NY, 8, WIDE), F32),
        pltpu.VMEM((NY, 8, WIDE), F32),
        pltpu.VMEM((NY, 8, WIDE), F32),
        pltpu.VMEM((8, WIDE), F32),
        pltpu.VMEM((SPAN, WIDE), BF16),
        pltpu.VMEM((SPAN, WIDE), BF16),
        pltpu.VMEM((DH, WIDE), F32),
        pltpu.VMEM((DH, WIDE), F32),
        pltpu.VMEM((NX, ROWS, DH), F32),
        pltpu.VMEM((NY - 1, NX, ROWS, DH), BF16),
        pltpu.VMEM((NY - 1, NX, ROWS, DH), BF16),
        pltpu.VMEM((NY, NX, ROWS, DH), BF16),
        pltpu.VMEM((NY, NX - 1, ROWS, DH), BF16),
        pltpu.VMEM((NY, ROWS, DH), BF16),
        pltpu.VMEM((NY, ROWS, DH), BF16),
        pltpu.VMEM((NX - 1, ROWS, DH), BF16),
        pltpu.VMEM((NX, ROWS, DH), BF16),
        pltpu.VMEM((ROWS, WIDE), F32),
        pltpu.VMEM((4, ROWS, WIDE), F32),
        pltpu.VMEM((HEADS, 2 * DH + 48, DH), BF16),
        pltpu.VMEM((NX, 2 * DH + 48, DH), BF16),
        pltpu.VMEM((2, DH + 48, DH), BF16),
        pltpu.VMEM((NY, DH + 48, DH), BF16),
        pltpu.VMEM((DH, DH), F32),
        pltpu.VMEM((DH, DH), F32),
        pltpu.VMEM((NX, 2 * DH, DH), BF16),
        pltpu.VMEM((HEADS, 2 * DH, DH), BF16),
        dma((NX - 1,)), dma((NX - 1,)),
        dma((NY,)), dma((NY,)),
        dma((NY - 1,)), dma((NY - 1,)),
        dma((NY, NX - 1)), dma((NY, NX - 1)),
        dma((NX,)), dma((NX,)),
        dma((NY - 1,)), dma((NY - 1,)),
        dma((NX,)), dma((NX,)),
        dma((NY - 1,)), dma((NY - 1,)),
        dma((NY, NX - 1)), dma((NY, NX - 1)),
        dma((NY,)), dma((NY,)),
        dma((NX - 1,)), dma((NX - 1,)),
    ]
    vmem = pl.BlockSpec(memory_space=pltpu.VMEM)
    return pl.pallas_call(
        kernel,
        out_shape=(wide, wide, wide, wide, wide, wide, narrow, narrow),
        in_specs=[vmem] * 9,
        out_specs=(vmem,) * 8,
        scratch_shapes=scratch,
        compiler_params=pltpu.CompilerParams(
            collective_id=0, has_side_effects=True, vmem_limit_bytes=48 * 1024 * 1024
        ),
    )(q_light, k_light, v_light, g_light, log_decay, q_soft, k_soft, v_soft, g_soft)


def solution(mesh):
    spec = P(("dp", "ctx"), "tp")
    return jax.shard_map(
        shards, mesh=mesh, in_specs=(spec,) * 9, out_specs=(spec,) * 8, check_vma=False
    )
```

```python
import jax
import jax.numpy as jnp
from jax import lax
from jax.experimental import pallas as pl
from jax.experimental.pallas import tpu as pltpu
from jax.sharding import PartitionSpec as P

DH = 128
ROWS = 128
NX = 4
NY = 8
HEADS = 4
WIDE = HEADS * DH
SPAN = NX * ROWS
CHUNK = 64
SCALE = DH**-0.5
LOG2E = 1.4426950408889634
MASKED = -1e30
F32 = jnp.float32
BF16 = jnp.bfloat16


def mm(a, b):
    return jnp.dot(a, b, preferred_element_type=F32)


def mm_nt(a, b):
    return lax.dot_general(a, b, (((1,), (1,)), ((), ())), preferred_element_type=F32)


def mm_tn(a, b):
    return lax.dot_general(a, b, (((0,), (0,)), ((), ())), preferred_element_type=F32)


def push(src, dst, send, recv, target):
    return pltpu.make_async_remote_copy(
        src_ref=src,
        dst_ref=dst,
        send_sem=send,
        recv_sem=recv,
        device_id={"ctx": target},
        device_id_type=pl.DeviceIdType.MESH,
    )


def split_log(total):
    high = total.astype(BF16)
    rest = total - high.astype(F32)
    middle = rest.astype(BF16)
    low = (rest - middle.astype(F32)).astype(BF16)
    return high, middle, low


def join_log(ref, first):
    return (
        ref[first : first + 16, :].astype(F32)
        + ref[first + 16 : first + 32, :].astype(F32)
        + ref[first + 32 : first + 48, :].astype(F32)
    )[0:1, :]


def kernel(
    q_hbm, k_hbm, v_hbm, g_hbm, ld_hbm, qs_hbm, ks_hbm, vs_hbm, gs_hbm,
    o_hbm, dq_hbm, dk_hbm, dv_hbm, os_hbm, dqs_hbm, dks_hbm, dvs_hbm,
    o_l, dq_l, dk_l, dv_l, o_s, dq_s, dk_s, dv_s,
    q_l, k_l, v_l, g_l, ld, qs, gs, qs_t, gs_t,
    kg, vg, e_ref, dp_ref, stat_m, stat_l, stat_t, dot_ref, wb_ref, ds_ref,
    out_t, dq_t, dkf, dkp, rbuf, dvp, vr, vsum, vfin, kfin, dks,
    lrow, lall, intra, lmsg, lin, ymsg, yin, cp, cg, lout, fin,
    in_s, out_s, kx_s, kx_r, kr_s, kr_r, vy_s, vy_r, vx_s, vx_r,
    l1_s, l1_r, y_s, y_r, l3_s, l3_r,
    dr_s, dr_r, du_s, du_r, dw_s, dw_r, kf_s, kf_r,
):
    me = lax.axis_index("ctx")
    y = lax.div(me, NX)
    x = lax.rem(me, NX)
    sigma = 1 - 2 * lax.rem(lax.axis_index("tp"), 2)

    def ring(value):
        return lax.rem(value + 2 * NY, NY)

    def at(yy, xx):
        return yy * NX + xx

    def col(step):
        return lax.rem(x + step + NX, NX)

    def when(condition):
        return pl.when(condition)

    barrier = pltpu.get_barrier_semaphore()
    for dx in range(1, NX):
        pl.semaphore_signal(
            barrier, inc=1, device_id={"ctx": at(y, col(dx))},
            device_id_type=pl.DeviceIdType.MESH,
        )
    for dy in range(1, NY):
        pl.semaphore_signal(
            barrier, inc=1, device_id={"ctx": at(ring(y + dy), x)},
            device_id_type=pl.DeviceIdType.MESH,
        )

    parts = [slice(h * DH, (h + 1) * DH) for h in range(HEADS)]
    moves = [(ks_hbm, kg.at[y, x]), (vs_hbm, vg.at[y, x]), (ld_hbm, ld)]
    moves += [(qs_hbm.at[:, part], qs.at[part, :]) for part in parts]
    moves += [(gs_hbm.at[:, part], gs.at[part, :]) for part in parts]
    moves += [(q_hbm, q_l), (k_hbm, k_l), (v_hbm, v_l), (g_hbm, g_l)]
    fetches = [
        pltpu.make_async_copy(src, dst, in_s.at[n]) for n, (src, dst) in enumerate(moves)
    ]
    for fetch in fetches:
        fetch.start()

    for r in range(NY):
        stat_m[r] = jnp.full((8, WIDE), MASKED, F32)
        stat_l[r] = jnp.zeros((8, WIDE), F32)
        stat_t[r] = jnp.zeros((8, WIDE), F32)
    out_t[...] = jnp.zeros_like(out_t)
    dq_t[...] = jnp.zeros_like(dq_t)
    cp[...] = jnp.zeros_like(cp)
    cg[...] = jnp.zeros_like(cg)
    for fetch in fetches[:3]:
        fetch.wait()
    pl.semaphore_wait(barrier, NX + NY - 2)

    def key_across(dx, owner):
        return push(
            kg.at[y, owner], kg.at[y, owner], kx_s.at[dx - 1], kx_r.at[dx - 1], at(y, col(dx))
        )

    def value_along(dy, owner):
        return push(
            vg.at[owner, x], vg.at[owner, x], vy_s.at[dy - 1], vy_r.at[dy - 1],
            at(ring(y + dy), x),
        )

    def value_across(dy, dx, row, owner):
        return push(
            vg.at[row, owner], vg.at[row, owner], vx_s.at[dy, dx - 1], vx_r.at[dy, dx - 1],
            at(y, col(dx)),
        )

    def key_ring(place, row, j, turn):
        block = kg.at[row, col(-j)]
        return push(
            block, block, kr_s.at[place - 1, j], kr_r.at[place - 1, j], at(ring(y + turn), x)
        )

    def wanted(row, turn, target, far):
        return jnp.where(turn > 0, row < target, row < far)

    def key_start(place, row, j, turn, far):
        @when(wanted(row, turn, ring(y + turn), far))
        def _():
            key_ring(place, row, j, turn).start()

    for dx in range(1, NX):
        key_across(dx, x).start()
    key_start(1, y, 0, sigma, 4)
    key_start(2, y, 0, -sigma, 3)
    for dy in (1, 7, 2, 6, 3, 5, 4):
        @when(y + dy < NY)
        def _():
            value_along(dy, y).start()
    for dx in range(1, NX):
        value_across(0, dx, y, x).start()

    def block_scores(row, b, masked):
        scores = mm(kg[row, b], qs_t[...])
        if masked:
            key_at = lax.broadcasted_iota(jnp.int32, (ROWS, WIDE), 0) + b * ROWS
            query_at = lax.rem(lax.broadcasted_iota(jnp.int32, (ROWS, WIDE), 1), ROWS)
            scores = jnp.where(key_at <= query_at + x * ROWS, scores, MASKED)
        e_ref[row, pl.ds(pl.multiple_of(b * ROWS, ROWS), ROWS), :] = scores
        top = jnp.max(scores.reshape(ROWS // 8, 8, WIDE), axis=0)
        stat_m[row] = jnp.maximum(stat_m[row], top)

    def row_weights(row):
        top = jnp.max(stat_m[row], axis=0, keepdims=True)
        stat_m[row] = jnp.broadcast_to(top, (8, WIDE))
        shift = top * (SCALE * LOG2E)

        def turn(i, total):
            rows = pl.ds(pl.multiple_of(i * CHUNK, CHUNK), CHUNK)
            grown = jnp.exp2(e_ref[row, rows, :] * (SCALE * LOG2E) - shift)
            e_ref[row, rows, :] = grown
            return total + jnp.sum(grown.reshape(CHUNK // 8, 8, WIDE), axis=0)

        total = lax.fori_loop(0, SPAN // CHUNK, turn, jnp.zeros((8, WIDE), F32))
        stat_l[row] = jnp.broadcast_to(jnp.sum(total, axis=0, keepdims=True), (8, WIDE))

    def light_send(h, owner):
        return push(lmsg.at[h], lin.at[owner], l1_s.at[h], l1_r.at[owner], at(y, h))

    def light_head(h):
        cols = pl.ds(pl.multiple_of(h * DH, DH), DH)
        qh, kh, vh, gh = q_l[:, cols], k_l[:, cols], v_l[:, cols], g_l[:, cols]
        flat = jnp.broadcast_to(lrow[pl.ds(h, 1), :], (ROWS, ROWS))
        level = flat.T
        lall[:, cols] = level
        row_at = lax.broadcasted_iota(jnp.int32, (ROWS, ROWS), 0)
        causal = row_at >= lax.broadcasted_iota(jnp.int32, (ROWS, ROWS), 1)
        gaps = jnp.where(causal, level - flat, 0.0)
        weights = jnp.where(causal, jnp.exp(gaps), 0.0) * SCALE
        mixing = (mm_nt(qh, kh) * weights).astype(BF16)
        back_mix = (mm_nt(gh, vh) * weights).astype(BF16)
        intra[0, :, cols] = mm(mixing, vh)
        intra[1, :, cols] = mm(back_mix, kh)
        intra[2, :, cols] = mm_tn(back_mix, qh)
        intra[3, :, cols] = mm_tn(mixing, gh)
        last = level[ROWS - 1 : ROWS, :]
        fading = (kh.astype(F32) * jnp.exp(last - level)).astype(BF16)
        entering = (qh.astype(F32) * jnp.exp(level)).astype(BF16)
        lmsg[h, 0:DH, :] = mm_tn(fading, vh).astype(BF16)
        lmsg[h, DH : 2 * DH, :] = mm_tn(entering, gh).astype(BF16)
        for n, term in enumerate(split_log(jnp.broadcast_to(last, (16, DH)))):
            lmsg[h, 2 * DH + 16 * n : 2 * DH + 16 * (n + 1), :] = term

        @when(h != x)
        def _():
            light_send(h, x).start()

        @when(h == x)
        def _():
            lin[x] = lmsg[h]

    upper = (
        lax.broadcasted_iota(jnp.int32, (ROWS, ROWS), 0)
        <= lax.broadcasted_iota(jnp.int32, (ROWS, ROWS), 1)
    ).astype(F32)
    lrow[...] = jnp.dot(
        ld[...], upper, precision=lax.Precision.HIGHEST, preferred_element_type=F32
    )
    for fetch in fetches[3:]:
        fetch.wait()
    for part in parts:
        qs_t[:, part] = qs[part, :].T
        gs_t[:, part] = gs[part, :].T

    block_scores(y, x, True)
    for j in range(1, NX):
        key_across(j, col(-j)).wait_recv()
        key_start(1, y, j, sigma, 4)
        key_start(2, y, j, -sigma, 3)
        block_scores(y, col(-j), True)
    light_head(0)
    row_weights(y)
    light_head(1)

    def key_take(place, row, j, turn, far, last):
        @when(wanted(row, turn, y, far))
        def _():
            key_ring(place, row, j, turn).wait_recv()

            @when(jnp.logical_not(last))
            def _():
                key_start(place + 2, row, j, turn, far)

            @when(row < y)
            def _():
                block_scores(row, col(-j), False)

    def value_pass(dy):
        @when(y >= dy)
        def _():
            value_along(dy, ring(y - dy)).wait_recv()
            for dx in range(1, NX):
                value_across(dy, dx, ring(y - dy), x).start()

    def value_take(dy):
        @when(y >= dy)
        def _():
            row = ring(y - dy)
            for dx in range(1, NX):
                value_across(dy, dx, row, col(-dx)).wait_recv()
            total = jnp.zeros((8, WIDE), F32)
            for b in range(NX):
                grads = mm(vg[row, b], gs_t[...])
                dp_ref[row, b * ROWS : (b + 1) * ROWS, :] = grads
                weighed = grads * e_ref[row, b * ROWS : (b + 1) * ROWS, :]
                total = total + jnp.sum(weighed.reshape(ROWS // 8, 8, WIDE), axis=0)
            stat_t[row] = jnp.broadcast_to(jnp.sum(total, axis=0, keepdims=True), (8, WIDE))

    def gather_turn(k, _):
        row_a = ring(y - sigma * k)
        row_b = ring(y + sigma * k)

        def block_turn(j, _):
            key_take(2 * k - 1, row_a, j, sigma, 4, k < 0)
            key_take(2 * k, row_b, j, -sigma, 3, k == 3)
            return 0

        lax.fori_loop(0, NX, block_turn, 0)
        value_pass(k)
        value_pass(NY - k)

        @when(row_a < y)
        def _():
            row_weights(row_a)

        @when(row_b < y)
        def _():
            row_weights(row_b)

        @when(k < 3)
        def _():
            light_head(k + 1)

        value_take(k - 1)

        @when(k > 1)
        def _():
            value_take(NY + 1 - k)

        return 0

    lax.fori_loop(1, NY // 2, gather_turn, 0)
    value_pass(NY // 2)
    row_far = ring(y - sigma * (NY // 2))

    def far_turn(j, _):
        key_take(NY - 1, row_far, j, sigma, 4, j >= 0)
        return 0

    lax.fori_loop(0, NX, far_turn, 0)

    @when(row_far < y)
    def _():
        row_weights(row_far)

    for h in range(NX):
        @when(h != x)
        def _():
            push(lmsg.at[h], lin.at[h], l1_s.at[h], l1_r.at[h], at(y, h)).wait_recv()
    levels = [join_log(lin.at[b], 2 * DH) for b in range(NX)]
    row_state = lin[0, 0:DH, :].astype(F32)
    for b in range(1, NX):
        row_state = jnp.exp(levels[b]) * row_state + lin[b, 0:DH, :].astype(F32)
    row_grad = lin[NX - 1, DH : 2 * DH, :].astype(F32)
    for b in range(NX - 2, -1, -1):
        row_grad = jnp.exp(levels[b]) * row_grad + lin[b, DH : 2 * DH, :].astype(F32)
    row_level = jnp.broadcast_to(levels[0] + levels[1] + levels[2] + levels[3], (16, DH))
    ymsg[0, 0:DH, :] = row_state.astype(BF16)
    ymsg[1, 0:DH, :] = row_grad.astype(BF16)
    for n, term in enumerate(split_log(row_level)):
        ymsg[0, DH + 16 * n : DH + 16 * (n + 1), :] = term
        ymsg[1, DH + 16 * n : DH + 16 * (n + 1), :] = term

    def state_along(dy, owner):
        kind = jnp.where(y + dy < NY, 0, 1)
        return push(
            ymsg.at[kind], yin.at[owner], y_s.at[dy - 1], y_r.at[dy - 1], at(ring(y + dy), x)
        )

    for dy in range(1, NY):
        state_along(dy, y).start()

    value_take(NY // 2 - 1)
    value_take(NY // 2 + 1)
    value_take(NY // 2)

    top = stat_m[0]
    for r in range(1, NY):
        top = jnp.maximum(top, stat_m[r])
    total = jnp.zeros((8, WIDE), F32)
    dots = jnp.zeros((8, WIDE), F32)
    for r in range(NY):
        factor = jnp.exp2((stat_m[r] - top) * (SCALE * LOG2E))
        total = total + factor * stat_l[r]
        dots = dots + factor * stat_t[r]
        stat_m[r] = factor
    inverse = 1.0 / total
    dot_ref[...] = dots * inverse
    for r in range(NY):
        stat_l[r] = stat_m[r] * inverse

    def state_back(b, owner):
        return push(lout.at[b], fin.at[owner], l3_s.at[b], l3_r.at[owner], at(y, b))

    def state_turn():
        for dy in range(1, NY):
            state_along(dy, ring(y - dy)).wait_recv()
        for yy in range(NY):
            @when(yy < y)
            def _():
                cp[...] = (
                    jnp.exp(join_log(yin.at[yy], DH)) * cp[...] + yin[yy, 0:DH, :].astype(F32)
                )
        for yy in range(NY - 1, -1, -1):
            @when(yy > y)
            def _():
                cg[...] = (
                    jnp.exp(join_log(yin.at[yy], DH)) * cg[...] + yin[yy, 0:DH, :].astype(F32)
                )
        factors = [jnp.exp(join_log(lin.at[b], 2 * DH)) for b in range(NX)]
        carried = cp[...]
        for b in range(NX):
            lout[b, 0:DH, :] = carried.astype(BF16)
            carried = factors[b] * carried + lin[b, 0:DH, :].astype(F32)
        carried = cg[...]
        for b in range(NX - 1, -1, -1):
            lout[b, DH : 2 * DH, :] = carried.astype(BF16)
            carried = factors[b] * carried + lin[b, DH : 2 * DH, :].astype(F32)
        for b in range(NX):
            @when(b != x)
            def _():
                state_back(b, x).start()
        fin[x] = lout[x]

    def grad_ring(place, b, turn):
        return push(
            dkp.at[place, b], rbuf.at[place, b], dr_s.at[place, b], dr_r.at[place, b],
            at(ring(y + turn), x),
        )

    def grad_sent(row, turn, sender, far):
        return jnp.where(turn < 0, row < sender, row < far)

    def dv_across(row, dx):
        return push(
            dvp.at[row, col(dx)], vr.at[row, dx - 1], du_s.at[row, dx - 1], du_r.at[row, dx - 1],
            at(y, col(dx)),
        )

    def dv_along(row, owner):
        return push(vsum.at[row], vfin.at[owner], dw_s.at[row], dw_r.at[owner], at(row, x))

    def dv_sum(row):
        for dx in range(1, NX):
            dv_across(row, dx).wait_recv()
        return (
            dvp[row, x].astype(F32)
            + vr[row, 0].astype(F32)
            + vr[row, 1].astype(F32)
            + vr[row, 2].astype(F32)
        )

    def place_row(place):
        forth = (lax.rem(place, 2) == 1) | (place == 0)
        turn = jnp.where(forth, sigma, -sigma)
        far = jnp.where(forth, 4, 3)
        return turn, far, ring(y + turn * (4 - lax.div(place + 1, 2)))

    def back_turn(place, _):
        turn, far, row = place_row(place)

        @when(row <= y)
        def _():
            def weigh(i, _):
                rows = pl.ds(pl.multiple_of(i * CHUNK, CHUNK), CHUNK)
                weights = e_ref[row, rows, :] * stat_l[row, 0:1, :]
                wb_ref[rows, :] = weights.astype(BF16)
                ds_ref[rows, :] = (weights * (dp_ref[row, rows, :] - dot_ref[0:1, :])).astype(BF16)
                return 0

            lax.fori_loop(0, SPAN // CHUNK, weigh, 0)
            dkf[...] = (mm(ds_ref[...], qs[...]) * SCALE).reshape(NX, ROWS, DH)
            dvp[row] = mm(wb_ref[...], gs[...]).astype(BF16).reshape(NX, ROWS, DH)
            for dx in range(1, NX):
                dv_across(row, dx).start()

        @when(row > y)
        def _():
            dkf[...] = jnp.zeros_like(dkf)

        before = jnp.where(place == 1, 0, jnp.maximum(place - 2, 0))
        takes = (place != 0) & (place != 2) & (place != NY - 1)
        takes = takes & grad_sent(row, turn, ring(y - turn), far)
        sends = (place < NY - 1) & grad_sent(row, turn, y, far)

        def ring_block(b, _):
            @when(takes)
            def _():
                grad_ring(before, b, turn).wait_recv()
                dkf[b] += rbuf[before, b].astype(F32)

            @when(sends)
            def _():
                dkp[place, b] = dkf[b].astype(BF16)
                grad_ring(place, b, turn).start()

            return 0

        lax.fori_loop(0, NX, ring_block, 0)

        @when(row <= y)
        def _():
            out_t[...] += mm_tn(vg[row].reshape(SPAN, DH), wb_ref[...])
            dq_t[...] += mm_tn(kg[row].reshape(SPAN, DH), ds_ref[...])

        @when(place >= 1)
        def _():
            _, _, before_row = place_row(place - 1)

            @when(before_row < y)
            def _():
                vsum[before_row] = dv_sum(before_row).astype(BF16)
                dv_along(before_row, y).start()

        @when(place == 2)
        def _():
            state_turn()

        return 0

    lax.fori_loop(0, NY, back_turn, 0)

    for b in range(NX):
        @when(b != x)
        def _():
            push(lout.at[b], fin.at[b], l3_s.at[b], l3_r.at[b], at(y, b)).wait_recv()

    def light_out(h, _):
        cols = pl.ds(pl.multiple_of(h * DH, DH), DH)
        qh, kh, vh, gh = q_l[:, cols], k_l[:, cols], v_l[:, cols], g_l[:, cols]
        level = lall[:, cols]
        entering = jnp.exp(level) * SCALE
        fading = jnp.exp(level[ROWS - 1 : ROWS, :] - level) * SCALE
        prior = fin[h, 0:DH, :]
        later = fin[h, DH : 2 * DH, :]
        o_l[:, cols] = (intra[0, :, cols] + entering * mm(qh, prior)).astype(BF16)
        dq_l[:, cols] = (intra[1, :, cols] + entering * mm_nt(gh, prior)).astype(BF16)
        dk_l[:, cols] = (intra[2, :, cols] + fading * mm_nt(vh, later)).astype(BF16)
        dv_l[:, cols] = (intra[3, :, cols] + fading * mm(kh, later)).astype(BF16)
        return 0

    lax.fori_loop(0, HEADS, light_out, 0)
    moves = [(o_l, o_hbm), (dq_l, dq_hbm), (dk_l, dk_hbm), (dv_l, dv_hbm)]
    moves += [(o_s, os_hbm), (dq_s, dqs_hbm), (dk_s, dks_hbm), (dv_s, dvs_hbm)]
    stores = [
        pltpu.make_async_copy(src, dst, out_s.at[n]) for n, (src, dst) in enumerate(moves)
    ]
    for store in stores[:4]:
        store.start()

    def dk_across(dx):
        return push(
            dks.at[col(dx)], kfin.at[dx - 1], kf_s.at[dx - 1], kf_r.at[dx - 1], at(y, col(dx))
        )

    for j in (1, 2, 3, 0):
        b = col(j)
        for place, turn, far in ((NY - 3, sigma, 4), (NY - 2, -sigma, 3)):
            @when(grad_sent(y, turn, ring(y - turn), far))
            def _():
                grad_ring(place, b, turn).wait_recv()
                dkf[b] += rbuf[place, b].astype(F32)
        if j:
            dks[b] = dkf[b].astype(BF16)
            dk_across(j).start()

    for part in parts:
        o_s[:, part] = out_t[:, part].T.astype(BF16)
        dq_s[:, part] = (dq_t[:, part].T * SCALE).astype(BF16)
    stores[4].start()
    stores[5].start()

    cp[...] = dv_sum(y)
    for yy in range(1, NY):
        @when(yy > y)
        def _():
            push(vsum.at[yy], vfin.at[yy], dw_s.at[yy], dw_r.at[yy], at(yy, x)).wait_recv()
            cp[...] += vfin[yy].astype(F32)
    dv_s[...] = cp[...].astype(BF16)
    stores[7].start()

    for dx in range(1, NX):
        dk_across(dx).wait_recv()
    dk_s[...] = (
        dkf[x] + kfin[0].astype(F32) + kfin[1].astype(F32) + kfin[2].astype(F32)
    ).astype(BF16)
    stores[6].start()

    for dx in range(1, NX):
        key_across(dx, x).wait_send()
        dk_across(dx).wait_send()

    def sent_turn(place, _):
        odd = lax.rem(place, 2) == 1
        turn = jnp.where(odd, sigma, -sigma)
        row = ring(y - turn * (lax.div(place + 1, 2) - 1))

        @when(wanted(row, turn, ring(y + turn), jnp.where(odd, 4, 3)))
        def _():
            for j in range(NX):
                key_ring(place, row, j, turn).wait_send()

        turn_back, far_back, row_back = place_row(place - 1)

        @when(grad_sent(row_back, turn_back, y, far_back))
        def _():
            for j in range(NX):
                grad_ring(place - 1, j, turn_back).wait_send()

        return 0

    lax.fori_loop(1, NY, sent_turn, 0)
    for dy in range(1, NY):
        state_along(dy, y).wait_send()

        @when(y + dy < NY)
        def _():
            value_along(dy, y).wait_send()

        @when(dy - 1 < y)
        def _():
            dv_along(dy - 1, y).wait_send()
    for b in range(NX):
        @when(b != x)
        def _():
            light_send(b, x).wait_send()
            state_back(b, x).wait_send()
    for dy in range(NY):
        @when(dy <= y)
        def _():
            for dx in range(1, NX):
                value_across(dy, dx, ring(y - dy), x).wait_send()
                dv_across(dy, dx).wait_send()
    for store in stores:
        store.wait()


def copy_out(*refs):
    ins, outs, sems = refs[:8], refs[8:16], refs[16]
    copies = [pltpu.make_async_copy(a, b, sems.at[n]) for n, (a, b) in enumerate(zip(ins, outs))]
    for copy in copies:
        copy.start()
    for copy in copies:
        copy.wait()


def shards(q_light, k_light, v_light, g_light, log_decay, q_soft, k_soft, v_soft, g_soft):
    dma = pltpu.SemaphoreType.DMA
    wide = jax.ShapeDtypeStruct((ROWS, WIDE), BF16)
    narrow = jax.ShapeDtypeStruct((ROWS, DH), BF16)
    scratch = [pltpu.VMEM((ROWS, WIDE), BF16)] * 6 + [pltpu.VMEM((ROWS, DH), BF16)] * 2
    scratch += [
        pltpu.VMEM((ROWS, WIDE), BF16),
        pltpu.VMEM((ROWS, WIDE), BF16),
        pltpu.VMEM((ROWS, WIDE), BF16),
        pltpu.VMEM((ROWS, WIDE), BF16),
        pltpu.VMEM((HEADS, ROWS), F32),
        pltpu.VMEM((WIDE, DH), BF16),
        pltpu.VMEM((WIDE, DH), BF16),
        pltpu.VMEM((DH, WIDE), BF16),
        pltpu.VMEM((DH, WIDE), BF16),
        pltpu.VMEM((NY, NX, ROWS, DH), BF16),
        pltpu.VMEM((NY, NX, ROWS, DH), BF16),
        pltpu.VMEM((NY, SPAN, WIDE), F32),
        pltpu.VMEM((NY, SPAN, WIDE), F32),
        pltpu.VMEM((NY, 8, WIDE), F32),
        pltpu.VMEM((NY, 8, WIDE), F32),
        pltpu.VMEM((NY, 8, WIDE), F32),
        pltpu.VMEM((8, WIDE), F32),
        pltpu.VMEM((SPAN, WIDE), BF16),
        pltpu.VMEM((SPAN, WIDE), BF16),
        pltpu.VMEM((DH, WIDE), F32),
        pltpu.VMEM((DH, WIDE), F32),
        pltpu.VMEM((NX, ROWS, DH), F32),
        pltpu.VMEM((NY - 1, NX, ROWS, DH), BF16),
        pltpu.VMEM((NY - 1, NX, ROWS, DH), BF16),
        pltpu.VMEM((NY, NX, ROWS, DH), BF16),
        pltpu.VMEM((NY, NX - 1, ROWS, DH), BF16),
        pltpu.VMEM((NY, ROWS, DH), BF16),
        pltpu.VMEM((NY, ROWS, DH), BF16),
        pltpu.VMEM((NX - 1, ROWS, DH), BF16),
        pltpu.VMEM((NX, ROWS, DH), BF16),
        pltpu.VMEM((HEADS, ROWS), F32),
        pltpu.VMEM((ROWS, WIDE), F32),
        pltpu.VMEM((4, ROWS, WIDE), F32),
        pltpu.VMEM((HEADS, 2 * DH + 48, DH), BF16),
        pltpu.VMEM((NX, 2 * DH + 48, DH), BF16),
        pltpu.VMEM((2, DH + 48, DH), BF16),
        pltpu.VMEM((NY, DH + 48, DH), BF16),
        pltpu.VMEM((DH, DH), F32),
        pltpu.VMEM((DH, DH), F32),
        pltpu.VMEM((NX, 2 * DH, DH), BF16),
        pltpu.VMEM((HEADS, 2 * DH, DH), BF16),
        dma((15,)),
        dma((8,)),
        dma((NX - 1,)), dma((NX - 1,)),
        dma((NY - 1, NX)), dma((NY - 1, NX)),
        dma((NY - 1,)), dma((NY - 1,)),
        dma((NY, NX - 1)), dma((NY, NX - 1)),
        dma((NX,)), dma((NX,)),
        dma((NY - 1,)), dma((NY - 1,)),
        dma((NX,)), dma((NX,)),
        dma((NY - 1, NX)), dma((NY - 1, NX)),
        dma((NY, NX - 1)), dma((NY, NX - 1)),
        dma((NY,)), dma((NY,)),
        dma((NX - 1,)), dma((NX - 1,)),
    ]
    hbm = pl.BlockSpec(memory_space=pltpu.HBM)
    room = 62 * 1024 * 1024
    shapes = (wide, wide, wide, wide, wide, wide, narrow, narrow)
    results = pl.pallas_call(
        kernel,
        out_shape=shapes,
        in_specs=[hbm] * 9,
        out_specs=(hbm,) * 8,
        scratch_shapes=scratch,
        compiler_params=pltpu.CompilerParams(
            collective_id=0, has_side_effects=True, vmem_limit_bytes=room
        ),
    )(q_light, k_light, v_light, g_light, log_decay.T, q_soft, k_soft, v_soft, g_soft)
    return pl.pallas_call(
        copy_out,
        out_shape=shapes,
        in_specs=[hbm] * 8,
        out_specs=(hbm,) * 8,
        scratch_shapes=[dma((8,))],
        compiler_params=pltpu.CompilerParams(vmem_limit_bytes=room),
    )(*results)


def solution(mesh):
    spec = P(("dp", "ctx"), "tp")
    return jax.shard_map(
        shards, mesh=mesh, in_specs=(spec,) * 9, out_specs=(spec,) * 8, check_vma=False
    )
```

```python
import jax
import jax.numpy as jnp
from jax import lax
from jax.experimental import pallas as pl
from jax.experimental.pallas import tpu as pltpu
from jax.sharding import PartitionSpec as P

DH = 128
ROWS = 128
NX = 4
NY = 8
HEADS = 4
WIDE = HEADS * DH
SPAN = NX * ROWS
SCALE = DH**-0.5
LOG2E = 1.4426950408889634
MASKED = -1e30
F32 = jnp.float32
BF16 = jnp.bfloat16


def mm(a, b):
    return jnp.dot(a, b, preferred_element_type=F32)


def mm_nt(a, b):
    return lax.dot_general(a, b, (((1,), (1,)), ((), ())), preferred_element_type=F32)


def mm_tn(a, b):
    return lax.dot_general(a, b, (((0,), (0,)), ((), ())), preferred_element_type=F32)


def push(src, dst, send, recv, target):
    return pltpu.make_async_remote_copy(
        src_ref=src,
        dst_ref=dst,
        send_sem=send,
        recv_sem=recv,
        device_id={"ctx": target},
        device_id_type=pl.DeviceIdType.MESH,
    )


def split_log(total):
    high = total.astype(BF16)
    rest = total - high.astype(F32)
    middle = rest.astype(BF16)
    low = (rest - middle.astype(F32)).astype(BF16)
    return high, middle, low


def join_log(ref, first):
    return (
        ref[first : first + 16, :].astype(F32)
        + ref[first + 16 : first + 32, :].astype(F32)
        + ref[first + 32 : first + 48, :].astype(F32)
    )[0:1, :]


def kernel(
    q_hbm, k_hbm, v_hbm, g_hbm, ld_hbm, qs_hbm, ks_hbm, vs_hbm, gs_hbm,
    o_hbm, dq_hbm, dk_hbm, dv_hbm, os_hbm, dqs_hbm, dks_hbm, dvs_hbm,
    o_l, dq_l, dk_l, dv_l, o_s, dq_s, dk_s, dv_s,
    q_l, k_l, v_l, g_l, ld, qs, gs, qs_t, gs_t,
    kg, vg, e_ref, dp_ref, stat_m, stat_l, stat_t, dot_ref, wb_ref, ds_ref,
    out_t, dq_t, dkf, dkp, rbuf, dvp, vr, vsum, vfin, vacc, kfin, dks,
    lrow, lall, intra, lmsg, lin, ymsg, yin, cp, cg, lout, fin,
    in_s, out_s, kx_s, kx_r, kr_s, kr_r, vx_s, vx_r,
    l1_s, l1_r, y_s, y_r, l3_s, l3_r,
    dr_s, dr_r, du_s, du_r, dw_s, dw_r, kf_s, kf_r,
):
    me = lax.axis_index("ctx")
    y = lax.div(me, NX)
    x = lax.rem(me, NX)
    sigma = 1 - 2 * lax.rem(lax.axis_index("tp"), 2)

    def ring(value):
        return lax.rem(value + 2 * NY, NY)

    def at(yy, xx):
        return yy * NX + xx

    def col(step):
        return lax.rem(x + step + NX, NX)

    def when(condition):
        return pl.when(condition)

    barrier = pltpu.get_barrier_semaphore()
    for dx in range(1, NX):
        pl.semaphore_signal(
            barrier, inc=1, device_id={"ctx": at(y, col(dx))},
            device_id_type=pl.DeviceIdType.MESH,
        )
    for dy in range(1, NY):
        pl.semaphore_signal(
            barrier, inc=1, device_id={"ctx": at(ring(y + dy), x)},
            device_id_type=pl.DeviceIdType.MESH,
        )

    parts = [slice(h * DH, (h + 1) * DH) for h in range(HEADS)]
    moves = [(ks_hbm, kg.at[y, x]), (vs_hbm, vg.at[y, x]), (ld_hbm, ld)]
    moves += [(qs_hbm.at[:, part], qs.at[part, :]) for part in parts]
    moves += [(gs_hbm.at[:, part], gs.at[part, :]) for part in parts]
    moves += [(q_hbm, q_l), (k_hbm, k_l), (v_hbm, v_l), (g_hbm, g_l)]
    fetches = [
        pltpu.make_async_copy(src, dst, in_s.at[n]) for n, (src, dst) in enumerate(moves)
    ]
    for fetch in fetches:
        fetch.start()

    halves = [slice(0, WIDE // 2), slice(WIDE // 2, WIDE)]
    stat_m[...] = jnp.full(stat_m.shape, MASKED, F32)
    stat_l[...] = jnp.zeros_like(stat_l)
    stat_t[...] = jnp.zeros_like(stat_t)
    out_t[...] = jnp.zeros_like(out_t)
    dq_t[...] = jnp.zeros_like(dq_t)
    cp[...] = jnp.zeros_like(cp)
    cg[...] = jnp.zeros_like(cg)
    for fetch in fetches[:3]:
        fetch.wait()
    pl.semaphore_wait(barrier, NX + NY - 2)

    def key_across(dx, owner):
        return push(
            kg.at[y, owner], kg.at[y, owner], kx_s.at[dx - 1], kx_r.at[dx - 1], at(y, col(dx))
        )

    def value_across(row, i, owner):
        return push(
            vg.at[row, owner], vg.at[row, owner], vx_s.at[row, i], vx_r.at[row, i],
            at(y, col(-sigma if i == 1 else sigma)),
        )

    def key_ring(place, row, j, turn):
        values = isinstance(j, int) and j == NX
        block = vg.at[row, x] if values else kg.at[row, col(-j)]
        return push(
            block, block, kr_s.at[place - 1, j], kr_r.at[place - 1, j], at(ring(y + turn), x)
        )

    def wanted(row, turn, target, far):
        return jnp.where(turn > 0, row < target, row < far)

    def key_start(place, row, j, turn, far):
        @when(wanted(row, turn, ring(y + turn), far))
        def _():
            key_ring(place, row, j, turn).start()

    for dx in range(1, NX):
        key_across(dx, x).start()
    for j in (NX, 0):
        key_start(1, y, j, sigma, 4)
        key_start(2, y, j, -sigma, 3)
    value_across(y, 0, x).start()
    value_across(y, 1, x).start()

    def row_scores(row, masked):
        for b in range(NX):
            rows = slice(b * ROWS, (b + 1) * ROWS)
            for cols in halves:
                scores = mm(kg[row, b], qs_t[:, cols])
                if masked:
                    key_at = lax.broadcasted_iota(jnp.int32, scores.shape, 0) + b * ROWS
                    query_at = lax.rem(lax.broadcasted_iota(jnp.int32, scores.shape, 1), ROWS)
                    scores = jnp.where(key_at <= query_at + x * ROWS, scores, MASKED)
                top = jnp.max(scores, axis=0, keepdims=True)
                grown = jnp.exp2(scores * (SCALE * LOG2E) - top * (SCALE * LOG2E))
                e_ref[row, rows, cols] = grown
                stat_m[pl.ds(row * NX + b, 1), cols] = top
                stat_l[pl.ds(row * NX + b, 1), cols] = jnp.sum(grown, axis=0, keepdims=True)

    def light_send(h, owner):
        return push(lmsg.at[h], lin.at[owner], l1_s.at[h], l1_r.at[owner], at(y, h))

    def light_head(h):
        cols = pl.ds(pl.multiple_of(h * DH, DH), DH)
        qh, kh, vh, gh = q_l[:, cols], k_l[:, cols], v_l[:, cols], g_l[:, cols]
        flat = jnp.broadcast_to(lrow[pl.ds(h, 1), :], (ROWS, ROWS))
        level = flat.T
        lall[:, cols] = level
        row_at = lax.broadcasted_iota(jnp.int32, (ROWS, ROWS), 0)
        causal = row_at >= lax.broadcasted_iota(jnp.int32, (ROWS, ROWS), 1)
        gaps = jnp.where(causal, level - flat, 0.0)
        weights = jnp.where(causal, jnp.exp(gaps), 0.0) * SCALE
        mixing = (mm_nt(qh, kh) * weights).astype(BF16)
        back_mix = (mm_nt(gh, vh) * weights).astype(BF16)
        intra[0, :, cols] = mm(mixing, vh)
        intra[1, :, cols] = mm(back_mix, kh)
        intra[2, :, cols] = mm_tn(back_mix, qh)
        intra[3, :, cols] = mm_tn(mixing, gh)
        last = level[ROWS - 1 : ROWS, :]
        fading = (kh.astype(F32) * jnp.exp(last - level)).astype(BF16)
        entering = (qh.astype(F32) * jnp.exp(level)).astype(BF16)
        lmsg[h, 0:DH, :] = mm_tn(fading, vh).astype(BF16)
        lmsg[h, DH : 2 * DH, :] = mm_tn(entering, gh).astype(BF16)
        for n, term in enumerate(split_log(jnp.broadcast_to(last, (16, DH)))):
            lmsg[h, 2 * DH + 16 * n : 2 * DH + 16 * (n + 1), :] = term

        @when(h != x)
        def _():
            light_send(h, x).start()

        @when(h == x)
        def _():
            lin[x] = lmsg[h]

    upper = (
        lax.broadcasted_iota(jnp.int32, (ROWS, ROWS), 0)
        <= lax.broadcasted_iota(jnp.int32, (ROWS, ROWS), 1)
    ).astype(F32)
    lrow[...] = jnp.dot(
        ld[...], upper, precision=lax.Precision.HIGHEST, preferred_element_type=F32
    )
    for fetch in fetches[3:]:
        fetch.wait()
    for part in parts:
        qs_t[:, part] = qs[part, :].T
        gs_t[:, part] = gs[part, :].T

    for j in range(1, NX):
        key_across(j, col(-j)).wait_recv()
        key_start(1, y, j, sigma, 4)
        key_start(2, y, j, -sigma, 3)
    row_scores(y, True)
    light_head(0)
    light_head(1)

    def key_take(place, row, j, turn, far, last):
        @when(wanted(row, turn, y, far))
        def _():
            key_ring(place, row, j, turn).wait_recv()

            @when(jnp.logical_not(last))
            def _():
                key_start(place + 2, row, j, turn, far)

    def value_pass(row):
        @when(row < y)
        def _():
            value_across(row, 0, x).start()
            value_across(row, 1, x).start()

    def value_relay(row):
        @when(row <= y)
        def _():
            value_across(row, 0, col(-sigma)).wait_recv()
            value_across(row, 2, col(-sigma)).start()

    def value_take(row):
        @when(row <= y)
        def _():
            value_across(row, 1, col(sigma)).wait_recv()
            value_across(row, 2, col(2)).wait_recv()
            for b in range(NX):
                rows = slice(b * ROWS, (b + 1) * ROWS)
                for cols in halves:
                    grads = mm(vg[row, b], gs_t[:, cols])
                    dp_ref[row, rows, cols] = grads
                    weighed = jnp.sum(grads * e_ref[row, rows, cols], axis=0, keepdims=True)
                    stat_t[pl.ds(row * NX + b, 1), cols] = weighed

    def rows_at(k):
        return ring(y - sigma * k), ring(y + sigma * k)

    def gather_turn(k, _):
        row_a, row_b = rows_at(k)
        past_a, past_b = rows_at(k - 1)
        key_take(2 * k - 1, row_a, NX, sigma, 4, k < 0)
        value_pass(row_a)
        key_take(2 * k, row_b, NX, -sigma, 3, k == 3)
        value_pass(row_b)

        def block_turn(j, _):
            key_take(2 * k - 1, row_a, j, sigma, 4, k < 0)
            key_take(2 * k, row_b, j, -sigma, 3, k == 3)
            return 0

        lax.fori_loop(0, NX, block_turn, 0)
        value_relay(past_a)

        @when(k > 1)
        def _():
            value_relay(past_b)

        @when(row_a < y)
        def _():
            row_scores(row_a, False)

        @when(row_b < y)
        def _():
            row_scores(row_b, False)

        @when(k < 3)
        def _():
            light_head(k + 1)

        value_take(past_a)

        @when(k > 1)
        def _():
            value_take(past_b)

        return 0

    lax.fori_loop(1, NY // 2, gather_turn, 0)
    past_a, past_b = rows_at(NY // 2 - 1)
    row_far = ring(y - sigma * (NY // 2))
    key_take(NY - 1, row_far, NX, sigma, 4, row_far >= 0)
    value_pass(row_far)

    def far_turn(j, _):
        key_take(NY - 1, row_far, j, sigma, 4, j >= 0)
        return 0

    lax.fori_loop(0, NX, far_turn, 0)
    value_relay(past_a)
    value_relay(past_b)

    @when(row_far < y)
    def _():
        row_scores(row_far, False)

    value_relay(row_far)

    for h in range(NX):
        @when(h != x)
        def _():
            push(lmsg.at[h], lin.at[h], l1_s.at[h], l1_r.at[h], at(y, h)).wait_recv()
    levels = [join_log(lin.at[b], 2 * DH) for b in range(NX)]
    row_state = lin[0, 0:DH, :].astype(F32)
    for b in range(1, NX):
        row_state = jnp.exp(levels[b]) * row_state + lin[b, 0:DH, :].astype(F32)
    row_grad = lin[NX - 1, DH : 2 * DH, :].astype(F32)
    for b in range(NX - 2, -1, -1):
        row_grad = jnp.exp(levels[b]) * row_grad + lin[b, DH : 2 * DH, :].astype(F32)
    row_level = jnp.broadcast_to(levels[0] + levels[1] + levels[2] + levels[3], (16, DH))
    ymsg[0, 0:DH, :] = row_state.astype(BF16)
    ymsg[1, 0:DH, :] = row_grad.astype(BF16)
    for n, term in enumerate(split_log(row_level)):
        ymsg[0, DH + 16 * n : DH + 16 * (n + 1), :] = term
        ymsg[1, DH + 16 * n : DH + 16 * (n + 1), :] = term

    def state_along(dy, owner):
        kind = jnp.where(y + dy < NY, 0, 1)
        return push(
            ymsg.at[kind], yin.at[owner], y_s.at[dy - 1], y_r.at[dy - 1], at(ring(y + dy), x)
        )

    for dy in range(1, NY):
        state_along(dy, y).start()

    value_take(past_a)
    value_take(past_b)
    value_take(row_far)

    top = jnp.max(stat_m[...], axis=0, keepdims=True)
    factor = jnp.exp2((stat_m[...] - top) * (SCALE * LOG2E))
    inverse = 1.0 / jnp.sum(factor * stat_l[...], axis=0, keepdims=True)
    dots = jnp.sum(factor * stat_t[...], axis=0, keepdims=True) * inverse
    dot_ref[...] = jnp.broadcast_to(dots, dot_ref.shape)
    stat_l[...] = factor * inverse

    def state_back(b, owner):
        return push(lout.at[b], fin.at[owner], l3_s.at[b], l3_r.at[owner], at(y, b))

    def state_turn():
        for dy in range(1, NY):
            state_along(dy, ring(y - dy)).wait_recv()
        for yy in range(NY):
            @when(yy < y)
            def _():
                cp[...] = (
                    jnp.exp(join_log(yin.at[yy], DH)) * cp[...] + yin[yy, 0:DH, :].astype(F32)
                )
        for yy in range(NY - 1, -1, -1):
            @when(yy > y)
            def _():
                cg[...] = (
                    jnp.exp(join_log(yin.at[yy], DH)) * cg[...] + yin[yy, 0:DH, :].astype(F32)
                )
        factors = [jnp.exp(join_log(lin.at[b], 2 * DH)) for b in range(NX)]
        carried = cp[...]
        for b in range(NX):
            lout[b, 0:DH, :] = carried.astype(BF16)
            carried = factors[b] * carried + lin[b, 0:DH, :].astype(F32)
        carried = cg[...]
        for b in range(NX - 1, -1, -1):
            lout[b, DH : 2 * DH, :] = carried.astype(BF16)
            carried = factors[b] * carried + lin[b, DH : 2 * DH, :].astype(F32)
        for b in range(NX):
            @when(b != x)
            def _():
                state_back(b, x).start()
        fin[x] = lout[x]

    def grad_ring(place, b, turn):
        return push(
            dkp.at[place, b], rbuf.at[place, b], dr_s.at[place, b], dr_r.at[place, b],
            at(ring(y + turn), x),
        )

    def grad_sent(row, turn, sender, far):
        return jnp.where(turn < 0, row < sender, row < far)

    def dv_across(row, i, straight):
        owner = col((sigma, -sigma, 2)[i])
        target = owner if i < 2 else jnp.where(straight, owner, col(sigma))
        return push(
            dvp.at[row, owner], vr.at[row, i], du_s.at[row, i], du_r.at[row, i], at(y, target)
        )

    def dv_ring(place, turn):
        return push(
            vsum.at[place], vfin.at[place], dw_s.at[place], dw_r.at[place], at(ring(y + turn), x)
        )

    def dv_relay(row):
        @when(row <= y)
        def _():
            dv_across(row, 2, False).wait_recv()
            dvp[row, col(sigma)] = (
                dvp[row, col(sigma)].astype(F32) + vr[row, 2].astype(F32)
            ).astype(BF16)
            dv_across(row, 0, False).start()

    def dv_sum(row):
        dv_across(row, 0, False).wait_recv()
        dv_across(row, 1, False).wait_recv()
        return dvp[row, x].astype(F32) + vr[row, 0].astype(F32) + vr[row, 1].astype(F32)

    def place_row(place):
        forth = (lax.rem(place, 2) == 1) | (place == 0)
        turn = jnp.where(forth, sigma, -sigma)
        far = jnp.where(forth, 4, 3)
        return turn, far, ring(y + turn * (4 - lax.div(place + 1, 2)))

    def earlier(place):
        return jnp.where(place == 1, 0, jnp.maximum(place - 2, 0))

    def dv_turn(place):
        turn, far, row = place_row(place)
        sends = grad_sent(row, turn, y, far)

        @when(row < y)
        def _():
            vacc[...] = dv_sum(row)

        @when(row > y)
        def _():
            vacc[...] = jnp.zeros_like(vacc)

        @when((place != 0) & (place != 2) & grad_sent(row, turn, ring(y - turn), far))
        def _():
            dv_ring(earlier(place), turn).wait_recv()
            vacc[...] += vfin[earlier(place)].astype(F32)

        @when(sends)
        def _():
            vsum[place] = vacc[...].astype(BF16)
            dv_ring(place, turn).start()

    def back_turn(place, _):
        turn, far, row = place_row(place)

        @when(row <= y)
        def _():
            for b in range(NX):
                rows = slice(b * ROWS, (b + 1) * ROWS)
                for cols in halves:
                    weights = e_ref[row, rows, cols] * stat_l[pl.ds(row * NX + b, 1), cols]
                    grads = weights * (dp_ref[row, rows, cols] - dot_ref[0:1, cols])
                    wb_ref[rows, cols] = weights.astype(BF16)
                    ds_ref[rows, cols] = grads.astype(BF16)
                dkf[b] = mm(ds_ref[rows, :], qs[...]) * SCALE
                dvp[row, b] = mm(wb_ref[rows, :], gs[...]).astype(BF16)
            dv_across(row, 2, place == NY - 1).start()
            dv_across(row, 1, False).start()

            @when(place == NY - 1)
            def _():
                dv_across(row, 0, False).start()

        @when(row > y)
        def _():
            dkf[...] = jnp.zeros_like(dkf)

        before = earlier(place)
        takes = (place != 0) & (place != 2) & (place != NY - 1)
        takes = takes & grad_sent(row, turn, ring(y - turn), far)
        sends = (place < NY - 1) & grad_sent(row, turn, y, far)

        def ring_block(b, _):
            @when(takes)
            def _():
                grad_ring(before, b, turn).wait_recv()
                dkf[b] += rbuf[before, b].astype(F32)

            @when(sends)
            def _():
                dkp[place, b] = dkf[b].astype(BF16)
                grad_ring(place, b, turn).start()

            return 0

        lax.fori_loop(0, NX, ring_block, 0)

        @when(row <= y)
        def _():
            out_t[...] += mm_tn(vg[row].reshape(SPAN, DH), wb_ref[...])
            dq_t[...] += mm_tn(kg[row].reshape(SPAN, DH), ds_ref[...])

        @when(place >= 1)
        def _():
            dv_relay(place_row(place - 1)[2])

        @when(place >= 2)
        def _():
            dv_turn(place - 2)

        @when(place == 2)
        def _():
            state_turn()

        return 0

    lax.fori_loop(0, NY, back_turn, 0)

    for b in range(NX):
        @when(b != x)
        def _():
            push(lout.at[b], fin.at[b], l3_s.at[b], l3_r.at[b], at(y, b)).wait_recv()

    def light_out(h, _):
        cols = pl.ds(pl.multiple_of(h * DH, DH), DH)
        qh, kh, vh, gh = q_l[:, cols], k_l[:, cols], v_l[:, cols], g_l[:, cols]
        level = lall[:, cols]
        entering = jnp.exp(level) * SCALE
        fading = jnp.exp(level[ROWS - 1 : ROWS, :] - level) * SCALE
        prior = fin[h, 0:DH, :]
        later = fin[h, DH : 2 * DH, :]
        o_l[:, cols] = (intra[0, :, cols] + entering * mm(qh, prior)).astype(BF16)
        dq_l[:, cols] = (intra[1, :, cols] + entering * mm_nt(gh, prior)).astype(BF16)
        dk_l[:, cols] = (intra[2, :, cols] + fading * mm_nt(vh, later)).astype(BF16)
        dv_l[:, cols] = (intra[3, :, cols] + fading * mm(kh, later)).astype(BF16)
        return 0

    lax.fori_loop(0, HEADS // 2, light_out, 0)
    dv_turn(NY - 2)
    lax.fori_loop(HEADS // 2, HEADS, light_out, 0)
    moves = [(o_l, o_hbm), (dq_l, dq_hbm), (dk_l, dk_hbm), (dv_l, dv_hbm)]
    moves += [(o_s, os_hbm), (dq_s, dqs_hbm), (dk_s, dks_hbm), (dv_s, dvs_hbm)]
    stores = [
        pltpu.make_async_copy(src, dst, out_s.at[n]) for n, (src, dst) in enumerate(moves)
    ]
    for store in stores[:4]:
        store.start()

    for dx in range(1, NX):
        key_across(dx, x).wait_send()

    def sent_turn(place, _):
        odd = lax.rem(place, 2) == 1
        turn = jnp.where(odd, sigma, -sigma)
        row = ring(y - turn * (lax.div(place + 1, 2) - 1))

        @when(wanted(row, turn, ring(y + turn), jnp.where(odd, 4, 3)))
        def _():
            for j in range(NX + 1):
                key_ring(place, row, j, turn).wait_send()

        turn_back, far_back, row_back = place_row(place - 1)

        @when(grad_sent(row_back, turn_back, y, far_back))
        def _():
            for j in range(NX):
                grad_ring(place - 1, j, turn_back).wait_send()
            dv_ring(place - 1, turn_back).wait_send()

        return 0

    lax.fori_loop(1, NY, sent_turn, 0)
    for dy in range(1, NY):
        state_along(dy, y).wait_send()
    for b in range(NX):
        @when(b != x)
        def _():
            light_send(b, x).wait_send()
            state_back(b, x).wait_send()
    for row in range(NY):
        @when(row <= y)
        def _():
            for i in range(3):
                value_across(row, i, x).wait_send()
                dv_across(row, i, False).wait_send()

    def dk_across(dx):
        return push(
            dks.at[col(dx)], kfin.at[dx - 1], kf_s.at[dx - 1], kf_r.at[dx - 1], at(y, col(dx))
        )

    for j in (1, 2, 3, 0):
        b = col(j)
        for place, turn, far in ((NY - 3, sigma, 4), (NY - 2, -sigma, 3)):
            @when(grad_sent(y, turn, ring(y - turn), far))
            def _():
                grad_ring(place, b, turn).wait_recv()
                dkf[b] += rbuf[place, b].astype(F32)
        if j:
            dks[b] = dkf[b].astype(BF16)
            dk_across(j).start()

    for part in parts:
        o_s[:, part] = out_t[:, part].T.astype(BF16)
        dq_s[:, part] = (dq_t[:, part].T * SCALE).astype(BF16)
    stores[4].start()
    stores[5].start()

    dv_across(y, 2, True).wait_recv()
    vacc[...] = dv_sum(y) + vr[y, 2].astype(F32)
    for place, turn, far in ((NY - 3, sigma, 4), (NY - 2, -sigma, 3)):
        @when(grad_sent(y, turn, ring(y - turn), far))
        def _():
            dv_ring(place, turn).wait_recv()
            vacc[...] += vfin[place].astype(F32)
    dv_s[...] = vacc[...].astype(BF16)
    stores[7].start()

    for dx in range(1, NX):
        dk_across(dx).wait_recv()
    dk_s[...] = (
        dkf[x] + kfin[0].astype(F32) + kfin[1].astype(F32) + kfin[2].astype(F32)
    ).astype(BF16)
    stores[6].start()

    for dx in range(1, NX):
        dk_across(dx).wait_send()
    for store in stores:
        store.wait()


def copy_out(*refs):
    ins, outs, held, sems = refs[:8], refs[8:16], refs[16:24], refs[24]
    reads = [pltpu.make_async_copy(a, b, sems.at[0, n]) for n, (a, b) in enumerate(zip(ins, held))]
    writes = [
        pltpu.make_async_copy(a, b, sems.at[1, n]) for n, (a, b) in enumerate(zip(held, outs))
    ]
    for read in reads:
        read.start()
    for read, write in zip(reads, writes):
        read.wait()
        write.start()
    for write in writes:
        write.wait()


def shards(q_light, k_light, v_light, g_light, log_decay, q_soft, k_soft, v_soft, g_soft):
    dma = pltpu.SemaphoreType.DMA
    wide = jax.ShapeDtypeStruct((ROWS, WIDE), BF16)
    narrow = jax.ShapeDtypeStruct((ROWS, DH), BF16)
    scratch = [pltpu.VMEM((ROWS, WIDE), BF16)] * 6 + [pltpu.VMEM((ROWS, DH), BF16)] * 2
    scratch += [
        pltpu.VMEM((ROWS, WIDE), BF16),
        pltpu.VMEM((ROWS, WIDE), BF16),
        pltpu.VMEM((ROWS, WIDE), BF16),
        pltpu.VMEM((ROWS, WIDE), BF16),
        pltpu.VMEM((HEADS, ROWS), F32),
        pltpu.VMEM((WIDE, DH), BF16),
        pltpu.VMEM((WIDE, DH), BF16),
        pltpu.VMEM((DH, WIDE), BF16),
        pltpu.VMEM((DH, WIDE), BF16),
        pltpu.VMEM((NY, NX, ROWS, DH), BF16),
        pltpu.VMEM((NY, NX, ROWS, DH), BF16),
        pltpu.VMEM((NY, SPAN, WIDE), F32),
        pltpu.VMEM((NY, SPAN, WIDE), F32),
        pltpu.VMEM((NY * NX, WIDE), F32),
        pltpu.VMEM((NY * NX, WIDE), F32),
        pltpu.VMEM((NY * NX, WIDE), F32),
        pltpu.VMEM((8, WIDE), F32),
        pltpu.VMEM((SPAN, WIDE), BF16),
        pltpu.VMEM((SPAN, WIDE), BF16),
        pltpu.VMEM((DH, WIDE), F32),
        pltpu.VMEM((DH, WIDE), F32),
        pltpu.VMEM((NX, ROWS, DH), F32),
        pltpu.VMEM((NY - 1, NX, ROWS, DH), BF16),
        pltpu.VMEM((NY - 1, NX, ROWS, DH), BF16),
        pltpu.VMEM((NY, NX, ROWS, DH), BF16),
        pltpu.VMEM((NY, NX - 1, ROWS, DH), BF16),
        pltpu.VMEM((NY - 1, ROWS, DH), BF16),
        pltpu.VMEM((NY - 1, ROWS, DH), BF16),
        pltpu.VMEM((ROWS, DH), F32),
        pltpu.VMEM((NX - 1, ROWS, DH), BF16),
        pltpu.VMEM((NX, ROWS, DH), BF16),
        pltpu.VMEM((HEADS, ROWS), F32),
        pltpu.VMEM((ROWS, WIDE), F32),
        pltpu.VMEM((4, ROWS, WIDE), F32),
        pltpu.VMEM((HEADS, 2 * DH + 48, DH), BF16),
        pltpu.VMEM((NX, 2 * DH + 48, DH), BF16),
        pltpu.VMEM((2, DH + 48, DH), BF16),
        pltpu.VMEM((NY, DH + 48, DH), BF16),
        pltpu.VMEM((DH, DH), F32),
        pltpu.VMEM((DH, DH), F32),
        pltpu.VMEM((NX, 2 * DH, DH), BF16),
        pltpu.VMEM((HEADS, 2 * DH, DH), BF16),
        dma((15,)),
        dma((8,)),
        dma((NX - 1,)), dma((NX - 1,)),
        dma((NY - 1, NX + 1)), dma((NY - 1, NX + 1)),
        dma((NY, NX - 1)), dma((NY, NX - 1)),
        dma((NX,)), dma((NX,)),
        dma((NY - 1,)), dma((NY - 1,)),
        dma((NX,)), dma((NX,)),
        dma((NY - 1, NX)), dma((NY - 1, NX)),
        dma((NY, NX - 1)), dma((NY, NX - 1)),
        dma((NY - 1,)), dma((NY - 1,)),
        dma((NX - 1,)), dma((NX - 1,)),
    ]
    hbm = pl.BlockSpec(memory_space=pltpu.HBM)
    room = 62 * 1024 * 1024
    shapes = (wide, wide, wide, wide, wide, wide, narrow, narrow)
    results = pl.pallas_call(
        kernel,
        out_shape=shapes,
        in_specs=[hbm] * 9,
        out_specs=(hbm,) * 8,
        scratch_shapes=scratch,
        compiler_params=pltpu.CompilerParams(
            collective_id=0, has_side_effects=True, vmem_limit_bytes=room
        ),
    )(q_light, k_light, v_light, g_light, log_decay.T, q_soft, k_soft, v_soft, g_soft)
    return pl.pallas_call(
        copy_out,
        out_shape=shapes,
        in_specs=[hbm] * 8,
        out_specs=(hbm,) * 8,
        scratch_shapes=[pltpu.VMEM(shape.shape, BF16) for shape in shapes] + [dma((2, 8))],
        compiler_params=pltpu.CompilerParams(vmem_limit_bytes=room),
    )(*results)


def solution(mesh):
    spec = P(("dp", "ctx"), "tp")
    return jax.shard_map(
        shards, mesh=mesh, in_specs=(spec,) * 9, out_specs=(spec,) * 8, check_vma=False
    )
```

```python
import jax
import jax.numpy as jnp
from jax import lax
from jax.experimental import pallas as pl
from jax.experimental.pallas import tpu as pltpu
from jax.sharding import PartitionSpec as P

DH = 128
ROWS = 128
NX = 4
NY = 8
HEADS = 4
WIDE = HEADS * DH
SPAN = NX * ROWS
SCALE = DH**-0.5
LOG2E = 1.4426950408889634
MASKED = -1e30
F32 = jnp.float32
BF16 = jnp.bfloat16


def mm(a, b):
    return jnp.dot(a, b, preferred_element_type=F32)


def mm_nt(a, b):
    return lax.dot_general(a, b, (((1,), (1,)), ((), ())), preferred_element_type=F32)


def mm_tn(a, b):
    return lax.dot_general(a, b, (((0,), (0,)), ((), ())), preferred_element_type=F32)


def push(src, dst, send, recv, target):
    return pltpu.make_async_remote_copy(
        src_ref=src,
        dst_ref=dst,
        send_sem=send,
        recv_sem=recv,
        device_id={"ctx": target},
        device_id_type=pl.DeviceIdType.MESH,
    )


def split_log(total):
    high = total.astype(BF16)
    rest = total - high.astype(F32)
    middle = rest.astype(BF16)
    low = (rest - middle.astype(F32)).astype(BF16)
    return high, middle, low


def join_log(ref, first):
    return (
        ref[first : first + 16, :].astype(F32)
        + ref[first + 16 : first + 32, :].astype(F32)
        + ref[first + 32 : first + 48, :].astype(F32)
    )[0:1, :]


def kernel(
    q_hbm, k_hbm, v_hbm, g_hbm, ld_hbm, qs_hbm, ks_hbm, vs_hbm, gs_hbm,
    o_hbm, dq_hbm, dk_hbm, dv_hbm, os_hbm, dqs_hbm, dks_hbm, dvs_hbm,
    o_l, dq_l, dk_l, dv_l, o_s, dq_s, dk_s, dv_s,
    q_l, k_l, v_l, g_l, ld, qs, gs, qs_t, gs_t,
    kg, vg, e_ref, dp_ref, stat_m, stat_l, stat_t, dot_ref, wb_ref, ds_ref,
    out_t, dq_t, dkf, dkp, rbuf, dvp, vr, vsum, vfin, vacc, kfin, dks,
    lrow, lall, intra, lmsg, lin, ymsg, yin, cp, cg, lout, fin,
    in_s, out_s, kx_s, kx_r, kr_s, kr_r, vx_s, vx_r,
    l1_s, l1_r, y_s, y_r, l3_s, l3_r,
    dr_s, dr_r, du_s, du_r, dw_s, dw_r, kf_s, kf_r,
):
    me = lax.axis_index("ctx")
    y = lax.div(me, NX)
    x = lax.rem(me, NX)
    sigma = -1

    def ring(value):
        return lax.rem(value + 2 * NY, NY)

    def at(yy, xx):
        return yy * NX + xx

    def col(step):
        return lax.rem(x + step + NX, NX)

    def when(condition):
        return pl.when(condition)

    barrier = pltpu.get_barrier_semaphore()
    for dx in range(1, NX):
        pl.semaphore_signal(
            barrier, inc=1, device_id={"ctx": at(y, col(dx))},
            device_id_type=pl.DeviceIdType.MESH,
        )
    for dy in range(1, NY):
        pl.semaphore_signal(
            barrier, inc=1, device_id={"ctx": at(ring(y + dy), x)},
            device_id_type=pl.DeviceIdType.MESH,
        )

    parts = [slice(h * DH, (h + 1) * DH) for h in range(HEADS)]
    moves = [(ks_hbm, kg.at[y, x]), (vs_hbm, vg.at[y, x]), (ld_hbm, ld)]
    moves += [(qs_hbm.at[:, part], qs.at[part, :]) for part in parts]
    moves += [(gs_hbm.at[:, part], gs.at[part, :]) for part in parts]
    moves += [(q_hbm, q_l), (k_hbm, k_l), (v_hbm, v_l), (g_hbm, g_l)]
    fetches = [
        pltpu.make_async_copy(src, dst, in_s.at[n]) for n, (src, dst) in enumerate(moves)
    ]
    for fetch in fetches:
        fetch.start()

    halves = [slice(0, WIDE // 2), slice(WIDE // 2, WIDE)]
    stat_m[...] = jnp.full(stat_m.shape, MASKED, F32)
    stat_l[...] = jnp.zeros_like(stat_l)
    stat_t[...] = jnp.zeros_like(stat_t)
    out_t[...] = jnp.zeros_like(out_t)
    dq_t[...] = jnp.zeros_like(dq_t)
    cp[...] = jnp.zeros_like(cp)
    cg[...] = jnp.zeros_like(cg)
    for fetch in fetches[:3]:
        fetch.wait()
    pl.semaphore_wait(barrier, NX + NY - 2)

    def key_across(dx, owner):
        return push(
            kg.at[y, owner], kg.at[y, owner], kx_s.at[dx - 1], kx_r.at[dx - 1], at(y, col(dx))
        )

    def value_across(row, i, owner):
        return push(
            vg.at[row, owner], vg.at[row, owner], vx_s.at[row, i], vx_r.at[row, i],
            at(y, col(-sigma if i == 1 else sigma)),
        )

    def key_ring(place, row, j, turn):
        values = isinstance(j, int) and j == NX
        block = vg.at[row, x] if values else kg.at[row, col(-j)]
        return push(
            block, block, kr_s.at[place - 1, j], kr_r.at[place - 1, j], at(ring(y + turn), x)
        )

    def wanted(row, turn, target, far):
        return jnp.where(turn > 0, row < target, row < far)

    def key_start(place, row, j, turn, far):
        @when(wanted(row, turn, ring(y + turn), far))
        def _():
            key_ring(place, row, j, turn).start()

    for dx in range(1, NX):
        key_across(dx, x).start()
    for j in (NX, 0):
        key_start(1, y, j, sigma, 4)
        key_start(2, y, j, -sigma, 3)
    value_across(y, 0, x).start()
    value_across(y, 1, x).start()

    def row_scores(row, masked):
        for b in range(NX):
            rows = slice(b * ROWS, (b + 1) * ROWS)
            for cols in halves:
                scores = mm(kg[row, b], qs_t[:, cols])
                if masked:
                    key_at = lax.broadcasted_iota(jnp.int32, scores.shape, 0) + b * ROWS
                    query_at = lax.rem(lax.broadcasted_iota(jnp.int32, scores.shape, 1), ROWS)
                    scores = jnp.where(key_at <= query_at + x * ROWS, scores, MASKED)
                top = jnp.max(scores, axis=0, keepdims=True)
                grown = jnp.exp2(scores * (SCALE * LOG2E) - top * (SCALE * LOG2E))
                e_ref[row, rows, cols] = grown
                stat_m[pl.ds(row * NX + b, 1), cols] = top
                stat_l[pl.ds(row * NX + b, 1), cols] = jnp.sum(grown, axis=0, keepdims=True)

    def light_send(h, owner):
        return push(lmsg.at[h], lin.at[owner], l1_s.at[h], l1_r.at[owner], at(y, h))

    def light_head(h):
        cols = pl.ds(pl.multiple_of(h * DH, DH), DH)
        qh, kh, vh, gh = q_l[:, cols], k_l[:, cols], v_l[:, cols], g_l[:, cols]
        flat = jnp.broadcast_to(lrow[pl.ds(h, 1), :], (ROWS, ROWS))
        level = flat.T
        lall[:, cols] = level
        row_at = lax.broadcasted_iota(jnp.int32, (ROWS, ROWS), 0)
        causal = row_at >= lax.broadcasted_iota(jnp.int32, (ROWS, ROWS), 1)
        gaps = jnp.where(causal, level - flat, 0.0)
        weights = jnp.where(causal, jnp.exp(gaps), 0.0) * SCALE
        mixing = (mm_nt(qh, kh) * weights).astype(BF16)
        back_mix = (mm_nt(gh, vh) * weights).astype(BF16)
        intra[0, :, cols] = mm(mixing, vh)
        intra[1, :, cols] = mm(back_mix, kh)
        intra[2, :, cols] = mm_tn(back_mix, qh)
        intra[3, :, cols] = mm_tn(mixing, gh)
        last = level[ROWS - 1 : ROWS, :]
        fading = (kh.astype(F32) * jnp.exp(last - level)).astype(BF16)
        entering = (qh.astype(F32) * jnp.exp(level)).astype(BF16)
        lmsg[h, 0:DH, :] = mm_tn(fading, vh).astype(BF16)
        lmsg[h, DH : 2 * DH, :] = mm_tn(entering, gh).astype(BF16)
        for n, term in enumerate(split_log(jnp.broadcast_to(last, (16, DH)))):
            lmsg[h, 2 * DH + 16 * n : 2 * DH + 16 * (n + 1), :] = term

        @when(h != x)
        def _():
            light_send(h, x).start()

        @when(h == x)
        def _():
            lin[x] = lmsg[h]

    upper = (
        lax.broadcasted_iota(jnp.int32, (ROWS, ROWS), 0)
        <= lax.broadcasted_iota(jnp.int32, (ROWS, ROWS), 1)
    ).astype(F32)
    lrow[...] = jnp.dot(
        ld[...], upper, precision=lax.Precision.HIGHEST, preferred_element_type=F32
    )
    for fetch in fetches[3:]:
        fetch.wait()
    for part in parts:
        qs_t[:, part] = qs[part, :].T
        gs_t[:, part] = gs[part, :].T

    for j in range(1, NX):
        key_across(j, col(-j)).wait_recv()
        key_start(1, y, j, sigma, 4)
        key_start(2, y, j, -sigma, 3)
    row_scores(y, True)
    light_head(0)
    light_head(1)

    def key_take(place, row, j, turn, far, last):
        @when(wanted(row, turn, y, far))
        def _():
            key_ring(place, row, j, turn).wait_recv()

            @when(jnp.logical_not(last))
            def _():
                key_start(place + 2, row, j, turn, far)

    def value_pass(row):
        @when(row < y)
        def _():
            value_across(row, 0, x).start()
            value_across(row, 1, x).start()

    def value_relay(row):
        @when(row <= y)
        def _():
            value_across(row, 0, col(-sigma)).wait_recv()
            value_across(row, 2, col(-sigma)).start()

    def value_take(row):
        @when(row <= y)
        def _():
            value_across(row, 1, col(sigma)).wait_recv()
            value_across(row, 2, col(2)).wait_recv()
            for b in range(NX):
                rows = slice(b * ROWS, (b + 1) * ROWS)
                for cols in halves:
                    grads = mm(vg[row, b], gs_t[:, cols])
                    dp_ref[row, rows, cols] = grads
                    weighed = jnp.sum(grads * e_ref[row, rows, cols], axis=0, keepdims=True)
                    stat_t[pl.ds(row * NX + b, 1), cols] = weighed

    def rows_at(k):
        return ring(y - sigma * k), ring(y + sigma * k)

    def gather_turn(k, _):
        row_a, row_b = rows_at(k)
        past_a, past_b = rows_at(k - 1)
        key_take(2 * k - 1, row_a, NX, sigma, 4, k < 0)
        value_pass(row_a)
        key_take(2 * k, row_b, NX, -sigma, 3, k == 3)
        value_pass(row_b)

        def block_turn(j, _):
            key_take(2 * k - 1, row_a, j, sigma, 4, k < 0)
            key_take(2 * k, row_b, j, -sigma, 3, k == 3)
            return 0

        lax.fori_loop(0, NX, block_turn, 0)
        value_relay(past_a)

        @when(k > 1)
        def _():
            value_relay(past_b)

        @when(row_a < y)
        def _():
            row_scores(row_a, False)

        @when(row_b < y)
        def _():
            row_scores(row_b, False)

        @when(k < 3)
        def _():
            light_head(k + 1)

        value_take(past_a)

        @when(k > 1)
        def _():
            value_take(past_b)

        return 0

    lax.fori_loop(1, NY // 2, gather_turn, 0)
    past_a, past_b = rows_at(NY // 2 - 1)
    row_far = ring(y - sigma * (NY // 2))
    key_take(NY - 1, row_far, NX, sigma, 4, row_far >= 0)
    value_pass(row_far)

    def far_turn(j, _):
        key_take(NY - 1, row_far, j, sigma, 4, j >= 0)
        return 0

    lax.fori_loop(0, NX, far_turn, 0)
    value_relay(past_a)
    value_relay(past_b)

    @when(row_far < y)
    def _():
        row_scores(row_far, False)

    value_relay(row_far)

    for h in range(NX):
        @when(h != x)
        def _():
            push(lmsg.at[h], lin.at[h], l1_s.at[h], l1_r.at[h], at(y, h)).wait_recv()
    levels = [join_log(lin.at[b], 2 * DH) for b in range(NX)]
    row_state = lin[0, 0:DH, :].astype(F32)
    for b in range(1, NX):
        row_state = jnp.exp(levels[b]) * row_state + lin[b, 0:DH, :].astype(F32)
    row_grad = lin[NX - 1, DH : 2 * DH, :].astype(F32)
    for b in range(NX - 2, -1, -1):
        row_grad = jnp.exp(levels[b]) * row_grad + lin[b, DH : 2 * DH, :].astype(F32)
    row_level = jnp.broadcast_to(levels[0] + levels[1] + levels[2] + levels[3], (16, DH))
    ymsg[0, 0:DH, :] = row_state.astype(BF16)
    ymsg[1, 0:DH, :] = row_grad.astype(BF16)
    for n, term in enumerate(split_log(row_level)):
        ymsg[0, DH + 16 * n : DH + 16 * (n + 1), :] = term
        ymsg[1, DH + 16 * n : DH + 16 * (n + 1), :] = term

    def state_along(dy, owner):
        kind = jnp.where(y + dy < NY, 0, 1)
        return push(
            ymsg.at[kind], yin.at[owner], y_s.at[dy - 1], y_r.at[dy - 1], at(ring(y + dy), x)
        )

    for dy in range(1, NY):
        state_along(dy, y).start()

    value_take(past_a)
    value_take(past_b)
    value_take(row_far)

    top = jnp.max(stat_m[...], axis=0, keepdims=True)
    factor = jnp.exp2((stat_m[...] - top) * (SCALE * LOG2E))
    inverse = 1.0 / jnp.sum(factor * stat_l[...], axis=0, keepdims=True)
    dots = jnp.sum(factor * stat_t[...], axis=0, keepdims=True) * inverse
    dot_ref[...] = jnp.broadcast_to(dots, dot_ref.shape)
    stat_l[...] = factor * inverse

    def state_back(b, owner):
        return push(lout.at[b], fin.at[owner], l3_s.at[b], l3_r.at[owner], at(y, b))

    def state_turn():
        for dy in range(1, NY):
            state_along(dy, ring(y - dy)).wait_recv()
        for yy in range(NY):
            @when(yy < y)
            def _():
                cp[...] = (
                    jnp.exp(join_log(yin.at[yy], DH)) * cp[...] + yin[yy, 0:DH, :].astype(F32)
                )
        for yy in range(NY - 1, -1, -1):
            @when(yy > y)
            def _():
                cg[...] = (
                    jnp.exp(join_log(yin.at[yy], DH)) * cg[...] + yin[yy, 0:DH, :].astype(F32)
                )
        factors = [jnp.exp(join_log(lin.at[b], 2 * DH)) for b in range(NX)]
        carried = cp[...]
        for b in range(NX):
            lout[b, 0:DH, :] = carried.astype(BF16)
            carried = factors[b] * carried + lin[b, 0:DH, :].astype(F32)
        carried = cg[...]
        for b in range(NX - 1, -1, -1):
            lout[b, DH : 2 * DH, :] = carried.astype(BF16)
            carried = factors[b] * carried + lin[b, DH : 2 * DH, :].astype(F32)
        for b in range(NX):
            @when(b != x)
            def _():
                state_back(b, x).start()
        fin[x] = lout[x]

    def grad_ring(place, b, turn):
        return push(
            dkp.at[place, b], rbuf.at[place, b], dr_s.at[place, b], dr_r.at[place, b],
            at(ring(y + turn), x),
        )

    def grad_sent(row, turn, sender, far):
        return jnp.where(turn < 0, row < sender, row < far)

    def dv_across(row, i, straight):
        owner = col((sigma, -sigma, 2)[i])
        target = owner if i < 2 else jnp.where(straight, owner, col(sigma))
        return push(
            dvp.at[row, owner], vr.at[row, i], du_s.at[row, i], du_r.at[row, i], at(y, target)
        )

    def dv_ring(place, turn):
        return push(
            vsum.at[place], vfin.at[place], dw_s.at[place], dw_r.at[place], at(ring(y + turn), x)
        )

    def dv_relay(row):
        @when(row <= y)
        def _():
            dv_across(row, 2, False).wait_recv()
            dvp[row, col(sigma)] = (
                dvp[row, col(sigma)].astype(F32) + vr[row, 2].astype(F32)
            ).astype(BF16)
            dv_across(row, 0, False).start()

    def dv_sum(row):
        dv_across(row, 0, False).wait_recv()
        dv_across(row, 1, False).wait_recv()
        return dvp[row, x].astype(F32) + vr[row, 0].astype(F32) + vr[row, 1].astype(F32)

    def place_row(place):
        forth = (lax.rem(place, 2) == 1) | (place == 0)
        turn = jnp.where(forth, sigma, -sigma)
        far = jnp.where(forth, 4, 3)
        return turn, far, ring(y + turn * (4 - lax.div(place + 1, 2)))

    def earlier(place):
        return jnp.where(place == 1, 0, jnp.maximum(place - 2, 0))

    def dv_turn(place):
        turn, far, row = place_row(place)
        sends = grad_sent(row, turn, y, far)

        @when(row < y)
        def _():
            vacc[...] = dv_sum(row)

        @when(row > y)
        def _():
            vacc[...] = jnp.zeros_like(vacc)

        @when((place != 0) & (place != 2) & grad_sent(row, turn, ring(y - turn), far))
        def _():
            dv_ring(earlier(place), turn).wait_recv()
            vacc[...] += vfin[earlier(place)].astype(F32)

        @when(sends)
        def _():
            vsum[place] = vacc[...].astype(BF16)
            dv_ring(place, turn).start()

    def back_turn(place, _):
        turn, far, row = place_row(place)

        @when(row <= y)
        def _():
            for b in range(NX):
                rows = slice(b * ROWS, (b + 1) * ROWS)
                for cols in halves:
                    weights = e_ref[row, rows, cols] * stat_l[pl.ds(row * NX + b, 1), cols]
                    grads = weights * (dp_ref[row, rows, cols] - dot_ref[0:1, cols])
                    wb_ref[rows, cols] = weights.astype(BF16)
                    ds_ref[rows, cols] = grads.astype(BF16)
                dkf[b] = mm(ds_ref[rows, :], qs[...]) * SCALE
                dvp[row, b] = mm(wb_ref[rows, :], gs[...]).astype(BF16)
            dv_across(row, 2, place == NY - 1).start()
            dv_across(row, 1, False).start()

            @when(place == NY - 1)
            def _():
                dv_across(row, 0, False).start()

        @when(row > y)
        def _():
            dkf[...] = jnp.zeros_like(dkf)

        before = earlier(place)
        takes = (place != 0) & (place != 2) & (place != NY - 1)
        takes = takes & grad_sent(row, turn, ring(y - turn), far)
        sends = (place < NY - 1) & grad_sent(row, turn, y, far)

        def ring_block(b, _):
            @when(takes)
            def _():
                grad_ring(before, b, turn).wait_recv()
                dkf[b] += rbuf[before, b].astype(F32)

            @when(sends)
            def _():
                dkp[place, b] = dkf[b].astype(BF16)
                grad_ring(place, b, turn).start()

            return 0

        lax.fori_loop(0, NX, ring_block, 0)

        @when(row <= y)
        def _():
            out_t[...] += mm_tn(vg[row].reshape(SPAN, DH), wb_ref[...])
            dq_t[...] += mm_tn(kg[row].reshape(SPAN, DH), ds_ref[...])

        @when(place >= 1)
        def _():
            dv_relay(place_row(place - 1)[2])

        @when(place >= 2)
        def _():
            dv_turn(place - 2)

        @when(place == 2)
        def _():
            state_turn()

        return 0

    lax.fori_loop(0, NY, back_turn, 0)

    for b in range(NX):
        @when(b != x)
        def _():
            push(lout.at[b], fin.at[b], l3_s.at[b], l3_r.at[b], at(y, b)).wait_recv()

    def light_out(h, _):
        cols = pl.ds(pl.multiple_of(h * DH, DH), DH)
        qh, kh, vh, gh = q_l[:, cols], k_l[:, cols], v_l[:, cols], g_l[:, cols]
        level = lall[:, cols]
        entering = jnp.exp(level) * SCALE
        fading = jnp.exp(level[ROWS - 1 : ROWS, :] - level) * SCALE
        prior = fin[h, 0:DH, :]
        later = fin[h, DH : 2 * DH, :]
        o_l[:, cols] = (intra[0, :, cols] + entering * mm(qh, prior)).astype(BF16)
        dq_l[:, cols] = (intra[1, :, cols] + entering * mm_nt(gh, prior)).astype(BF16)
        dk_l[:, cols] = (intra[2, :, cols] + fading * mm_nt(vh, later)).astype(BF16)
        dv_l[:, cols] = (intra[3, :, cols] + fading * mm(kh, later)).astype(BF16)
        return 0

    lax.fori_loop(0, HEADS // 2, light_out, 0)
    dv_turn(NY - 2)
    lax.fori_loop(HEADS // 2, HEADS, light_out, 0)
    moves = [(o_l, o_hbm), (dq_l, dq_hbm), (dk_l, dk_hbm), (dv_l, dv_hbm)]
    moves += [(o_s, os_hbm), (dq_s, dqs_hbm), (dk_s, dks_hbm), (dv_s, dvs_hbm)]
    stores = [
        pltpu.make_async_copy(src, dst, out_s.at[n]) for n, (src, dst) in enumerate(moves)
    ]
    for store in stores[:4]:
        store.start()

    for dx in range(1, NX):
        key_across(dx, x).wait_send()

    def sent_turn(place, _):
        odd = lax.rem(place, 2) == 1
        turn = jnp.where(odd, sigma, -sigma)
        row = ring(y - turn * (lax.div(place + 1, 2) - 1))

        @when(wanted(row, turn, ring(y + turn), jnp.where(odd, 4, 3)))
        def _():
            for j in range(NX + 1):
                key_ring(place, row, j, turn).wait_send()

        turn_back, far_back, row_back = place_row(place - 1)

        @when(grad_sent(row_back, turn_back, y, far_back))
        def _():
            for j in range(NX):
                grad_ring(place - 1, j, turn_back).wait_send()
            dv_ring(place - 1, turn_back).wait_send()

        return 0

    lax.fori_loop(1, NY, sent_turn, 0)
    for dy in range(1, NY):
        state_along(dy, y).wait_send()
    for b in range(NX):
        @when(b != x)
        def _():
            light_send(b, x).wait_send()
            state_back(b, x).wait_send()
    for row in range(NY):
        @when(row <= y)
        def _():
            for i in range(3):
                value_across(row, i, x).wait_send()
                dv_across(row, i, False).wait_send()

    def dk_across(dx):
        return push(
            dks.at[col(dx)], kfin.at[dx - 1], kf_s.at[dx - 1], kf_r.at[dx - 1], at(y, col(dx))
        )

    for j in (1, 2, 3, 0):
        b = col(j)
        for place, turn, far in ((NY - 3, sigma, 4), (NY - 2, -sigma, 3)):
            @when(grad_sent(y, turn, ring(y - turn), far))
            def _():
                grad_ring(place, b, turn).wait_recv()
                dkf[b] += rbuf[place, b].astype(F32)
        if j:
            dks[b] = dkf[b].astype(BF16)
            dk_across(j).start()

    for part in parts:
        o_s[:, part] = out_t[:, part].T.astype(BF16)
        dq_s[:, part] = (dq_t[:, part].T * SCALE).astype(BF16)
    stores[4].start()
    stores[5].start()

    dv_across(y, 2, True).wait_recv()
    vacc[...] = dv_sum(y) + vr[y, 2].astype(F32)
    for place, turn, far in ((NY - 3, sigma, 4), (NY - 2, -sigma, 3)):
        @when(grad_sent(y, turn, ring(y - turn), far))
        def _():
            dv_ring(place, turn).wait_recv()
            vacc[...] += vfin[place].astype(F32)
    dv_s[...] = vacc[...].astype(BF16)
    stores[7].start()

    for dx in range(1, NX):
        dk_across(dx).wait_recv()
    dk_s[...] = (
        dkf[x] + kfin[0].astype(F32) + kfin[1].astype(F32) + kfin[2].astype(F32)
    ).astype(BF16)
    stores[6].start()

    for dx in range(1, NX):
        dk_across(dx).wait_send()
    for store in stores:
        store.wait()


def copy_out(*refs):
    ins, outs, held, sems = refs[:8], refs[8:16], refs[16:24], refs[24]
    reads = [pltpu.make_async_copy(a, b, sems.at[0, n]) for n, (a, b) in enumerate(zip(ins, held))]
    writes = [
        pltpu.make_async_copy(a, b, sems.at[1, n]) for n, (a, b) in enumerate(zip(held, outs))
    ]
    for read in reads:
        read.start()
    for read, write in zip(reads, writes):
        read.wait()
        write.start()
    for write in writes:
        write.wait()


def shards(q_light, k_light, v_light, g_light, log_decay, q_soft, k_soft, v_soft, g_soft):
    dma = pltpu.SemaphoreType.DMA
    wide = jax.ShapeDtypeStruct((ROWS, WIDE), BF16)
    narrow = jax.ShapeDtypeStruct((ROWS, DH), BF16)
    scratch = [pltpu.VMEM((ROWS, WIDE), BF16)] * 6 + [pltpu.VMEM((ROWS, DH), BF16)] * 2
    scratch += [
        pltpu.VMEM((ROWS, WIDE), BF16),
        pltpu.VMEM((ROWS, WIDE), BF16),
        pltpu.VMEM((ROWS, WIDE), BF16),
        pltpu.VMEM((ROWS, WIDE), BF16),
        pltpu.VMEM((HEADS, ROWS), F32),
        pltpu.VMEM((WIDE, DH), BF16),
        pltpu.VMEM((WIDE, DH), BF16),
        pltpu.VMEM((DH, WIDE), BF16),
        pltpu.VMEM((DH, WIDE), BF16),
        pltpu.VMEM((NY, NX, ROWS, DH), BF16),
        pltpu.VMEM((NY, NX, ROWS, DH), BF16),
        pltpu.VMEM((NY, SPAN, WIDE), F32),
        pltpu.VMEM((NY, SPAN, WIDE), F32),
        pltpu.VMEM((NY * NX, WIDE), F32),
        pltpu.VMEM((NY * NX, WIDE), F32),
        pltpu.VMEM((NY * NX, WIDE), F32),
        pltpu.VMEM((8, WIDE), F32),
        pltpu.VMEM((SPAN, WIDE), BF16),
        pltpu.VMEM((SPAN, WIDE), BF16),
        pltpu.VMEM((DH, WIDE), F32),
        pltpu.VMEM((DH, WIDE), F32),
        pltpu.VMEM((NX, ROWS, DH), F32),
        pltpu.VMEM((NY - 1, NX, ROWS, DH), BF16),
        pltpu.VMEM((NY - 1, NX, ROWS, DH), BF16),
        pltpu.VMEM((NY, NX, ROWS, DH), BF16),
        pltpu.VMEM((NY, NX - 1, ROWS, DH), BF16),
        pltpu.VMEM((NY - 1, ROWS, DH), BF16),
        pltpu.VMEM((NY - 1, ROWS, DH), BF16),
        pltpu.VMEM((ROWS, DH), F32),
        pltpu.VMEM((NX - 1, ROWS, DH), BF16),
        pltpu.VMEM((NX, ROWS, DH), BF16),
        pltpu.VMEM((HEADS, ROWS), F32),
        pltpu.VMEM((ROWS, WIDE), F32),
        pltpu.VMEM((4, ROWS, WIDE), F32),
        pltpu.VMEM((HEADS, 2 * DH + 48, DH), BF16),
        pltpu.VMEM((NX, 2 * DH + 48, DH), BF16),
        pltpu.VMEM((2, DH + 48, DH), BF16),
        pltpu.VMEM((NY, DH + 48, DH), BF16),
        pltpu.VMEM((DH, DH), F32),
        pltpu.VMEM((DH, DH), F32),
        pltpu.VMEM((NX, 2 * DH, DH), BF16),
        pltpu.VMEM((HEADS, 2 * DH, DH), BF16),
        dma((15,)),
        dma((8,)),
        dma((NX - 1,)), dma((NX - 1,)),
        dma((NY - 1, NX + 1)), dma((NY - 1, NX + 1)),
        dma((NY, NX - 1)), dma((NY, NX - 1)),
        dma((NX,)), dma((NX,)),
        dma((NY - 1,)), dma((NY - 1,)),
        dma((NX,)), dma((NX,)),
        dma((NY - 1, NX)), dma((NY - 1, NX)),
        dma((NY, NX - 1)), dma((NY, NX - 1)),
        dma((NY - 1,)), dma((NY - 1,)),
        dma((NX - 1,)), dma((NX - 1,)),
    ]
    hbm = pl.BlockSpec(memory_space=pltpu.HBM)
    room = 62 * 1024 * 1024
    shapes = (wide, wide, wide, wide, wide, wide, narrow, narrow)
    results = pl.pallas_call(
        kernel,
        out_shape=shapes,
        in_specs=[hbm] * 9,
        out_specs=(hbm,) * 8,
        scratch_shapes=scratch,
        compiler_params=pltpu.CompilerParams(
            collective_id=0, has_side_effects=True, vmem_limit_bytes=room
        ),
    )(q_light, k_light, v_light, g_light, log_decay.T, q_soft, k_soft, v_soft, g_soft)
    return pl.pallas_call(
        copy_out,
        out_shape=shapes,
        in_specs=[hbm] * 8,
        out_specs=(hbm,) * 8,
        scratch_shapes=[pltpu.VMEM(shape.shape, BF16) for shape in shapes] + [dma((2, 8))],
        compiler_params=pltpu.CompilerParams(vmem_limit_bytes=room),
    )(*results)


def solution(mesh):
    spec = P(("dp", "ctx"), "tp")
    return jax.shard_map(
        shards, mesh=mesh, in_specs=(spec,) * 9, out_specs=(spec,) * 8, check_vma=False
    )
```

```python
import jax
import jax.numpy as jnp
from jax import lax
from jax.experimental import pallas as pl
from jax.experimental.pallas import tpu as pltpu
from jax.sharding import PartitionSpec as P

DH = 128
ROWS = 128
NX = 4
NY = 8
HEADS = 4
WIDE = HEADS * DH
SPAN = NX * ROWS
SCALE = DH**-0.5
LOG2E = 1.4426950408889634
MASKED = -1e30
F32 = jnp.float32
BF16 = jnp.bfloat16


def mm(a, b):
    return jnp.dot(a, b, preferred_element_type=F32)


def mm_nt(a, b):
    return lax.dot_general(a, b, (((1,), (1,)), ((), ())), preferred_element_type=F32)


def mm_tn(a, b):
    return lax.dot_general(a, b, (((0,), (0,)), ((), ())), preferred_element_type=F32)


def push(src, dst, send, recv, target):
    return pltpu.make_async_remote_copy(
        src_ref=src,
        dst_ref=dst,
        send_sem=send,
        recv_sem=recv,
        device_id={"ctx": target},
        device_id_type=pl.DeviceIdType.MESH,
    )


def split_log(total):
    high = total.astype(BF16)
    rest = total - high.astype(F32)
    middle = rest.astype(BF16)
    low = (rest - middle.astype(F32)).astype(BF16)
    return high, middle, low


def join_log(ref, first):
    return (
        ref[first : first + 16, :].astype(F32)
        + ref[first + 16 : first + 32, :].astype(F32)
        + ref[first + 32 : first + 48, :].astype(F32)
    )[0:1, :]


def kernel(
    q_hbm, k_hbm, v_hbm, g_hbm, ld_hbm, qs_hbm, ks_hbm, vs_hbm, gs_hbm,
    o_hbm, dq_hbm, dk_hbm, dv_hbm, os_hbm, dqs_hbm, dks_hbm, dvs_hbm,
    o_l, dq_l, dk_l, dv_l, o_s, dq_s, dk_s, dv_s,
    q_l, k_l, v_l, g_l, ld, qa, ga, ohead, oin, qs, gs, qs_t, gs_t,
    kg, vg, e_ref, dp_ref, stat_m, stat_l, stat_t, dot_ref, wb_ref, ds_ref,
    out_t, dq_t, dkf, dkp, rbuf, dvp, vr, vsum, vfin, vacc, kfin, dks,
    lrow, lall, intra, lmsg, lin, ymsg, yin, cp, cg, lout, fin,
    qx_s, qx_r, ox_s, ox_r,
    in_s, out_s, kx_s, kx_r, kr_s, kr_r, vx_s, vx_r,
    l1_s, l1_r, y_s, y_r, l3_s, l3_r,
    dr_s, dr_r, du_s, du_r, dw_s, dw_r, kf_s, kf_r,
):
    me = lax.axis_index("ctx")
    y = lax.div(me, NX)
    x = lax.rem(me, NX)
    sigma = 1 - 2 * lax.rem(lax.axis_index("tp"), 2)

    side = jnp.where(y < NY // 2, 0, 1)
    low = jnp.minimum(y, NY - 1 - y)
    high = NY - 1 - low

    def ring(value):
        return lax.rem(value + 2 * NY, NY)

    def at(yy, xx):
        return yy * NX + xx

    def col(step):
        return lax.rem(x + step + NX, NX)

    def when(condition):
        return pl.when(condition)

    barrier = pltpu.get_barrier_semaphore()
    for dx in range(1, NX):
        pl.semaphore_signal(
            barrier, inc=1, device_id={"ctx": at(y, col(dx))},
            device_id_type=pl.DeviceIdType.MESH,
        )
    for dy in range(1, NY):
        pl.semaphore_signal(
            barrier, inc=1, device_id={"ctx": at(ring(y + dy), x)},
            device_id_type=pl.DeviceIdType.MESH,
        )

    parts = [slice(h * DH, (h + 1) * DH) for h in range(HEADS)]
    moves = [(ks_hbm, kg.at[y, x]), (vs_hbm, vg.at[y, x]), (ld_hbm, ld)]
    moves += [(qs_hbm.at[:, part], qa.at[h]) for h, part in enumerate(parts)]
    moves += [(gs_hbm.at[:, part], ga.at[h]) for h, part in enumerate(parts)]
    moves += [(q_hbm, q_l), (k_hbm, k_l), (v_hbm, v_l), (g_hbm, g_l)]
    fetches = [
        pltpu.make_async_copy(src, dst, in_s.at[n]) for n, (src, dst) in enumerate(moves)
    ]
    for fetch in fetches:
        fetch.start()

    halves = [slice(0, WIDE // 2), slice(WIDE // 2, WIDE)]
    stat_m[...] = jnp.full(stat_m.shape, MASKED, F32)
    stat_l[...] = jnp.zeros_like(stat_l)
    stat_t[...] = jnp.zeros_like(stat_t)
    out_t[...] = jnp.zeros_like(out_t)
    dq_t[...] = jnp.zeros_like(dq_t)
    cp[...] = jnp.zeros_like(cp)
    cg[...] = jnp.zeros_like(cg)
    for fetch in fetches[:11]:
        fetch.wait()
    qs[side] = qa[pl.ds(2 * side, 2)]
    gs[side] = ga[pl.ds(2 * side, 2)]
    pl.semaphore_wait(barrier, NX + NY - 2)

    def key_across(dx, owner):
        return push(
            kg.at[y, owner], kg.at[y, owner], kx_s.at[dx - 1], kx_r.at[dx - 1], at(y, col(dx))
        )

    def value_across(row, dx, owner):
        return push(
            vg.at[row, owner], vg.at[row, owner], vx_s.at[row, dx - 1], vx_r.at[row, dx - 1],
            at(y, col(dx)),
        )

    def query_swap(n):
        src, dst = ((qa, qs), (ga, gs))[n]
        return push(
            src.at[pl.ds(2 - 2 * side, 2)], dst.at[side], qx_s.at[n], qx_r.at[n],
            at(NY - 1 - y, x),
        )

    def key_ring(place, row, j, turn):
        values = isinstance(j, int) and j == NX
        block = vg.at[row, x] if values else kg.at[row, col(-j)]
        return push(
            block, block, kr_s.at[place - 1, j], kr_r.at[place - 1, j], at(ring(y + turn), x)
        )

    for dx in range(1, NX):
        key_across(dx, x).start()
    for j in (NX, 0):
        key_ring(1, y, j, sigma).start()
        key_ring(2, y, j, -sigma).start()
    for n in range(2):
        query_swap(n).start()
    for dx in range(1, NX):
        value_across(y, dx, x).start()

    def part_scores(row, s, masked):
        for b in range(NX):
            scores = mm(kg[row, b], qs_t[s])
            if masked:
                key_at = lax.broadcasted_iota(jnp.int32, scores.shape, 0) + b * ROWS
                query_at = lax.rem(lax.broadcasted_iota(jnp.int32, scores.shape, 1), ROWS)
                scores = jnp.where(key_at <= query_at + x * ROWS, scores, MASKED)
            top = jnp.max(scores, axis=0, keepdims=True)
            grown = jnp.exp2(scores * (SCALE * LOG2E) - top * (SCALE * LOG2E))
            e_ref[row, b * ROWS : (b + 1) * ROWS, halves[s]] = grown
            stat_m[pl.ds(row * NX + b, 1), halves[s]] = top
            stat_l[pl.ds(row * NX + b, 1), halves[s]] = jnp.sum(grown, axis=0, keepdims=True)

    def row_scores(row):
        @when(row < low)
        def _():
            part_scores(row, 0, False)
            part_scores(row, 1, False)

        @when(row == low)
        def _():
            part_scores(row, 0, True)
            part_scores(row, 1, False)

        @when((row > low) & (row < high))
        def _():
            part_scores(row, 1, False)

        @when(row == high)
        def _():
            part_scores(row, 1, True)

    def part_grads(row, s):
        for b in range(NX):
            rows = slice(b * ROWS, (b + 1) * ROWS)
            grads = mm(vg[row, b], gs_t[s])
            dp_ref[row, rows, halves[s]] = grads
            weighed = jnp.sum(grads * e_ref[row, rows, halves[s]], axis=0, keepdims=True)
            stat_t[pl.ds(row * NX + b, 1), halves[s]] = weighed

    def light_send(h, owner):
        return push(lmsg.at[h], lin.at[owner], l1_s.at[h], l1_r.at[owner], at(y, h))

    def light_head(h):
        cols = pl.ds(pl.multiple_of(h * DH, DH), DH)
        qh, kh, vh, gh = q_l[:, cols], k_l[:, cols], v_l[:, cols], g_l[:, cols]
        flat = jnp.broadcast_to(lrow[pl.ds(h, 1), :], (ROWS, ROWS))
        level = flat.T
        lall[:, cols] = level
        row_at = lax.broadcasted_iota(jnp.int32, (ROWS, ROWS), 0)
        causal = row_at >= lax.broadcasted_iota(jnp.int32, (ROWS, ROWS), 1)
        gaps = jnp.where(causal, level - flat, 0.0)
        weights = jnp.where(causal, jnp.exp(gaps), 0.0) * SCALE
        mixing = (mm_nt(qh, kh) * weights).astype(BF16)
        back_mix = (mm_nt(gh, vh) * weights).astype(BF16)
        intra[0, :, cols] = mm(mixing, vh)
        intra[1, :, cols] = mm(back_mix, kh)
        intra[2, :, cols] = mm_tn(back_mix, qh)
        intra[3, :, cols] = mm_tn(mixing, gh)
        last = level[ROWS - 1 : ROWS, :]
        fading = (kh.astype(F32) * jnp.exp(last - level)).astype(BF16)
        entering = (qh.astype(F32) * jnp.exp(level)).astype(BF16)
        lmsg[h, 0:DH, :] = mm_tn(fading, vh).astype(BF16)
        lmsg[h, DH : 2 * DH, :] = mm_tn(entering, gh).astype(BF16)
        for n, term in enumerate(split_log(jnp.broadcast_to(last, (16, DH)))):
            lmsg[h, 2 * DH + 16 * n : 2 * DH + 16 * (n + 1), :] = term

        @when(h != x)
        def _():
            light_send(h, x).start()

        @when(h == x)
        def _():
            lin[x] = lmsg[h]

    upper = (
        lax.broadcasted_iota(jnp.int32, (ROWS, ROWS), 0)
        <= lax.broadcasted_iota(jnp.int32, (ROWS, ROWS), 1)
    ).astype(F32)
    lrow[...] = jnp.dot(
        ld[...], upper, precision=lax.Precision.HIGHEST, preferred_element_type=F32
    )
    for fetch in fetches[11:]:
        fetch.wait()

    def turned(s):
        for i in range(2):
            qs_t[s, :, i * ROWS : (i + 1) * ROWS] = qs[s, i].T
            gs_t[s, :, i * ROWS : (i + 1) * ROWS] = gs[s, i].T

    turned(side)

    for j in range(1, NX):
        key_across(j, col(-j)).wait_recv()
        key_ring(1, y, j, sigma).start()
        key_ring(2, y, j, -sigma).start()
    light_head(0)
    for n in range(2):
        query_swap(n).wait_recv()
    turned(1 - side)
    row_scores(y)
    light_head(1)

    def key_take(place, row, j, turn, last):
        key_ring(place, row, j, turn).wait_recv()

        @when(jnp.logical_not(last))
        def _():
            key_ring(place + 2, row, j, turn).start()

    def value_pass(row):
        @when(row <= high)
        def _():
            for dx in range(1, NX):
                value_across(row, dx, x).start()

    def value_take(row):
        @when(row <= high)
        def _():
            for dx in range(1, NX):
                value_across(row, dx, col(-dx)).wait_recv()

        @when(row <= low)
        def _():
            part_grads(row, 0)
            part_grads(row, 1)

        @when((row > low) & (row <= high))
        def _():
            part_grads(row, 1)

    def rows_at(k):
        return ring(y - sigma * k), ring(y + sigma * k)

    def gather_turn(k, _):
        row_a, row_b = rows_at(k)
        past_a, past_b = rows_at(k - 1)
        key_take(2 * k - 1, row_a, NX, sigma, k < 0)
        value_pass(row_a)
        key_take(2 * k, row_b, NX, -sigma, k == 3)
        value_pass(row_b)

        def block_turn(j, _):
            key_take(2 * k - 1, row_a, j, sigma, k < 0)
            key_take(2 * k, row_b, j, -sigma, k == 3)
            return 0

        lax.fori_loop(0, NX, block_turn, 0)
        row_scores(row_a)
        row_scores(row_b)

        @when(k < 3)
        def _():
            light_head(k + 1)

        value_take(past_a)

        @when(k > 1)
        def _():
            value_take(past_b)

        return 0

    lax.fori_loop(1, NY // 2, gather_turn, 0)
    past_a, past_b = rows_at(NY // 2 - 1)
    row_far = ring(y - sigma * (NY // 2))
    key_take(NY - 1, row_far, NX, sigma, row_far >= 0)
    value_pass(row_far)

    def far_turn(j, _):
        key_take(NY - 1, row_far, j, sigma, j >= 0)
        return 0

    lax.fori_loop(0, NX, far_turn, 0)
    row_scores(row_far)

    for h in range(NX):
        @when(h != x)
        def _():
            push(lmsg.at[h], lin.at[h], l1_s.at[h], l1_r.at[h], at(y, h)).wait_recv()
    levels = [join_log(lin.at[b], 2 * DH) for b in range(NX)]
    row_state = lin[0, 0:DH, :].astype(F32)
    for b in range(1, NX):
        row_state = jnp.exp(levels[b]) * row_state + lin[b, 0:DH, :].astype(F32)
    row_grad = lin[NX - 1, DH : 2 * DH, :].astype(F32)
    for b in range(NX - 2, -1, -1):
        row_grad = jnp.exp(levels[b]) * row_grad + lin[b, DH : 2 * DH, :].astype(F32)
    row_level = jnp.broadcast_to(levels[0] + levels[1] + levels[2] + levels[3], (16, DH))
    ymsg[0, 0:DH, :] = row_state.astype(BF16)
    ymsg[1, 0:DH, :] = row_grad.astype(BF16)
    for n, term in enumerate(split_log(row_level)):
        ymsg[0, DH + 16 * n : DH + 16 * (n + 1), :] = term
        ymsg[1, DH + 16 * n : DH + 16 * (n + 1), :] = term

    def state_along(dy, owner):
        kind = jnp.where(y + dy < NY, 0, 1)
        return push(
            ymsg.at[kind], yin.at[owner], y_s.at[dy - 1], y_r.at[dy - 1], at(ring(y + dy), x)
        )

    for dy in range(1, NY):
        state_along(dy, y).start()

    value_take(past_a)
    value_take(past_b)
    value_take(row_far)

    top = jnp.max(stat_m[...], axis=0, keepdims=True)
    factor = jnp.exp2((stat_m[...] - top) * (SCALE * LOG2E))
    inverse = 1.0 / jnp.sum(factor * stat_l[...], axis=0, keepdims=True)
    dots = jnp.sum(factor * stat_t[...], axis=0, keepdims=True) * inverse
    dot_ref[...] = jnp.broadcast_to(dots, dot_ref.shape)
    stat_l[...] = factor * inverse

    def state_back(b, owner):
        return push(lout.at[b], fin.at[owner], l3_s.at[b], l3_r.at[owner], at(y, b))

    def state_turn():
        for dy in range(1, NY):
            state_along(dy, ring(y - dy)).wait_recv()
        for yy in range(NY):
            @when(yy < y)
            def _():
                cp[...] = (
                    jnp.exp(join_log(yin.at[yy], DH)) * cp[...] + yin[yy, 0:DH, :].astype(F32)
                )
        for yy in range(NY - 1, -1, -1):
            @when(yy > y)
            def _():
                cg[...] = (
                    jnp.exp(join_log(yin.at[yy], DH)) * cg[...] + yin[yy, 0:DH, :].astype(F32)
                )
        factors = [jnp.exp(join_log(lin.at[b], 2 * DH)) for b in range(NX)]
        carried = cp[...]
        for b in range(NX):
            lout[b, 0:DH, :] = carried.astype(BF16)
            carried = factors[b] * carried + lin[b, 0:DH, :].astype(F32)
        carried = cg[...]
        for b in range(NX - 1, -1, -1):
            lout[b, DH : 2 * DH, :] = carried.astype(BF16)
            carried = factors[b] * carried + lin[b, DH : 2 * DH, :].astype(F32)
        for b in range(NX):
            @when(b != x)
            def _():
                state_back(b, x).start()
        fin[x] = lout[x]

    def grad_ring(place, b, turn):
        return push(
            dkp.at[place, b], rbuf.at[place, b], dr_s.at[place, b], dr_r.at[place, b],
            at(ring(y + turn), x),
        )

    def dv_across(row, dx):
        return push(
            dvp.at[row, col(dx)], vr.at[row, dx - 1], du_s.at[row, dx - 1], du_r.at[row, dx - 1],
            at(y, col(dx)),
        )

    def dv_ring(place, turn):
        return push(
            vsum.at[place], vfin.at[place], dw_s.at[place], dw_r.at[place], at(ring(y + turn), x)
        )

    def dv_sum(row):
        for dx in range(1, NX):
            dv_across(row, dx).wait_recv()
        return (
            dvp[row, x].astype(F32)
            + vr[row, 0].astype(F32)
            + vr[row, 1].astype(F32)
            + vr[row, 2].astype(F32)
        )

    def place_row(place):
        forth = (lax.rem(place, 2) == 1) | (place == 0)
        turn = jnp.where(forth, sigma, -sigma)
        return turn, ring(y + turn * (4 - lax.div(place + 1, 2)))

    def earlier(place):
        return jnp.where(place == 1, 0, jnp.maximum(place - 2, 0))

    def dv_turn(place):
        turn, row = place_row(place)

        @when(row <= high)
        def _():
            vacc[...] = dv_sum(row)

        @when(row > high)
        def _():
            vacc[...] = jnp.zeros_like(vacc)

        @when((place != 0) & (place != 2))
        def _():
            dv_ring(earlier(place), turn).wait_recv()
            vacc[...] += vfin[earlier(place)].astype(F32)

        vsum[place] = vacc[...].astype(BF16)
        dv_ring(place, turn).start()

    def back_part(row, sides):
        for b in range(NX):
            rows = slice(b * ROWS, (b + 1) * ROWS)
            dk_part, dv_part = 0.0, 0.0
            for s in sides:
                cols = halves[s]
                weights = e_ref[row, rows, cols] * stat_l[pl.ds(row * NX + b, 1), cols]
                grads = weights * (dp_ref[row, rows, cols] - dot_ref[0:1, cols])
                wb_ref[rows, cols] = weights.astype(BF16)
                ds_ref[rows, cols] = grads.astype(BF16)
                dk_part += mm(ds_ref[rows, cols], qs[s].reshape(2 * ROWS, DH))
                dv_part += mm(wb_ref[rows, cols], gs[s].reshape(2 * ROWS, DH))
            dkf[b] = dk_part * SCALE
            dvp[row, b] = dv_part.astype(BF16)
        for dx in range(1, NX):
            dv_across(row, dx).start()

    def query_part(row, sides):
        values_t = vg[row].reshape(SPAN, DH)
        keys_t = kg[row].reshape(SPAN, DH)
        for s in sides:
            out_t[s] += mm_tn(values_t, wb_ref[:, halves[s]])
            dq_t[s] += mm_tn(keys_t, ds_ref[:, halves[s]])

    def back_turn(place, _):
        turn, row = place_row(place)

        @when(row <= low)
        def _():
            back_part(row, (0, 1))

        @when((row > low) & (row <= high))
        def _():
            back_part(row, (1,))

        @when(row > high)
        def _():
            dkf[...] = jnp.zeros_like(dkf)

        before = earlier(place)
        takes = (place != 0) & (place != 2) & (place != NY - 1)

        def ring_block(b, _):
            @when(takes)
            def _():
                grad_ring(before, b, turn).wait_recv()
                dkf[b] += rbuf[before, b].astype(F32)

            @when(place < NY - 1)
            def _():
                dkp[place, b] = dkf[b].astype(BF16)
                grad_ring(place, b, turn).start()

            return 0

        lax.fori_loop(0, NX, ring_block, 0)

        @when(row <= low)
        def _():
            query_part(row, (0, 1))

        @when((row > low) & (row <= high))
        def _():
            query_part(row, (1,))

        @when(place >= 1)
        def _():
            dv_turn(place - 1)

        @when(place == 2)
        def _():
            state_turn()

        return 0

    lax.fori_loop(0, NY, back_turn, 0)

    def turned_back(s, i):
        cols = slice(i * ROWS, (i + 1) * ROWS)
        return out_t[s, :, cols].T.astype(BF16), (dq_t[s, :, cols].T * SCALE).astype(BF16)

    def head_back(n):
        return push(ohead.at[n], oin.at[n], ox_s.at[n], ox_r.at[n], at(NY - 1 - y, x))

    for i in range(2):
        ohead[0, i], ohead[1, i] = turned_back(1 - side, i)
    for n in range(2):
        head_back(n).start()

    for b in range(NX):
        @when(b != x)
        def _():
            push(lout.at[b], fin.at[b], l3_s.at[b], l3_r.at[b], at(y, b)).wait_recv()

    def light_out(h, _):
        cols = pl.ds(pl.multiple_of(h * DH, DH), DH)
        qh, kh, vh, gh = q_l[:, cols], k_l[:, cols], v_l[:, cols], g_l[:, cols]
        level = lall[:, cols]
        entering = jnp.exp(level) * SCALE
        fading = jnp.exp(level[ROWS - 1 : ROWS, :] - level) * SCALE
        prior = fin[h, 0:DH, :]
        later = fin[h, DH : 2 * DH, :]
        o_l[:, cols] = (intra[0, :, cols] + entering * mm(qh, prior)).astype(BF16)
        dq_l[:, cols] = (intra[1, :, cols] + entering * mm_nt(gh, prior)).astype(BF16)
        dk_l[:, cols] = (intra[2, :, cols] + fading * mm_nt(vh, later)).astype(BF16)
        dv_l[:, cols] = (intra[3, :, cols] + fading * mm(kh, later)).astype(BF16)
        return 0

    lax.fori_loop(0, HEADS, light_out, 0)
    moves = [(o_l, o_hbm), (dq_l, dq_hbm), (dk_l, dk_hbm), (dv_l, dv_hbm)]
    moves += [(o_s, os_hbm), (dq_s, dqs_hbm), (dk_s, dks_hbm), (dv_s, dvs_hbm)]
    stores = [
        pltpu.make_async_copy(src, dst, out_s.at[n]) for n, (src, dst) in enumerate(moves)
    ]
    for store in stores[:4]:
        store.start()

    for dx in range(1, NX):
        key_across(dx, x).wait_send()

    def sent_turn(place, _carry):
        odd = lax.rem(place, 2) == 1
        turn = jnp.where(odd, sigma, -sigma)
        row = ring(y - turn * (lax.div(place + 1, 2) - 1))

        for j in range(NX + 1):
            key_ring(place, row, j, turn).wait_send()
        turn_back, _ = place_row(place - 1)
        for j in range(NX):
            grad_ring(place - 1, j, turn_back).wait_send()
        dv_ring(place - 1, turn_back).wait_send()
        return 0

    lax.fori_loop(1, NY, sent_turn, 0)
    for dy in range(1, NY):
        state_along(dy, y).wait_send()
    for b in range(NX):
        @when(b != x)
        def _():
            light_send(b, x).wait_send()
            state_back(b, x).wait_send()
    for n in range(2):
        query_swap(n).wait_send()
        head_back(n).wait_send()
    for row in range(NY):
        @when(row <= high)
        def _():
            for dx in range(1, NX):
                value_across(row, dx, x).wait_send()
                dv_across(row, dx).wait_send()

    def dk_across(dx):
        return push(
            dks.at[col(dx)], kfin.at[dx - 1], kf_s.at[dx - 1], kf_r.at[dx - 1], at(y, col(dx))
        )

    for j in (1, 2, 3, 0):
        b = col(j)
        for place, turn in ((NY - 3, sigma), (NY - 2, -sigma)):
            grad_ring(place, b, turn).wait_recv()
            dkf[b] += rbuf[place, b].astype(F32)
        if j:
            dks[b] = dkf[b].astype(BF16)
            dk_across(j).start()

    def head_cols(s, i):
        return pl.ds(pl.multiple_of((2 * s + i) * DH, DH), DH)

    for i in range(2):
        o_s[:, head_cols(side, i)], dq_s[:, head_cols(side, i)] = turned_back(side, i)
    for n in range(2):
        head_back(n).wait_recv()
    for i in range(2):
        o_s[:, head_cols(1 - side, i)] = oin[0, i]
        dq_s[:, head_cols(1 - side, i)] = oin[1, i]
    stores[4].start()
    stores[5].start()

    vacc[...] = dv_sum(y)
    for place, turn in ((NY - 3, sigma), (NY - 2, -sigma)):
        dv_ring(place, turn).wait_recv()
        vacc[...] += vfin[place].astype(F32)
    dv_s[...] = vacc[...].astype(BF16)
    stores[7].start()

    for dx in range(1, NX):
        dk_across(dx).wait_recv()
    dk_s[...] = (
        dkf[x] + kfin[0].astype(F32) + kfin[1].astype(F32) + kfin[2].astype(F32)
    ).astype(BF16)
    stores[6].start()

    for dx in range(1, NX):
        dk_across(dx).wait_send()
    for store in stores:
        store.wait()


def copy_out(*refs):
    ins, outs, held, sems = refs[:8], refs[8:16], refs[16:24], refs[24]
    reads = [pltpu.make_async_copy(a, b, sems.at[0, n]) for n, (a, b) in enumerate(zip(ins, held))]
    writes = [
        pltpu.make_async_copy(a, b, sems.at[1, n]) for n, (a, b) in enumerate(zip(held, outs))
    ]
    for read in reads:
        read.start()
    for read, write in zip(reads, writes):
        read.wait()
        write.start()
    for write in writes:
        write.wait()


def shards(q_light, k_light, v_light, g_light, log_decay, q_soft, k_soft, v_soft, g_soft):
    dma = pltpu.SemaphoreType.DMA
    wide = jax.ShapeDtypeStruct((ROWS, WIDE), BF16)
    narrow = jax.ShapeDtypeStruct((ROWS, DH), BF16)
    scratch = [pltpu.VMEM((ROWS, WIDE), BF16)] * 6 + [pltpu.VMEM((ROWS, DH), BF16)] * 2
    scratch += [
        pltpu.VMEM((ROWS, WIDE), BF16),
        pltpu.VMEM((ROWS, WIDE), BF16),
        pltpu.VMEM((ROWS, WIDE), BF16),
        pltpu.VMEM((ROWS, WIDE), BF16),
        pltpu.VMEM((HEADS, ROWS), F32),
        pltpu.VMEM((HEADS, ROWS, DH), BF16),
        pltpu.VMEM((HEADS, ROWS, DH), BF16),
        pltpu.VMEM((2, 2, ROWS, DH), BF16),
        pltpu.VMEM((2, 2, ROWS, DH), BF16),
        pltpu.VMEM((2, 2, ROWS, DH), BF16),
        pltpu.VMEM((2, 2, ROWS, DH), BF16),
        pltpu.VMEM((2, DH, 2 * ROWS), BF16),
        pltpu.VMEM((2, DH, 2 * ROWS), BF16),
        pltpu.VMEM((NY, NX, ROWS, DH), BF16),
        pltpu.VMEM((NY, NX, ROWS, DH), BF16),
        pltpu.VMEM((NY, SPAN, WIDE), F32),
        pltpu.VMEM((NY, SPAN, WIDE), F32),
        pltpu.VMEM((NY * NX, WIDE), F32),
        pltpu.VMEM((NY * NX, WIDE), F32),
        pltpu.VMEM((NY * NX, WIDE), F32),
        pltpu.VMEM((8, WIDE), F32),
        pltpu.VMEM((SPAN, WIDE), BF16),
        pltpu.VMEM((SPAN, WIDE), BF16),
        pltpu.VMEM((2, DH, 2 * ROWS), F32),
        pltpu.VMEM((2, DH, 2 * ROWS), F32),
        pltpu.VMEM((NX, ROWS, DH), F32),
        pltpu.VMEM((NY - 1, NX, ROWS, DH), BF16),
        pltpu.VMEM((NY - 1, NX, ROWS, DH), BF16),
        pltpu.VMEM((NY, NX, ROWS, DH), BF16),
        pltpu.VMEM((NY, NX - 1, ROWS, DH), BF16),
        pltpu.VMEM((NY - 1, ROWS, DH), BF16),
        pltpu.VMEM((NY - 1, ROWS, DH), BF16),
        pltpu.VMEM((ROWS, DH), F32),
        pltpu.VMEM((NX - 1, ROWS, DH), BF16),
        pltpu.VMEM((NX, ROWS, DH), BF16),
        pltpu.VMEM((HEADS, ROWS), F32),
        pltpu.VMEM((ROWS, WIDE), F32),
        pltpu.VMEM((4, ROWS, WIDE), F32),
        pltpu.VMEM((HEADS, 2 * DH + 48, DH), BF16),
        pltpu.VMEM((NX, 2 * DH + 48, DH), BF16),
        pltpu.VMEM((2, DH + 48, DH), BF16),
        pltpu.VMEM((NY, DH + 48, DH), BF16),
        pltpu.VMEM((DH, DH), F32),
        pltpu.VMEM((DH, DH), F32),
        pltpu.VMEM((NX, 2 * DH, DH), BF16),
        pltpu.VMEM((HEADS, 2 * DH, DH), BF16),
        dma((2,)), dma((2,)),
        dma((2,)), dma((2,)),
        dma((15,)),
        dma((8,)),
        dma((NX - 1,)), dma((NX - 1,)),
        dma((NY - 1, NX + 1)), dma((NY - 1, NX + 1)),
        dma((NY, NX - 1)), dma((NY, NX - 1)),
        dma((NX,)), dma((NX,)),
        dma((NY - 1,)), dma((NY - 1,)),
        dma((NX,)), dma((NX,)),
        dma((NY - 1, NX)), dma((NY - 1, NX)),
        dma((NY, NX - 1)), dma((NY, NX - 1)),
        dma((NY - 1,)), dma((NY - 1,)),
        dma((NX - 1,)), dma((NX - 1,)),
    ]
    hbm = pl.BlockSpec(memory_space=pltpu.HBM)
    room = 62 * 1024 * 1024
    shapes = (wide, wide, wide, wide, wide, wide, narrow, narrow)
    results = pl.pallas_call(
        kernel,
        out_shape=shapes,
        in_specs=[hbm] * 9,
        out_specs=(hbm,) * 8,
        scratch_shapes=scratch,
        compiler_params=pltpu.CompilerParams(
            collective_id=0, has_side_effects=True, vmem_limit_bytes=room
        ),
    )(q_light, k_light, v_light, g_light, log_decay.T, q_soft, k_soft, v_soft, g_soft)
    return pl.pallas_call(
        copy_out,
        out_shape=shapes,
        in_specs=[hbm] * 8,
        out_specs=(hbm,) * 8,
        scratch_shapes=[pltpu.VMEM(shape.shape, BF16) for shape in shapes] + [dma((2, 8))],
        compiler_params=pltpu.CompilerParams(vmem_limit_bytes=room),
    )(*results)


def solution(mesh):
    spec = P(("dp", "ctx"), "tp")
    return jax.shard_map(
        shards, mesh=mesh, in_specs=(spec,) * 9, out_specs=(spec,) * 8, check_vma=False
    )
```

```python
import jax
import jax.numpy as jnp
from jax import lax
from jax.experimental import pallas as pl
from jax.experimental.pallas import tpu as pltpu
from jax.sharding import PartitionSpec as P

DH = 128
ROWS = 128
NX = 4
NY = 8
HEADS = 4
WIDE = HEADS * DH
SPAN = NX * ROWS
SCALE = DH**-0.5
LOG2E = 1.4426950408889634
MASKED = -1e30
F32 = jnp.float32
BF16 = jnp.bfloat16


def mm(a, b):
    return jnp.dot(a, b, preferred_element_type=F32)


def mm_nt(a, b):
    return lax.dot_general(a, b, (((1,), (1,)), ((), ())), preferred_element_type=F32)


def mm_tn(a, b):
    return lax.dot_general(a, b, (((0,), (0,)), ((), ())), preferred_element_type=F32)


def push(src, dst, send, recv, target):
    return pltpu.make_async_remote_copy(
        src_ref=src,
        dst_ref=dst,
        send_sem=send,
        recv_sem=recv,
        device_id={"ctx": target},
        device_id_type=pl.DeviceIdType.MESH,
    )


def split_log(total):
    high = total.astype(BF16)
    rest = total - high.astype(F32)
    middle = rest.astype(BF16)
    low = (rest - middle.astype(F32)).astype(BF16)
    return high, middle, low


def join_log(ref, first):
    return (
        ref[first : first + 16, :].astype(F32)
        + ref[first + 16 : first + 32, :].astype(F32)
        + ref[first + 32 : first + 48, :].astype(F32)
    )[0:1, :]


def kernel(
    q_hbm, k_hbm, v_hbm, g_hbm, ld_hbm, qs_hbm, ks_hbm, vs_hbm, gs_hbm,
    o_hbm, dq_hbm, dk_hbm, dv_hbm, os_hbm, dqs_hbm, dks_hbm, dvs_hbm,
    o_l, dq_l, dk_l, dv_l, o_s, dq_s, dk_s, dv_s,
    q_l, k_l, v_l, g_l, ld, qs, gs, qs_t, gs_t,
    kg, vg, e_ref, dp_ref, stat_m, stat_l, stat_t, dot_ref, wb_ref, ds_ref,
    out_t, dq_t, dkf, dkp, rbuf, dvp, vr, vsum, vfin, vacc, kfin, dks,
    lrow, lall, intra, lmsg, lin, ymsg, yin, cp, cg, lout, fin,
    in_s, out_s, kx_s, kx_r, kr_s, kr_r, vx_s, vx_r,
    l1_s, l1_r, y_s, y_r, l3_s, l3_r,
    dr_s, dr_r, du_s, du_r, dw_s, dw_r, kf_s, kf_r,
):
    me = lax.axis_index("ctx")
    y = lax.div(me, NX)
    x = lax.rem(me, NX)
    sigma = 1 - 2 * lax.rem(lax.axis_index("tp"), 2)

    def ring(value):
        return lax.rem(value + 2 * NY, NY)

    def at(yy, xx):
        return yy * NX + xx

    def col(step):
        return lax.rem(x + step + NX, NX)

    def when(condition):
        return pl.when(condition)

    barrier = pltpu.get_barrier_semaphore()
    for dx in range(1, NX):
        pl.semaphore_signal(
            barrier, inc=1, device_id={"ctx": at(y, col(dx))},
            device_id_type=pl.DeviceIdType.MESH,
        )
    for dy in range(1, NY):
        pl.semaphore_signal(
            barrier, inc=1, device_id={"ctx": at(ring(y + dy), x)},
            device_id_type=pl.DeviceIdType.MESH,
        )

    parts = [slice(h * DH, (h + 1) * DH) for h in range(HEADS)]
    moves = [(ks_hbm, kg.at[y, x]), (vs_hbm, vg.at[y, x]), (ld_hbm, ld)]
    moves += [(qs_hbm.at[:, part], qs.at[part, :]) for part in parts]
    moves += [(gs_hbm.at[:, part], gs.at[part, :]) for part in parts]
    moves += [(q_hbm, q_l), (k_hbm, k_l), (v_hbm, v_l), (g_hbm, g_l)]
    fetches = [
        pltpu.make_async_copy(src, dst, in_s.at[n]) for n, (src, dst) in enumerate(moves)
    ]
    for fetch in fetches:
        fetch.start()

    halves = [slice(0, WIDE // 2), slice(WIDE // 2, WIDE)]
    stat_m[...] = jnp.full(stat_m.shape, MASKED, F32)
    stat_l[...] = jnp.zeros_like(stat_l)
    stat_t[...] = jnp.zeros_like(stat_t)
    out_t[...] = jnp.zeros_like(out_t)
    dq_t[...] = jnp.zeros_like(dq_t)
    cp[...] = jnp.zeros_like(cp)
    cg[...] = jnp.zeros_like(cg)
    for fetch in fetches[:3]:
        fetch.wait()
    pl.semaphore_wait(barrier, NX + NY - 2)

    def key_across(dx, owner):
        return push(
            kg.at[y, owner], kg.at[y, owner], kx_s.at[dx - 1], kx_r.at[dx - 1], at(y, col(dx))
        )

    def value_across(row, dx, owner):
        return push(
            vg.at[row, owner], vg.at[row, owner], vx_s.at[row, dx - 1], vx_r.at[row, dx - 1],
            at(y, col(dx)),
        )

    def key_ring(place, row, j, turn):
        values = isinstance(j, int) and j == NX
        block = vg.at[row, x] if values else kg.at[row, col(-j)]
        return push(
            block, block, kr_s.at[place - 1, j], kr_r.at[place - 1, j], at(ring(y + turn), x)
        )

    def wanted(row, turn, target, far):
        return jnp.where(turn > 0, row < target, row < far)

    def key_start(place, row, j, turn, far):
        @when(wanted(row, turn, ring(y + turn), far))
        def _():
            key_ring(place, row, j, turn).start()

    for dx in range(1, NX):
        key_across(dx, x).start()
    for j in (NX, 0):
        key_start(1, y, j, sigma, 4)
        key_start(2, y, j, -sigma, 3)
    for dx in range(1, NX):
        value_across(y, dx, x).start()

    def row_scores(row, masked):
        for b in range(NX):
            rows = slice(b * ROWS, (b + 1) * ROWS)
            for cols in halves:
                scores = mm(kg[row, b], qs_t[:, cols])
                if masked:
                    key_at = lax.broadcasted_iota(jnp.int32, scores.shape, 0) + b * ROWS
                    query_at = lax.rem(lax.broadcasted_iota(jnp.int32, scores.shape, 1), ROWS)
                    scores = jnp.where(key_at <= query_at + x * ROWS, scores, MASKED)
                top = jnp.max(scores, axis=0, keepdims=True)
                grown = jnp.exp2(scores * (SCALE * LOG2E) - top * (SCALE * LOG2E))
                e_ref[row, rows, cols] = grown
                stat_m[pl.ds(row * NX + b, 1), cols] = top
                stat_l[pl.ds(row * NX + b, 1), cols] = jnp.sum(grown, axis=0, keepdims=True)

    def light_send(h, owner):
        return push(lmsg.at[h], lin.at[owner], l1_s.at[h], l1_r.at[owner], at(y, h))

    def light_head(h):
        cols = pl.ds(pl.multiple_of(h * DH, DH), DH)
        qh, kh, vh, gh = q_l[:, cols], k_l[:, cols], v_l[:, cols], g_l[:, cols]
        flat = jnp.broadcast_to(lrow[pl.ds(h, 1), :], (ROWS, ROWS))
        level = flat.T
        lall[:, cols] = level
        row_at = lax.broadcasted_iota(jnp.int32, (ROWS, ROWS), 0)
        causal = row_at >= lax.broadcasted_iota(jnp.int32, (ROWS, ROWS), 1)
        gaps = jnp.where(causal, level - flat, 0.0)
        weights = jnp.where(causal, jnp.exp(gaps), 0.0) * SCALE
        mixing = (mm_nt(qh, kh) * weights).astype(BF16)
        back_mix = (mm_nt(gh, vh) * weights).astype(BF16)
        intra[0, :, cols] = mm(mixing, vh)
        intra[1, :, cols] = mm(back_mix, kh)
        intra[2, :, cols] = mm_tn(back_mix, qh)
        intra[3, :, cols] = mm_tn(mixing, gh)
        last = level[ROWS - 1 : ROWS, :]
        fading = (kh.astype(F32) * jnp.exp(last - level)).astype(BF16)
        entering = (qh.astype(F32) * jnp.exp(level)).astype(BF16)
        lmsg[h, 0:DH, :] = mm_tn(fading, vh).astype(BF16)
        lmsg[h, DH : 2 * DH, :] = mm_tn(entering, gh).astype(BF16)
        for n, term in enumerate(split_log(jnp.broadcast_to(last, (16, DH)))):
            lmsg[h, 2 * DH + 16 * n : 2 * DH + 16 * (n + 1), :] = term

        @when(h != x)
        def _():
            light_send(h, x).start()

        @when(h == x)
        def _():
            lin[x] = lmsg[h]

    upper = (
        lax.broadcasted_iota(jnp.int32, (ROWS, ROWS), 0)
        <= lax.broadcasted_iota(jnp.int32, (ROWS, ROWS), 1)
    ).astype(F32)
    lrow[...] = jnp.dot(
        ld[...], upper, precision=lax.Precision.HIGHEST, preferred_element_type=F32
    )
    for fetch in fetches[3:]:
        fetch.wait()
    for part in parts:
        qs_t[:, part] = qs[part, :].T
        gs_t[:, part] = gs[part, :].T

    for j in range(1, NX):
        key_across(j, col(-j)).wait_recv()
        key_start(1, y, j, sigma, 4)
        key_start(2, y, j, -sigma, 3)
    row_scores(y, True)
    light_head(0)
    light_head(1)

    def key_take(place, row, j, turn, far, last):
        @when(wanted(row, turn, y, far))
        def _():
            key_ring(place, row, j, turn).wait_recv()

            @when(jnp.logical_not(last))
            def _():
                key_start(place + 2, row, j, turn, far)

    def value_pass(row):
        @when(row < y)
        def _():
            for dx in range(1, NX):
                value_across(row, dx, x).start()

    def value_take(row):
        @when(row <= y)
        def _():
            for dx in range(1, NX):
                value_across(row, dx, col(-dx)).wait_recv()
            for b in range(NX):
                rows = slice(b * ROWS, (b + 1) * ROWS)
                for cols in halves:
                    grads = mm(vg[row, b], gs_t[:, cols])
                    dp_ref[row, rows, cols] = grads
                    weighed = jnp.sum(grads * e_ref[row, rows, cols], axis=0, keepdims=True)
                    stat_t[pl.ds(row * NX + b, 1), cols] = weighed

    def rows_at(k):
        return ring(y - sigma * k), ring(y + sigma * k)

    def gather_turn(k, _):
        row_a, row_b = rows_at(k)
        past_a, past_b = rows_at(k - 1)
        key_take(2 * k - 1, row_a, NX, sigma, 4, k < 0)
        value_pass(row_a)
        key_take(2 * k, row_b, NX, -sigma, 3, k == 3)
        value_pass(row_b)

        def block_turn(j, _):
            key_take(2 * k - 1, row_a, j, sigma, 4, k < 0)
            key_take(2 * k, row_b, j, -sigma, 3, k == 3)
            return 0

        lax.fori_loop(0, NX, block_turn, 0)
        @when(row_a < y)
        def _():
            row_scores(row_a, False)

        @when(row_b < y)
        def _():
            row_scores(row_b, False)

        @when(k < 3)
        def _():
            light_head(k + 1)

        value_take(past_a)

        @when(k > 1)
        def _():
            value_take(past_b)

        return 0

    lax.fori_loop(1, NY // 2, gather_turn, 0)
    past_a, past_b = rows_at(NY // 2 - 1)
    row_far = ring(y - sigma * (NY // 2))
    key_take(NY - 1, row_far, NX, sigma, 4, row_far >= 0)
    value_pass(row_far)

    def far_turn(j, _):
        key_take(NY - 1, row_far, j, sigma, 4, j >= 0)
        return 0

    lax.fori_loop(0, NX, far_turn, 0)

    @when(row_far < y)
    def _():
        row_scores(row_far, False)

    for h in range(NX):
        @when(h != x)
        def _():
            push(lmsg.at[h], lin.at[h], l1_s.at[h], l1_r.at[h], at(y, h)).wait_recv()
    levels = [join_log(lin.at[b], 2 * DH) for b in range(NX)]
    row_state = lin[0, 0:DH, :].astype(F32)
    for b in range(1, NX):
        row_state = jnp.exp(levels[b]) * row_state + lin[b, 0:DH, :].astype(F32)
    row_grad = lin[NX - 1, DH : 2 * DH, :].astype(F32)
    for b in range(NX - 2, -1, -1):
        row_grad = jnp.exp(levels[b]) * row_grad + lin[b, DH : 2 * DH, :].astype(F32)
    row_level = jnp.broadcast_to(levels[0] + levels[1] + levels[2] + levels[3], (16, DH))
    ymsg[0, 0:DH, :] = row_state.astype(BF16)
    ymsg[1, 0:DH, :] = row_grad.astype(BF16)
    for n, term in enumerate(split_log(row_level)):
        ymsg[0, DH + 16 * n : DH + 16 * (n + 1), :] = term
        ymsg[1, DH + 16 * n : DH + 16 * (n + 1), :] = term

    def state_along(dy, owner):
        kind = jnp.where(y + dy < NY, 0, 1)
        return push(
            ymsg.at[kind], yin.at[owner], y_s.at[dy - 1], y_r.at[dy - 1], at(ring(y + dy), x)
        )

    for dy in range(1, NY):
        state_along(dy, y).start()

    value_take(past_a)
    value_take(past_b)
    value_take(row_far)

    top = jnp.max(stat_m[...], axis=0, keepdims=True)
    factor = jnp.exp2((stat_m[...] - top) * (SCALE * LOG2E))
    inverse = 1.0 / jnp.sum(factor * stat_l[...], axis=0, keepdims=True)
    dots = jnp.sum(factor * stat_t[...], axis=0, keepdims=True) * inverse
    dot_ref[...] = jnp.broadcast_to(dots, dot_ref.shape)
    stat_l[...] = factor * inverse

    def state_back(b, owner):
        return push(lout.at[b], fin.at[owner], l3_s.at[b], l3_r.at[owner], at(y, b))

    def state_turn():
        for dy in range(1, NY):
            state_along(dy, ring(y - dy)).wait_recv()
        for yy in range(NY):
            @when(yy < y)
            def _():
                cp[...] = (
                    jnp.exp(join_log(yin.at[yy], DH)) * cp[...] + yin[yy, 0:DH, :].astype(F32)
                )
        for yy in range(NY - 1, -1, -1):
            @when(yy > y)
            def _():
                cg[...] = (
                    jnp.exp(join_log(yin.at[yy], DH)) * cg[...] + yin[yy, 0:DH, :].astype(F32)
                )
        factors = [jnp.exp(join_log(lin.at[b], 2 * DH)) for b in range(NX)]
        carried = cp[...]
        for b in range(NX):
            lout[b, 0:DH, :] = carried.astype(BF16)
            carried = factors[b] * carried + lin[b, 0:DH, :].astype(F32)
        carried = cg[...]
        for b in range(NX - 1, -1, -1):
            lout[b, DH : 2 * DH, :] = carried.astype(BF16)
            carried = factors[b] * carried + lin[b, DH : 2 * DH, :].astype(F32)
        for b in range(NX):
            @when(b != x)
            def _():
                state_back(b, x).start()
        fin[x] = lout[x]

    def grad_ring(place, b, turn):
        return push(
            dkp.at[place, b], rbuf.at[place, b], dr_s.at[place, b], dr_r.at[place, b],
            at(ring(y + turn), x),
        )

    def grad_sent(row, turn, sender, far):
        return jnp.where(turn < 0, row < sender, row < far)

    def dv_across(row, dx):
        return push(
            dvp.at[row, col(dx)], vr.at[row, dx - 1], du_s.at[row, dx - 1], du_r.at[row, dx - 1],
            at(y, col(dx)),
        )

    def dv_ring(place, turn):
        return push(
            vsum.at[place], vfin.at[place], dw_s.at[place], dw_r.at[place], at(ring(y + turn), x)
        )

    def dv_sum(row):
        for dx in range(1, NX):
            dv_across(row, dx).wait_recv()
        return (
            dvp[row, x].astype(F32)
            + vr[row, 0].astype(F32)
            + vr[row, 1].astype(F32)
            + vr[row, 2].astype(F32)
        )

    def place_row(place):
        forth = (lax.rem(place, 2) == 1) | (place == 0)
        turn = jnp.where(forth, sigma, -sigma)
        far = jnp.where(forth, 4, 3)
        return turn, far, ring(y + turn * (4 - lax.div(place + 1, 2)))

    def earlier(place):
        return jnp.where(place == 1, 0, jnp.maximum(place - 2, 0))

    def dv_turn(place):
        turn, far, row = place_row(place)
        sends = grad_sent(row, turn, y, far)

        @when(row < y)
        def _():
            vacc[...] = dv_sum(row)

        @when(row > y)
        def _():
            vacc[...] = jnp.zeros_like(vacc)

        @when((place != 0) & (place != 2) & grad_sent(row, turn, ring(y - turn), far))
        def _():
            dv_ring(earlier(place), turn).wait_recv()
            vacc[...] += vfin[earlier(place)].astype(F32)

        @when(sends)
        def _():
            vsum[place] = vacc[...].astype(BF16)
            dv_ring(place, turn).start()

    def back_turn(place, _):
        turn, far, row = place_row(place)

        @when(row <= y)
        def _():
            for b in range(NX):
                rows = slice(b * ROWS, (b + 1) * ROWS)
                for cols in halves:
                    weights = e_ref[row, rows, cols] * stat_l[pl.ds(row * NX + b, 1), cols]
                    grads = weights * (dp_ref[row, rows, cols] - dot_ref[0:1, cols])
                    wb_ref[rows, cols] = weights.astype(BF16)
                    ds_ref[rows, cols] = grads.astype(BF16)
                dkf[b] = mm(ds_ref[rows, :], qs[...]) * SCALE
                dvp[row, b] = mm(wb_ref[rows, :], gs[...]).astype(BF16)
            for dx in range(1, NX):
                dv_across(row, dx).start()

        @when(row > y)
        def _():
            dkf[...] = jnp.zeros_like(dkf)

        before = earlier(place)
        takes = (place != 0) & (place != 2) & (place != NY - 1)
        takes = takes & grad_sent(row, turn, ring(y - turn), far)
        sends = (place < NY - 1) & grad_sent(row, turn, y, far)

        def ring_block(b, _):
            @when(takes)
            def _():
                grad_ring(before, b, turn).wait_recv()
                dkf[b] += rbuf[before, b].astype(F32)

            @when(sends)
            def _():
                dkp[place, b] = dkf[b].astype(BF16)
                grad_ring(place, b, turn).start()

            return 0

        lax.fori_loop(0, NX, ring_block, 0)

        @when(row <= y)
        def _():
            out_t[...] += mm_tn(vg[row].reshape(SPAN, DH), wb_ref[...])
            dq_t[...] += mm_tn(kg[row].reshape(SPAN, DH), ds_ref[...])

        @when(place >= 1)
        def _():
            dv_turn(place - 1)

        @when(place == 2)
        def _():
            state_turn()

        return 0

    lax.fori_loop(0, NY, back_turn, 0)

    for b in range(NX):
        @when(b != x)
        def _():
            push(lout.at[b], fin.at[b], l3_s.at[b], l3_r.at[b], at(y, b)).wait_recv()

    def light_out(h, _):
        cols = pl.ds(pl.multiple_of(h * DH, DH), DH)
        qh, kh, vh, gh = q_l[:, cols], k_l[:, cols], v_l[:, cols], g_l[:, cols]
        level = lall[:, cols]
        entering = jnp.exp(level) * SCALE
        fading = jnp.exp(level[ROWS - 1 : ROWS, :] - level) * SCALE
        prior = fin[h, 0:DH, :]
        later = fin[h, DH : 2 * DH, :]
        o_l[:, cols] = (intra[0, :, cols] + entering * mm(qh, prior)).astype(BF16)
        dq_l[:, cols] = (intra[1, :, cols] + entering * mm_nt(gh, prior)).astype(BF16)
        dk_l[:, cols] = (intra[2, :, cols] + fading * mm_nt(vh, later)).astype(BF16)
        dv_l[:, cols] = (intra[3, :, cols] + fading * mm(kh, later)).astype(BF16)
        return 0

    lax.fori_loop(0, HEADS, light_out, 0)
    moves = [(o_l, o_hbm), (dq_l, dq_hbm), (dk_l, dk_hbm), (dv_l, dv_hbm)]
    moves += [(o_s, os_hbm), (dq_s, dqs_hbm), (dk_s, dks_hbm), (dv_s, dvs_hbm)]
    stores = [
        pltpu.make_async_copy(src, dst, out_s.at[n]) for n, (src, dst) in enumerate(moves)
    ]
    for store in stores[:4]:
        store.start()

    for dx in range(1, NX):
        key_across(dx, x).wait_send()

    def sent_turn(place, _):
        odd = lax.rem(place, 2) == 1
        turn = jnp.where(odd, sigma, -sigma)
        row = ring(y - turn * (lax.div(place + 1, 2) - 1))

        @when(wanted(row, turn, ring(y + turn), jnp.where(odd, 4, 3)))
        def _():
            for j in range(NX + 1):
                key_ring(place, row, j, turn).wait_send()

        turn_back, far_back, row_back = place_row(place - 1)

        @when(grad_sent(row_back, turn_back, y, far_back))
        def _():
            for j in range(NX):
                grad_ring(place - 1, j, turn_back).wait_send()
            dv_ring(place - 1, turn_back).wait_send()

        return 0

    lax.fori_loop(1, NY, sent_turn, 0)
    for dy in range(1, NY):
        state_along(dy, y).wait_send()
    for b in range(NX):
        @when(b != x)
        def _():
            light_send(b, x).wait_send()
            state_back(b, x).wait_send()
    for row in range(NY):
        @when(row <= y)
        def _():
            for dx in range(1, NX):
                value_across(row, dx, x).wait_send()
                dv_across(row, dx).wait_send()

    def dk_across(dx):
        return push(
            dks.at[col(dx)], kfin.at[dx - 1], kf_s.at[dx - 1], kf_r.at[dx - 1], at(y, col(dx))
        )

    for j in (1, 2, 3, 0):
        b = col(j)
        for place, turn, far in ((NY - 3, sigma, 4), (NY - 2, -sigma, 3)):
            @when(grad_sent(y, turn, ring(y - turn), far))
            def _():
                grad_ring(place, b, turn).wait_recv()
                dkf[b] += rbuf[place, b].astype(F32)
        if j:
            dks[b] = dkf[b].astype(BF16)
            dk_across(j).start()

    for part in parts:
        o_s[:, part] = out_t[:, part].T.astype(BF16)
        dq_s[:, part] = (dq_t[:, part].T * SCALE).astype(BF16)
    stores[4].start()
    stores[5].start()

    vacc[...] = dv_sum(y)
    for place, turn, far in ((NY - 3, sigma, 4), (NY - 2, -sigma, 3)):
        @when(grad_sent(y, turn, ring(y - turn), far))
        def _():
            dv_ring(place, turn).wait_recv()
            vacc[...] += vfin[place].astype(F32)
    dv_s[...] = vacc[...].astype(BF16)
    stores[7].start()

    for dx in range(1, NX):
        dk_across(dx).wait_recv()
    dk_s[...] = (
        dkf[x] + kfin[0].astype(F32) + kfin[1].astype(F32) + kfin[2].astype(F32)
    ).astype(BF16)
    stores[6].start()

    for dx in range(1, NX):
        dk_across(dx).wait_send()
    for store in stores:
        store.wait()


def copy_out(*refs):
    ins, outs, held, sems = refs[:8], refs[8:16], refs[16:24], refs[24]
    reads = [pltpu.make_async_copy(a, b, sems.at[0, n]) for n, (a, b) in enumerate(zip(ins, held))]
    writes = [
        pltpu.make_async_copy(a, b, sems.at[1, n]) for n, (a, b) in enumerate(zip(held, outs))
    ]
    for read in reads:
        read.start()
    for read, write in zip(reads, writes):
        read.wait()
        write.start()
    for write in writes:
        write.wait()


def shards(q_light, k_light, v_light, g_light, log_decay, q_soft, k_soft, v_soft, g_soft):
    dma = pltpu.SemaphoreType.DMA
    wide = jax.ShapeDtypeStruct((ROWS, WIDE), BF16)
    narrow = jax.ShapeDtypeStruct((ROWS, DH), BF16)
    scratch = [pltpu.VMEM((ROWS, WIDE), BF16)] * 6 + [pltpu.VMEM((ROWS, DH), BF16)] * 2
    scratch += [
        pltpu.VMEM((ROWS, WIDE), BF16),
        pltpu.VMEM((ROWS, WIDE), BF16),
        pltpu.VMEM((ROWS, WIDE), BF16),
        pltpu.VMEM((ROWS, WIDE), BF16),
        pltpu.VMEM((HEADS, ROWS), F32),
        pltpu.VMEM((WIDE, DH), BF16),
        pltpu.VMEM((WIDE, DH), BF16),
        pltpu.VMEM((DH, WIDE), BF16),
        pltpu.VMEM((DH, WIDE), BF16),
        pltpu.VMEM((NY, NX, ROWS, DH), BF16),
        pltpu.VMEM((NY, NX, ROWS, DH), BF16),
        pltpu.VMEM((NY, SPAN, WIDE), F32),
        pltpu.VMEM((NY, SPAN, WIDE), F32),
        pltpu.VMEM((NY * NX, WIDE), F32),
        pltpu.VMEM((NY * NX, WIDE), F32),
        pltpu.VMEM((NY * NX, WIDE), F32),
        pltpu.VMEM((8, WIDE), F32),
        pltpu.VMEM((SPAN, WIDE), BF16),
        pltpu.VMEM((SPAN, WIDE), BF16),
        pltpu.VMEM((DH, WIDE), F32),
        pltpu.VMEM((DH, WIDE), F32),
        pltpu.VMEM((NX, ROWS, DH), F32),
        pltpu.VMEM((NY - 1, NX, ROWS, DH), BF16),
        pltpu.VMEM((NY - 1, NX, ROWS, DH), BF16),
        pltpu.VMEM((NY, NX, ROWS, DH), BF16),
        pltpu.VMEM((NY, NX - 1, ROWS, DH), BF16),
        pltpu.VMEM((NY - 1, ROWS, DH), BF16),
        pltpu.VMEM((NY - 1, ROWS, DH), BF16),
        pltpu.VMEM((ROWS, DH), F32),
        pltpu.VMEM((NX - 1, ROWS, DH), BF16),
        pltpu.VMEM((NX, ROWS, DH), BF16),
        pltpu.VMEM((HEADS, ROWS), F32),
        pltpu.VMEM((ROWS, WIDE), F32),
        pltpu.VMEM((4, ROWS, WIDE), F32),
        pltpu.VMEM((HEADS, 2 * DH + 48, DH), BF16),
        pltpu.VMEM((NX, 2 * DH + 48, DH), BF16),
        pltpu.VMEM((2, DH + 48, DH), BF16),
        pltpu.VMEM((NY, DH + 48, DH), BF16),
        pltpu.VMEM((DH, DH), F32),
        pltpu.VMEM((DH, DH), F32),
        pltpu.VMEM((NX, 2 * DH, DH), BF16),
        pltpu.VMEM((HEADS, 2 * DH, DH), BF16),
        dma((15,)),
        dma((8,)),
        dma((NX - 1,)), dma((NX - 1,)),
        dma((NY - 1, NX + 1)), dma((NY - 1, NX + 1)),
        dma((NY, NX - 1)), dma((NY, NX - 1)),
        dma((NX,)), dma((NX,)),
        dma((NY - 1,)), dma((NY - 1,)),
        dma((NX,)), dma((NX,)),
        dma((NY - 1, NX)), dma((NY - 1, NX)),
        dma((NY, NX - 1)), dma((NY, NX - 1)),
        dma((NY - 1,)), dma((NY - 1,)),
        dma((NX - 1,)), dma((NX - 1,)),
    ]
    hbm = pl.BlockSpec(memory_space=pltpu.HBM)
    room = 62 * 1024 * 1024
    shapes = (wide, wide, wide, wide, wide, wide, narrow, narrow)
    results = pl.pallas_call(
        kernel,
        out_shape=shapes,
        in_specs=[hbm] * 9,
        out_specs=(hbm,) * 8,
        scratch_shapes=scratch,
        compiler_params=pltpu.CompilerParams(
            collective_id=0, has_side_effects=True, vmem_limit_bytes=room
        ),
    )(q_light, k_light, v_light, g_light, log_decay.T, q_soft, k_soft, v_soft, g_soft)
    return pl.pallas_call(
        copy_out,
        out_shape=shapes,
        in_specs=[hbm] * 8,
        out_specs=(hbm,) * 8,
        scratch_shapes=[pltpu.VMEM(shape.shape, BF16) for shape in shapes] + [dma((2, 8))],
        compiler_params=pltpu.CompilerParams(vmem_limit_bytes=room),
    )(*results)


def solution(mesh):
    spec = P(("dp", "ctx"), "tp")
    return jax.shard_map(
        shards, mesh=mesh, in_specs=(spec,) * 9, out_specs=(spec,) * 8, check_vma=False
    )
```

```python
import jax
import jax.numpy as jnp
from jax import lax
from jax.experimental import pallas as pl
from jax.experimental.pallas import tpu as pltpu
from jax.sharding import PartitionSpec as P

DH = 128
ROWS = 128
NX = 4
NY = 8
HEADS = 4
WIDE = HEADS * DH
SPAN = NX * ROWS
SCALE = DH**-0.5
LOG2E = 1.4426950408889634
MASKED = -1e30
F32 = jnp.float32
BF16 = jnp.bfloat16


def mm(a, b):
    return jnp.dot(a, b, preferred_element_type=F32)


def mm_nt(a, b):
    return lax.dot_general(a, b, (((1,), (1,)), ((), ())), preferred_element_type=F32)


def mm_tn(a, b):
    return lax.dot_general(a, b, (((0,), (0,)), ((), ())), preferred_element_type=F32)


def push(src, dst, send, recv, target):
    return pltpu.make_async_remote_copy(
        src_ref=src,
        dst_ref=dst,
        send_sem=send,
        recv_sem=recv,
        device_id={"ctx": target},
        device_id_type=pl.DeviceIdType.MESH,
    )


def split_log(total):
    high = total.astype(BF16)
    rest = total - high.astype(F32)
    middle = rest.astype(BF16)
    low = (rest - middle.astype(F32)).astype(BF16)
    return high, middle, low


def join_log(ref, first):
    return (
        ref[first : first + 16, :].astype(F32)
        + ref[first + 16 : first + 32, :].astype(F32)
        + ref[first + 32 : first + 48, :].astype(F32)
    )[0:1, :]


def kernel(
    q_hbm, k_hbm, v_hbm, g_hbm, ld_hbm, qs_hbm, ks_hbm, vs_hbm, gs_hbm,
    o_hbm, dq_hbm, dk_hbm, dv_hbm, os_hbm, dqs_hbm, dks_hbm, dvs_hbm,
    o_l, dq_l, dk_l, dv_l, o_s, dq_s, dk_s, dv_s,
    q_l, k_l, v_l, g_l, ld, qs, gs, qs_t, gs_t,
    kg, vg, e_ref, dp_ref, stat_m, stat_l, stat_t, dot_ref, wb_ref, ds_ref,
    out_t, dq_t, dkf, dkp, rbuf, dvp, vr, vsum, vfin, vacc, kfin, dks,
    lrow, lall, intra, lmsg, lin, ymsg, yin, cp, cg, lout, fin,
    in_s, out_s, kx_s, kx_r, kr_s, kr_r, vx_s, vx_r,
    l1_s, l1_r, y_s, y_r, l3_s, l3_r,
    dr_s, dr_r, du_s, du_r, dw_s, dw_r, kf_s, kf_r,
):
    me = lax.axis_index("ctx")
    y = lax.div(me, NX)
    x = lax.rem(me, NX)
    sigma = 1 - 2 * lax.rem(lax.axis_index("tp"), 2)

    def ring(value):
        return lax.rem(value + 2 * NY, NY)

    def at(yy, xx):
        return yy * NX + xx

    def col(step):
        return lax.rem(x + step + NX, NX)

    def when(condition):
        return pl.when(condition)

    barrier = pltpu.get_barrier_semaphore()
    for dx in range(1, NX):
        pl.semaphore_signal(
            barrier, inc=1, device_id={"ctx": at(y, col(dx))},
            device_id_type=pl.DeviceIdType.MESH,
        )
    for dy in range(1, NY):
        pl.semaphore_signal(
            barrier, inc=1, device_id={"ctx": at(ring(y + dy), x)},
            device_id_type=pl.DeviceIdType.MESH,
        )

    parts = [slice(h * DH, (h + 1) * DH) for h in range(HEADS)]
    moves = [(ks_hbm, kg.at[y, x]), (vs_hbm, vg.at[y, x]), (ld_hbm, ld)]
    moves += [(qs_hbm.at[:, part], qs.at[part, :]) for part in parts]
    moves += [(gs_hbm.at[:, part], gs.at[part, :]) for part in parts]
    moves += [(q_hbm, q_l), (k_hbm, k_l), (v_hbm, v_l), (g_hbm, g_l)]
    fetches = [
        pltpu.make_async_copy(src, dst, in_s.at[n]) for n, (src, dst) in enumerate(moves)
    ]
    for fetch in fetches:
        fetch.start()

    halves = [slice(0, WIDE // 2), slice(WIDE // 2, WIDE)]
    stat_m[...] = jnp.full(stat_m.shape, MASKED, F32)
    stat_l[...] = jnp.zeros_like(stat_l)
    stat_t[...] = jnp.zeros_like(stat_t)
    out_t[...] = jnp.zeros_like(out_t)
    dq_t[...] = jnp.zeros_like(dq_t)
    cp[...] = jnp.zeros_like(cp)
    cg[...] = jnp.zeros_like(cg)
    for fetch in fetches[:3]:
        fetch.wait()
    pl.semaphore_wait(barrier, NX + NY - 2)

    def key_across(dx, owner):
        return push(
            kg.at[y, owner], kg.at[y, owner], kx_s.at[dx - 1], kx_r.at[dx - 1], at(y, col(dx))
        )

    def value_across(row, dx, owner):
        return push(
            vg.at[row, owner], vg.at[row, owner], vx_s.at[row, dx - 1], vx_r.at[row, dx - 1],
            at(y, col(dx)),
        )

    def key_ring(place, row, j, turn):
        values = isinstance(j, int) and j == NX
        block = vg.at[row, x] if values else kg.at[row, col(-j)]
        return push(
            block, block, kr_s.at[place - 1, j], kr_r.at[place - 1, j], at(ring(y + turn), x)
        )

    def wanted(row, turn, target, far):
        return jnp.where(turn > 0, row < target, row < far)

    def key_start(place, row, j, turn, far):
        @when(wanted(row, turn, ring(y + turn), far))
        def _():
            key_ring(place, row, j, turn).start()

    for dx in range(1, NX):
        key_across(dx, x).start()
    for j in (NX, 0):
        key_start(1, y, j, sigma, 4)
        key_start(2, y, j, -sigma, 3)
    for dx in range(1, NX):
        value_across(y, dx, x).start()

    def row_scores(row, masked):
        for b in range(NX):
            rows = slice(b * ROWS, (b + 1) * ROWS)
            for cols in halves:
                scores = mm(kg[row, b], qs_t[:, cols])
                if masked:
                    key_at = lax.broadcasted_iota(jnp.int32, scores.shape, 0) + b * ROWS
                    query_at = lax.rem(lax.broadcasted_iota(jnp.int32, scores.shape, 1), ROWS)
                    scores = jnp.where(key_at <= query_at + x * ROWS, scores, MASKED)
                top = jnp.max(scores, axis=0, keepdims=True)
                grown = jnp.exp2(scores * (SCALE * LOG2E) - top * (SCALE * LOG2E))
                e_ref[row, rows, cols] = grown
                stat_m[pl.ds(row * NX + b, 1), cols] = top
                stat_l[pl.ds(row * NX + b, 1), cols] = jnp.sum(grown, axis=0, keepdims=True)

    def light_send(h, owner):
        return push(lmsg.at[h], lin.at[owner], l1_s.at[h], l1_r.at[owner], at(y, h))

    def light_head(h):
        cols = pl.ds(pl.multiple_of(h * DH, DH), DH)
        qh, kh, vh, gh = q_l[:, cols], k_l[:, cols], v_l[:, cols], g_l[:, cols]
        flat = jnp.broadcast_to(lrow[pl.ds(h, 1), :], (ROWS, ROWS))
        level = flat.T
        lall[:, cols] = level
        row_at = lax.broadcasted_iota(jnp.int32, (ROWS, ROWS), 0)
        causal = row_at >= lax.broadcasted_iota(jnp.int32, (ROWS, ROWS), 1)
        gaps = jnp.where(causal, level - flat, 0.0)
        weights = jnp.where(causal, jnp.exp(gaps), 0.0) * SCALE
        mixing = (mm_nt(qh, kh) * weights).astype(BF16)
        back_mix = (mm_nt(gh, vh) * weights).astype(BF16)
        intra[0, :, cols] = mm(mixing, vh)
        intra[1, :, cols] = mm(back_mix, kh)
        intra[2, :, cols] = mm_tn(back_mix, qh)
        intra[3, :, cols] = mm_tn(mixing, gh)
        last = level[ROWS - 1 : ROWS, :]
        fading = (kh.astype(F32) * jnp.exp(last - level)).astype(BF16)
        entering = (qh.astype(F32) * jnp.exp(level)).astype(BF16)
        lmsg[h, 0:DH, :] = mm_tn(fading, vh).astype(BF16)
        lmsg[h, DH : 2 * DH, :] = mm_tn(entering, gh).astype(BF16)
        for n, term in enumerate(split_log(jnp.broadcast_to(last, (16, DH)))):
            lmsg[h, 2 * DH + 16 * n : 2 * DH + 16 * (n + 1), :] = term

        @when(h != x)
        def _():
            light_send(h, x).start()

        @when(h == x)
        def _():
            lin[x] = lmsg[h]

    upper = (
        lax.broadcasted_iota(jnp.int32, (ROWS, ROWS), 0)
        <= lax.broadcasted_iota(jnp.int32, (ROWS, ROWS), 1)
    ).astype(F32)
    lrow[...] = jnp.dot(
        ld[...], upper, precision=lax.Precision.HIGHEST, preferred_element_type=F32
    )
    for fetch in fetches[3:]:
        fetch.wait()
    for part in parts:
        qs_t[:, part] = qs[part, :].T
        gs_t[:, part] = gs[part, :].T

    for j in range(1, NX):
        key_across(j, col(-j)).wait_recv()
        key_start(1, y, j, sigma, 4)
        key_start(2, y, j, -sigma, 3)
    row_scores(y, True)
    light_head(0)
    light_head(1)

    def key_take(place, row, j, turn, far, last):
        @when(wanted(row, turn, y, far))
        def _():
            key_ring(place, row, j, turn).wait_recv()

            @when(jnp.logical_not(last))
            def _():
                key_start(place + 2, row, j, turn, far)

    def value_pass(row):
        @when(row < y)
        def _():
            for dx in range(1, NX):
                value_across(row, dx, x).start()

    def value_take(row):
        @when(row <= y)
        def _():
            for dx in range(1, NX):
                value_across(row, dx, col(-dx)).wait_recv()
            for b in range(NX):
                rows = slice(b * ROWS, (b + 1) * ROWS)
                for cols in halves:
                    grads = mm(vg[row, b], gs_t[:, cols])
                    dp_ref[row, rows, cols] = grads
                    weighed = jnp.sum(grads * e_ref[row, rows, cols], axis=0, keepdims=True)
                    stat_t[pl.ds(row * NX + b, 1), cols] = weighed

    def rows_at(k):
        return ring(y - sigma * k), ring(y + sigma * k)

    def gather_turn(k, _):
        row_a, row_b = rows_at(k)
        past_a, past_b = rows_at(k - 1)
        key_take(2 * k - 1, row_a, NX, sigma, 4, k < 0)
        value_pass(row_a)
        key_take(2 * k, row_b, NX, -sigma, 3, k == 3)
        value_pass(row_b)

        def block_turn(j, _):
            key_take(2 * k - 1, row_a, j, sigma, 4, k < 0)
            key_take(2 * k, row_b, j, -sigma, 3, k == 3)
            return 0

        lax.fori_loop(0, NX, block_turn, 0)
        @when(row_a < y)
        def _():
            row_scores(row_a, False)

        @when(row_b < y)
        def _():
            row_scores(row_b, False)

        @when(k < 3)
        def _():
            light_head(k + 1)

        value_take(past_a)

        @when(k > 1)
        def _():
            value_take(past_b)

        return 0

    lax.fori_loop(1, NY // 2, gather_turn, 0)
    past_a, past_b = rows_at(NY // 2 - 1)
    row_far = ring(y - sigma * (NY // 2))
    key_take(NY - 1, row_far, NX, sigma, 4, row_far >= 0)
    value_pass(row_far)

    def far_turn(j, _):
        key_take(NY - 1, row_far, j, sigma, 4, j >= 0)
        return 0

    lax.fori_loop(0, NX, far_turn, 0)

    @when(row_far < y)
    def _():
        row_scores(row_far, False)

    for h in range(NX):
        @when(h != x)
        def _():
            push(lmsg.at[h], lin.at[h], l1_s.at[h], l1_r.at[h], at(y, h)).wait_recv()
    levels = [join_log(lin.at[b], 2 * DH) for b in range(NX)]
    row_state = lin[0, 0:DH, :].astype(F32)
    for b in range(1, NX):
        row_state = jnp.exp(levels[b]) * row_state + lin[b, 0:DH, :].astype(F32)
    row_grad = lin[NX - 1, DH : 2 * DH, :].astype(F32)
    for b in range(NX - 2, -1, -1):
        row_grad = jnp.exp(levels[b]) * row_grad + lin[b, DH : 2 * DH, :].astype(F32)
    row_level = jnp.broadcast_to(levels[0] + levels[1] + levels[2] + levels[3], (16, DH))
    ymsg[0, 0:DH, :] = row_state.astype(BF16)
    ymsg[1, 0:DH, :] = row_grad.astype(BF16)
    for n, term in enumerate(split_log(row_level)):
        ymsg[0, DH + 16 * n : DH + 16 * (n + 1), :] = term
        ymsg[1, DH + 16 * n : DH + 16 * (n + 1), :] = term

    def state_along(dy, owner):
        kind = jnp.where(y + dy < NY, 0, 1)
        return push(
            ymsg.at[kind], yin.at[owner], y_s.at[dy - 1], y_r.at[dy - 1], at(ring(y + dy), x)
        )

    for dy in range(1, NY):
        state_along(dy, y).start()

    value_take(past_a)
    value_take(past_b)
    value_take(row_far)

    top = jnp.max(stat_m[...], axis=0, keepdims=True)
    factor = jnp.exp2((stat_m[...] - top) * (SCALE * LOG2E))
    inverse = 1.0 / jnp.sum(factor * stat_l[...], axis=0, keepdims=True)
    dots = jnp.sum(factor * stat_t[...], axis=0, keepdims=True) * inverse
    dot_ref[...] = jnp.broadcast_to(dots, dot_ref.shape)
    stat_l[...] = factor * inverse

    def state_back(b, owner):
        return push(lout.at[b], fin.at[owner], l3_s.at[b], l3_r.at[owner], at(y, b))

    def state_turn():
        for dy in range(1, NY):
            state_along(dy, ring(y - dy)).wait_recv()
        for yy in range(NY):
            @when(yy < y)
            def _():
                cp[...] = (
                    jnp.exp(join_log(yin.at[yy], DH)) * cp[...] + yin[yy, 0:DH, :].astype(F32)
                )
        for yy in range(NY - 1, -1, -1):
            @when(yy > y)
            def _():
                cg[...] = (
                    jnp.exp(join_log(yin.at[yy], DH)) * cg[...] + yin[yy, 0:DH, :].astype(F32)
                )
        factors = [jnp.exp(join_log(lin.at[b], 2 * DH)) for b in range(NX)]
        carried = cp[...]
        for b in range(NX):
            lout[b, 0:DH, :] = carried.astype(BF16)
            carried = factors[b] * carried + lin[b, 0:DH, :].astype(F32)
        carried = cg[...]
        for b in range(NX - 1, -1, -1):
            lout[b, DH : 2 * DH, :] = carried.astype(BF16)
            carried = factors[b] * carried + lin[b, DH : 2 * DH, :].astype(F32)
        for b in range(NX):
            @when(b != x)
            def _():
                state_back(b, x).start()
        fin[x] = lout[x]

    def grad_ring(place, b, turn):
        return push(
            dkp.at[place, b], rbuf.at[place, b], dr_s.at[place, b], dr_r.at[place, b],
            at(ring(y + turn), x),
        )

    def grad_sent(row, turn, sender, far):
        return jnp.where(turn < 0, row < sender, row < far)

    def dv_across(row, dx):
        return push(
            dvp.at[row, col(dx)], vr.at[row, dx - 1], du_s.at[row, dx - 1], du_r.at[row, dx - 1],
            at(y, col(dx)),
        )

    def dv_ring(place, turn):
        return push(
            vsum.at[place], vfin.at[place], dw_s.at[place], dw_r.at[place], at(ring(y + turn), x)
        )

    def dv_sum(row):
        for dx in range(1, NX):
            dv_across(row, dx).wait_recv()
        return (
            dvp[row, x].astype(F32)
            + vr[row, 0].astype(F32)
            + vr[row, 1].astype(F32)
            + vr[row, 2].astype(F32)
        )

    def place_row(place):
        forth = (lax.rem(place, 2) == 1) | (place == 0)
        turn = jnp.where(forth, sigma, -sigma)
        far = jnp.where(forth, 4, 3)
        return turn, far, ring(y + turn * (4 - lax.div(place + 1, 2)))

    def earlier(place):
        return jnp.where(place == 1, 0, jnp.maximum(place - 2, 0))

    def dv_turn(place):
        turn, far, row = place_row(place)
        sends = grad_sent(row, turn, y, far)

        @when(row < y)
        def _():
            vacc[...] = dv_sum(row)

        @when(row > y)
        def _():
            vacc[...] = jnp.zeros_like(vacc)

        @when((place != 0) & (place != 2) & grad_sent(row, turn, ring(y - turn), far))
        def _():
            dv_ring(earlier(place), turn).wait_recv()
            vacc[...] += vfin[earlier(place)].astype(F32)

        @when(sends)
        def _():
            vsum[place] = vacc[...].astype(BF16)
            dv_ring(place, turn).start()

    def back_turn(place, _):
        turn, far, row = place_row(place)

        @when(row <= y)
        def _():
            for b in range(NX):
                rows = slice(b * ROWS, (b + 1) * ROWS)
                for cols in halves:
                    weights = e_ref[row, rows, cols] * stat_l[pl.ds(row * NX + b, 1), cols]
                    grads = weights * (dp_ref[row, rows, cols] - dot_ref[0:1, cols])
                    wb_ref[row, rows, cols] = weights.astype(BF16)
                    ds_ref[row, rows, cols] = grads.astype(BF16)
                dkf[b] = mm(ds_ref[row, rows, :], qs[...]) * SCALE
                dvp[row, b] = mm(wb_ref[row, rows, :], gs[...]).astype(BF16)
            for dx in range(1, NX):
                dv_across(row, dx).start()

        @when(row > y)
        def _():
            dkf[...] = jnp.zeros_like(dkf)

        before = earlier(place)
        takes = (place != 0) & (place != 2) & (place != NY - 1)
        takes = takes & grad_sent(row, turn, ring(y - turn), far)
        sends = (place < NY - 1) & grad_sent(row, turn, y, far)

        def ring_block(b, _):
            @when(takes)
            def _():
                grad_ring(before, b, turn).wait_recv()
                dkf[b] += rbuf[before, b].astype(F32)

            @when(sends)
            def _():
                dkp[place, b] = dkf[b].astype(BF16)
                grad_ring(place, b, turn).start()

            return 0

        lax.fori_loop(0, NX, ring_block, 0)

        @when(place >= 1)
        def _():
            dv_turn(place - 1)

        @when(place == 2)
        def _():
            state_turn()

        return 0

    lax.fori_loop(0, NY, back_turn, 0)

    for b in range(NX):
        @when(b != x)
        def _():
            push(lout.at[b], fin.at[b], l3_s.at[b], l3_r.at[b], at(y, b)).wait_recv()

    def light_out(h, _):
        cols = pl.ds(pl.multiple_of(h * DH, DH), DH)
        qh, kh, vh, gh = q_l[:, cols], k_l[:, cols], v_l[:, cols], g_l[:, cols]
        level = lall[:, cols]
        entering = jnp.exp(level) * SCALE
        fading = jnp.exp(level[ROWS - 1 : ROWS, :] - level) * SCALE
        prior = fin[h, 0:DH, :]
        later = fin[h, DH : 2 * DH, :]
        o_l[:, cols] = (intra[0, :, cols] + entering * mm(qh, prior)).astype(BF16)
        dq_l[:, cols] = (intra[1, :, cols] + entering * mm_nt(gh, prior)).astype(BF16)
        dk_l[:, cols] = (intra[2, :, cols] + fading * mm_nt(vh, later)).astype(BF16)
        dv_l[:, cols] = (intra[3, :, cols] + fading * mm(kh, later)).astype(BF16)
        return 0

    lax.fori_loop(0, HEADS, light_out, 0)
    moves = [(o_l, o_hbm), (dq_l, dq_hbm), (dk_l, dk_hbm), (dv_l, dv_hbm)]
    moves += [(o_s, os_hbm), (dq_s, dqs_hbm), (dk_s, dks_hbm), (dv_s, dvs_hbm)]
    stores = [
        pltpu.make_async_copy(src, dst, out_s.at[n]) for n, (src, dst) in enumerate(moves)
    ]
    for store in stores[:4]:
        store.start()

    for dx in range(1, NX):
        key_across(dx, x).wait_send()

    def sent_turn(place, _):
        odd = lax.rem(place, 2) == 1
        turn = jnp.where(odd, sigma, -sigma)
        row = ring(y - turn * (lax.div(place + 1, 2) - 1))

        @when(wanted(row, turn, ring(y + turn), jnp.where(odd, 4, 3)))
        def _():
            for j in range(NX + 1):
                key_ring(place, row, j, turn).wait_send()

        turn_back, far_back, row_back = place_row(place - 1)

        @when(grad_sent(row_back, turn_back, y, far_back))
        def _():
            for j in range(NX):
                grad_ring(place - 1, j, turn_back).wait_send()
            dv_ring(place - 1, turn_back).wait_send()

        return 0

    lax.fori_loop(1, NY, sent_turn, 0)
    for dy in range(1, NY):
        state_along(dy, y).wait_send()
    for b in range(NX):
        @when(b != x)
        def _():
            light_send(b, x).wait_send()
            state_back(b, x).wait_send()
    for row in range(NY):
        @when(row <= y)
        def _():
            for dx in range(1, NX):
                value_across(row, dx, x).wait_send()
                dv_across(row, dx).wait_send()

    def dk_across(dx):
        return push(
            dks.at[col(dx)], kfin.at[dx - 1], kf_s.at[dx - 1], kf_r.at[dx - 1], at(y, col(dx))
        )

    for j in (1, 2, 3, 0):
        b = col(j)
        for place, turn, far in ((NY - 3, sigma, 4), (NY - 2, -sigma, 3)):
            @when(grad_sent(y, turn, ring(y - turn), far))
            def _():
                grad_ring(place, b, turn).wait_recv()
                dkf[b] += rbuf[place, b].astype(F32)
        if j:
            dks[b] = dkf[b].astype(BF16)
            dk_across(j).start()

    def query_turn(row, _):
        out_t[...] += mm_tn(vg[row].reshape(SPAN, DH), wb_ref[row])
        dq_t[...] += mm_tn(kg[row].reshape(SPAN, DH), ds_ref[row])
        return 0

    lax.fori_loop(0, y + 1, query_turn, 0)
    for part in parts:
        o_s[:, part] = out_t[:, part].T.astype(BF16)
        dq_s[:, part] = (dq_t[:, part].T * SCALE).astype(BF16)
    stores[4].start()
    stores[5].start()

    vacc[...] = dv_sum(y)
    for place, turn, far in ((NY - 3, sigma, 4), (NY - 2, -sigma, 3)):
        @when(grad_sent(y, turn, ring(y - turn), far))
        def _():
            dv_ring(place, turn).wait_recv()
            vacc[...] += vfin[place].astype(F32)
    dv_s[...] = vacc[...].astype(BF16)
    stores[7].start()

    for dx in range(1, NX):
        dk_across(dx).wait_recv()
    dk_s[...] = (
        dkf[x] + kfin[0].astype(F32) + kfin[1].astype(F32) + kfin[2].astype(F32)
    ).astype(BF16)
    stores[6].start()

    for dx in range(1, NX):
        dk_across(dx).wait_send()
    for store in stores:
        store.wait()


def copy_out(*refs):
    ins, outs, held, sems = refs[:8], refs[8:16], refs[16:24], refs[24]
    reads = [pltpu.make_async_copy(a, b, sems.at[0, n]) for n, (a, b) in enumerate(zip(ins, held))]
    writes = [
        pltpu.make_async_copy(a, b, sems.at[1, n]) for n, (a, b) in enumerate(zip(held, outs))
    ]
    for read in reads:
        read.start()
    for read, write in zip(reads, writes):
        read.wait()
        write.start()
    for write in writes:
        write.wait()


def shards(q_light, k_light, v_light, g_light, log_decay, q_soft, k_soft, v_soft, g_soft):
    dma = pltpu.SemaphoreType.DMA
    wide = jax.ShapeDtypeStruct((ROWS, WIDE), BF16)
    narrow = jax.ShapeDtypeStruct((ROWS, DH), BF16)
    scratch = [pltpu.VMEM((ROWS, WIDE), BF16)] * 6 + [pltpu.VMEM((ROWS, DH), BF16)] * 2
    scratch += [
        pltpu.VMEM((ROWS, WIDE), BF16),
        pltpu.VMEM((ROWS, WIDE), BF16),
        pltpu.VMEM((ROWS, WIDE), BF16),
        pltpu.VMEM((ROWS, WIDE), BF16),
        pltpu.VMEM((HEADS, ROWS), F32),
        pltpu.VMEM((WIDE, DH), BF16),
        pltpu.VMEM((WIDE, DH), BF16),
        pltpu.VMEM((DH, WIDE), BF16),
        pltpu.VMEM((DH, WIDE), BF16),
        pltpu.VMEM((NY, NX, ROWS, DH), BF16),
        pltpu.VMEM((NY, NX, ROWS, DH), BF16),
        pltpu.VMEM((NY, SPAN, WIDE), F32),
        pltpu.VMEM((NY, SPAN, WIDE), F32),
        pltpu.VMEM((NY * NX, WIDE), F32),
        pltpu.VMEM((NY * NX, WIDE), F32),
        pltpu.VMEM((NY * NX, WIDE), F32),
        pltpu.VMEM((8, WIDE), F32),
        pltpu.VMEM((NY, SPAN, WIDE), BF16),
        pltpu.VMEM((NY, SPAN, WIDE), BF16),
        pltpu.VMEM((DH, WIDE), F32),
        pltpu.VMEM((DH, WIDE), F32),
        pltpu.VMEM((NX, ROWS, DH), F32),
        pltpu.VMEM((NY - 1, NX, ROWS, DH), BF16),
        pltpu.VMEM((NY - 1, NX, ROWS, DH), BF16),
        pltpu.VMEM((NY, NX, ROWS, DH), BF16),
        pltpu.VMEM((NY, NX - 1, ROWS, DH), BF16),
        pltpu.VMEM((NY - 1, ROWS, DH), BF16),
        pltpu.VMEM((NY - 1, ROWS, DH), BF16),
        pltpu.VMEM((ROWS, DH), F32),
        pltpu.VMEM((NX - 1, ROWS, DH), BF16),
        pltpu.VMEM((NX, ROWS, DH), BF16),
        pltpu.VMEM((HEADS, ROWS), F32),
        pltpu.VMEM((ROWS, WIDE), F32),
        pltpu.VMEM((4, ROWS, WIDE), F32),
        pltpu.VMEM((HEADS, 2 * DH + 48, DH), BF16),
        pltpu.VMEM((NX, 2 * DH + 48, DH), BF16),
        pltpu.VMEM((2, DH + 48, DH), BF16),
        pltpu.VMEM((NY, DH + 48, DH), BF16),
        pltpu.VMEM((DH, DH), F32),
        pltpu.VMEM((DH, DH), F32),
        pltpu.VMEM((NX, 2 * DH, DH), BF16),
        pltpu.VMEM((HEADS, 2 * DH, DH), BF16),
        dma((15,)),
        dma((8,)),
        dma((NX - 1,)), dma((NX - 1,)),
        dma((NY - 1, NX + 1)), dma((NY - 1, NX + 1)),
        dma((NY, NX - 1)), dma((NY, NX - 1)),
        dma((NX,)), dma((NX,)),
        dma((NY - 1,)), dma((NY - 1,)),
        dma((NX,)), dma((NX,)),
        dma((NY - 1, NX)), dma((NY - 1, NX)),
        dma((NY, NX - 1)), dma((NY, NX - 1)),
        dma((NY - 1,)), dma((NY - 1,)),
        dma((NX - 1,)), dma((NX - 1,)),
    ]
    hbm = pl.BlockSpec(memory_space=pltpu.HBM)
    room = 62 * 1024 * 1024
    shapes = (wide, wide, wide, wide, wide, wide, narrow, narrow)
    results = pl.pallas_call(
        kernel,
        out_shape=shapes,
        in_specs=[hbm] * 9,
        out_specs=(hbm,) * 8,
        scratch_shapes=scratch,
        compiler_params=pltpu.CompilerParams(
            collective_id=0, has_side_effects=True, vmem_limit_bytes=room
        ),
    )(q_light, k_light, v_light, g_light, log_decay.T, q_soft, k_soft, v_soft, g_soft)
    return pl.pallas_call(
        copy_out,
        out_shape=shapes,
        in_specs=[hbm] * 8,
        out_specs=(hbm,) * 8,
        scratch_shapes=[pltpu.VMEM(shape.shape, BF16) for shape in shapes] + [dma((2, 8))],
        compiler_params=pltpu.CompilerParams(vmem_limit_bytes=room),
    )(*results)


def solution(mesh):
    spec = P(("dp", "ctx"), "tp")
    return jax.shard_map(
        shards, mesh=mesh, in_specs=(spec,) * 9, out_specs=(spec,) * 8, check_vma=False
    )
```

```python
import jax
import jax.numpy as jnp
from jax import lax
from jax.experimental import pallas as pl
from jax.experimental.pallas import tpu as pltpu
from jax.sharding import PartitionSpec as P

DH = 128
ROWS = 128
NX = 4
NY = 8
HEADS = 4
WIDE = HEADS * DH
SPAN = NX * ROWS
SCALE = DH**-0.5
LOG2E = 1.4426950408889634
MASKED = -1e30
F32 = jnp.float32
BF16 = jnp.bfloat16


def mm(a, b):
    return jnp.dot(a, b, preferred_element_type=F32)


def mm_nt(a, b):
    return lax.dot_general(a, b, (((1,), (1,)), ((), ())), preferred_element_type=F32)


def mm_tn(a, b):
    return lax.dot_general(a, b, (((0,), (0,)), ((), ())), preferred_element_type=F32)


def push(src, dst, send, recv, target):
    return pltpu.make_async_remote_copy(
        src_ref=src,
        dst_ref=dst,
        send_sem=send,
        recv_sem=recv,
        device_id={"ctx": target},
        device_id_type=pl.DeviceIdType.MESH,
    )


def split_log(total):
    high = total.astype(BF16)
    rest = total - high.astype(F32)
    middle = rest.astype(BF16)
    low = (rest - middle.astype(F32)).astype(BF16)
    return high, middle, low


def join_log(ref, first):
    return (
        ref[first : first + 16, :].astype(F32)
        + ref[first + 16 : first + 32, :].astype(F32)
        + ref[first + 32 : first + 48, :].astype(F32)
    )[0:1, :]


def kernel(
    q_hbm, k_hbm, v_hbm, g_hbm, ld_hbm, qs_hbm, ks_hbm, vs_hbm, gs_hbm,
    o_hbm, dq_hbm, dk_hbm, dv_hbm, os_hbm, dqs_hbm, dks_hbm, dvs_hbm,
    o_l, dq_l, dk_l, dv_l, o_s, dq_s, dk_s, dv_s,
    q_l, k_l, v_l, g_l, ld, qs, gs, qs_t, gs_t,
    kg, vg, e_ref, dp_ref, stat_m, stat_l, stat_t, dot_ref, wb_ref, ds_ref,
    out_t, dq_t, dkf, dkp, rbuf, dvp, vr, vsum, vfin, vacc, kfin, dks,
    lrow, lall, intra, lmsg, lin, ymsg, yin, cp, cg, lout, fin,
    in_s, out_s, kx_s, kx_r, kr_s, kr_r, vx_s, vx_r,
    l1_s, l1_r, y_s, y_r, l3_s, l3_r,
    dr_s, dr_r, du_s, du_r, dw_s, dw_r, kf_s, kf_r,
):
    me = lax.axis_index("ctx")
    y = lax.div(me, NX)
    x = lax.rem(me, NX)
    sigma = 1 - 2 * lax.rem(lax.axis_index("tp"), 2)

    def ring(value):
        return lax.rem(value + 2 * NY, NY)

    def at(yy, xx):
        return yy * NX + xx

    def col(step):
        return lax.rem(x + step + NX, NX)

    def when(condition):
        return pl.when(condition)

    barrier = pltpu.get_barrier_semaphore()
    for dx in range(1, NX):
        pl.semaphore_signal(
            barrier, inc=1, device_id={"ctx": at(y, col(dx))},
            device_id_type=pl.DeviceIdType.MESH,
        )
    for dy in range(1, NY):
        pl.semaphore_signal(
            barrier, inc=1, device_id={"ctx": at(ring(y + dy), x)},
            device_id_type=pl.DeviceIdType.MESH,
        )

    parts = [slice(h * DH, (h + 1) * DH) for h in range(HEADS)]
    moves = [(ks_hbm, kg.at[y, x]), (vs_hbm, vg.at[y, x]), (ld_hbm, ld)]
    moves += [(qs_hbm.at[:, part], qs.at[part, :]) for part in parts]
    moves += [(gs_hbm.at[:, part], gs.at[part, :]) for part in parts]
    moves += [(q_hbm, q_l), (k_hbm, k_l), (v_hbm, v_l), (g_hbm, g_l)]
    fetches = [
        pltpu.make_async_copy(src, dst, in_s.at[n]) for n, (src, dst) in enumerate(moves)
    ]
    for fetch in fetches:
        fetch.start()

    halves = [slice(0, WIDE // 2), slice(WIDE // 2, WIDE)]
    stat_m[...] = jnp.full(stat_m.shape, MASKED, F32)
    stat_l[...] = jnp.zeros_like(stat_l)
    stat_t[...] = jnp.zeros_like(stat_t)
    out_t[...] = jnp.zeros_like(out_t)
    dq_t[...] = jnp.zeros_like(dq_t)
    cp[...] = jnp.zeros_like(cp)
    cg[...] = jnp.zeros_like(cg)
    for fetch in fetches[:3]:
        fetch.wait()
    pl.semaphore_wait(barrier, NX + NY - 2)

    def key_across(dx, owner):
        return push(
            kg.at[y, owner], kg.at[y, owner], kx_s.at[dx - 1], kx_r.at[dx - 1], at(y, col(dx))
        )

    def value_across(row, dx, owner):
        return push(
            vg.at[row, owner], vg.at[row, owner], vx_s.at[row, dx - 1], vx_r.at[row, dx - 1],
            at(y, col(dx)),
        )

    def key_ring(place, row, j, turn):
        values = isinstance(j, int) and j == NX
        block = vg.at[row, x] if values else kg.at[row, col(-j)]
        return push(
            block, block, kr_s.at[place - 1, j], kr_r.at[place - 1, j], at(ring(y + turn), x)
        )

    def wanted(row, turn, target, far):
        return jnp.where(turn > 0, row < target, row < far)

    def key_start(place, row, j, turn, far):
        @when(wanted(row, turn, ring(y + turn), far))
        def _():
            key_ring(place, row, j, turn).start()

    for dx in range(1, NX):
        key_across(dx, x).start()
    for j in (NX, 0):
        key_start(1, y, j, sigma, 4)
        key_start(2, y, j, -sigma, 3)
    for dx in range(1, NX):
        value_across(y, dx, x).start()

    def row_scores(row, masked):
        for b in range(NX):
            rows = slice(b * ROWS, (b + 1) * ROWS)
            for cols in halves:
                scores = mm(kg[row, b], qs_t[:, cols])
                if masked:
                    key_at = lax.broadcasted_iota(jnp.int32, scores.shape, 0) + b * ROWS
                    query_at = lax.rem(lax.broadcasted_iota(jnp.int32, scores.shape, 1), ROWS)
                    scores = jnp.where(key_at <= query_at + x * ROWS, scores, MASKED)
                top = jnp.max(scores, axis=0, keepdims=True)
                grown = jnp.exp2(scores * (SCALE * LOG2E) - top * (SCALE * LOG2E))
                e_ref[row, rows, cols] = grown
                stat_m[pl.ds(row * NX + b, 1), cols] = top
                stat_l[pl.ds(row * NX + b, 1), cols] = jnp.sum(grown, axis=0, keepdims=True)

    def light_send(h, owner):
        return push(lmsg.at[h], lin.at[owner], l1_s.at[h], l1_r.at[owner], at(y, h))

    def light_head(h):
        cols = pl.ds(pl.multiple_of(h * DH, DH), DH)
        qh, kh, vh, gh = q_l[:, cols], k_l[:, cols], v_l[:, cols], g_l[:, cols]
        flat = jnp.broadcast_to(lrow[pl.ds(h, 1), :], (ROWS, ROWS))
        level = flat.T
        lall[:, cols] = level
        row_at = lax.broadcasted_iota(jnp.int32, (ROWS, ROWS), 0)
        causal = row_at >= lax.broadcasted_iota(jnp.int32, (ROWS, ROWS), 1)
        gaps = jnp.where(causal, level - flat, 0.0)
        weights = jnp.where(causal, jnp.exp(gaps), 0.0) * SCALE
        mixing = (mm_nt(qh, kh) * weights).astype(BF16)
        back_mix = (mm_nt(gh, vh) * weights).astype(BF16)
        intra[0, :, cols] = mm(mixing, vh)
        intra[1, :, cols] = mm(back_mix, kh)
        intra[2, :, cols] = mm_tn(back_mix, qh)
        intra[3, :, cols] = mm_tn(mixing, gh)
        last = level[ROWS - 1 : ROWS, :]
        fading = (kh.astype(F32) * jnp.exp(last - level)).astype(BF16)
        entering = (qh.astype(F32) * jnp.exp(level)).astype(BF16)
        lmsg[h, 0:DH, :] = mm_tn(fading, vh).astype(BF16)
        lmsg[h, DH : 2 * DH, :] = mm_tn(entering, gh).astype(BF16)
        for n, term in enumerate(split_log(jnp.broadcast_to(last, (16, DH)))):
            lmsg[h, 2 * DH + 16 * n : 2 * DH + 16 * (n + 1), :] = term

        @when(h != x)
        def _():
            light_send(h, x).start()

        @when(h == x)
        def _():
            lin[x] = lmsg[h]

    upper = (
        lax.broadcasted_iota(jnp.int32, (ROWS, ROWS), 0)
        <= lax.broadcasted_iota(jnp.int32, (ROWS, ROWS), 1)
    ).astype(F32)
    lrow[...] = jnp.dot(
        ld[...], upper, precision=lax.Precision.HIGHEST, preferred_element_type=F32
    )
    for fetch in fetches[3:]:
        fetch.wait()
    for part in parts:
        qs_t[:, part] = qs[part, :].T
        gs_t[:, part] = gs[part, :].T

    for j in range(1, NX):
        key_across(j, col(-j)).wait_recv()
        key_start(1, y, j, sigma, 4)
        key_start(2, y, j, -sigma, 3)
    row_scores(y, True)
    light_head(0)
    light_head(1)

    def key_take(place, row, j, turn, far, last):
        @when(wanted(row, turn, y, far))
        def _():
            key_ring(place, row, j, turn).wait_recv()

            @when(jnp.logical_not(last))
            def _():
                key_start(place + 2, row, j, turn, far)

    def value_pass(row):
        @when(row < y)
        def _():
            for dx in range(1, NX):
                value_across(row, dx, x).start()

    def value_take(row):
        @when(row <= y)
        def _():
            for dx in range(1, NX):
                value_across(row, dx, col(-dx)).wait_recv()
            for b in range(NX):
                rows = slice(b * ROWS, (b + 1) * ROWS)
                for cols in halves:
                    grads = mm(vg[row, b], gs_t[:, cols])
                    dp_ref[row, rows, cols] = grads
                    weighed = jnp.sum(grads * e_ref[row, rows, cols], axis=0, keepdims=True)
                    stat_t[pl.ds(row * NX + b, 1), cols] = weighed

    def rows_at(k):
        return ring(y - sigma * k), ring(y + sigma * k)

    def gather_turn(k, _):
        row_a, row_b = rows_at(k)
        past_a, past_b = rows_at(k - 1)
        key_take(2 * k - 1, row_a, NX, sigma, 4, k < 0)
        value_pass(row_a)
        key_take(2 * k, row_b, NX, -sigma, 3, k == 3)
        value_pass(row_b)

        def block_turn(j, _):
            key_take(2 * k - 1, row_a, j, sigma, 4, k < 0)
            key_take(2 * k, row_b, j, -sigma, 3, k == 3)
            return 0

        lax.fori_loop(0, NX, block_turn, 0)
        @when(row_a < y)
        def _():
            row_scores(row_a, False)

        @when(row_b < y)
        def _():
            row_scores(row_b, False)

        @when(k < 3)
        def _():
            light_head(k + 1)

        value_take(past_a)

        @when(k > 1)
        def _():
            value_take(past_b)

        return 0

    lax.fori_loop(1, NY // 2, gather_turn, 0)
    past_a, past_b = rows_at(NY // 2 - 1)
    row_far = ring(y - sigma * (NY // 2))
    key_take(NY - 1, row_far, NX, sigma, 4, row_far >= 0)
    value_pass(row_far)

    def far_turn(j, _):
        key_take(NY - 1, row_far, j, sigma, 4, j >= 0)
        return 0

    lax.fori_loop(0, NX, far_turn, 0)

    @when(row_far < y)
    def _():
        row_scores(row_far, False)

    for h in range(NX):
        @when(h != x)
        def _():
            push(lmsg.at[h], lin.at[h], l1_s.at[h], l1_r.at[h], at(y, h)).wait_recv()
    levels = [join_log(lin.at[b], 2 * DH) for b in range(NX)]
    row_state = lin[0, 0:DH, :].astype(F32)
    for b in range(1, NX):
        row_state = jnp.exp(levels[b]) * row_state + lin[b, 0:DH, :].astype(F32)
    row_grad = lin[NX - 1, DH : 2 * DH, :].astype(F32)
    for b in range(NX - 2, -1, -1):
        row_grad = jnp.exp(levels[b]) * row_grad + lin[b, DH : 2 * DH, :].astype(F32)
    row_level = jnp.broadcast_to(levels[0] + levels[1] + levels[2] + levels[3], (16, DH))
    ymsg[0, 0:DH, :] = row_state.astype(BF16)
    ymsg[1, 0:DH, :] = row_grad.astype(BF16)
    for n, term in enumerate(split_log(row_level)):
        ymsg[0, DH + 16 * n : DH + 16 * (n + 1), :] = term
        ymsg[1, DH + 16 * n : DH + 16 * (n + 1), :] = term

    def state_along(dy, owner):
        kind = jnp.where(y + dy < NY, 0, 1)
        return push(
            ymsg.at[kind], yin.at[owner], y_s.at[dy - 1], y_r.at[dy - 1], at(ring(y + dy), x)
        )

    for dy in range(1, NY):
        state_along(dy, y).start()

    value_take(past_a)
    value_take(past_b)
    value_take(row_far)

    top = jnp.max(stat_m[...], axis=0, keepdims=True)
    factor = jnp.exp2((stat_m[...] - top) * (SCALE * LOG2E))
    inverse = 1.0 / jnp.sum(factor * stat_l[...], axis=0, keepdims=True)
    dots = jnp.sum(factor * stat_t[...], axis=0, keepdims=True) * inverse
    dot_ref[...] = jnp.broadcast_to(dots, dot_ref.shape)
    stat_l[...] = factor * inverse

    def state_back(b, owner):
        return push(lout.at[b], fin.at[owner], l3_s.at[b], l3_r.at[owner], at(y, b))

    def state_turn():
        for dy in range(1, NY):
            state_along(dy, ring(y - dy)).wait_recv()
        for yy in range(NY):
            @when(yy < y)
            def _():
                cp[...] = (
                    jnp.exp(join_log(yin.at[yy], DH)) * cp[...] + yin[yy, 0:DH, :].astype(F32)
                )
        for yy in range(NY - 1, -1, -1):
            @when(yy > y)
            def _():
                cg[...] = (
                    jnp.exp(join_log(yin.at[yy], DH)) * cg[...] + yin[yy, 0:DH, :].astype(F32)
                )
        factors = [jnp.exp(join_log(lin.at[b], 2 * DH)) for b in range(NX)]
        carried = cp[...]
        for b in range(NX):
            lout[b, 0:DH, :] = carried.astype(BF16)
            carried = factors[b] * carried + lin[b, 0:DH, :].astype(F32)
        carried = cg[...]
        for b in range(NX - 1, -1, -1):
            lout[b, DH : 2 * DH, :] = carried.astype(BF16)
            carried = factors[b] * carried + lin[b, DH : 2 * DH, :].astype(F32)
        for b in range(NX):
            @when(b != x)
            def _():
                state_back(b, x).start()
        fin[x] = lout[x]

    def grad_ring(place, b, turn):
        return push(
            dkp.at[place, b], rbuf.at[place, b], dr_s.at[place, b], dr_r.at[place, b],
            at(ring(y + turn), x),
        )

    def grad_sent(row, turn, sender, far):
        return jnp.where(turn < 0, row < sender, row < far)

    def dv_across(row, dx):
        return push(
            dvp.at[row, col(dx)], vr.at[row, dx - 1], du_s.at[row, dx - 1], du_r.at[row, dx - 1],
            at(y, col(dx)),
        )

    def dv_ring(place, turn):
        return push(
            vsum.at[place], vfin.at[place], dw_s.at[place], dw_r.at[place], at(ring(y + turn), x)
        )

    def dv_sum(row):
        for dx in range(1, NX):
            dv_across(row, dx).wait_recv()
        return (
            dvp[row, x].astype(F32)
            + vr[row, 0].astype(F32)
            + vr[row, 1].astype(F32)
            + vr[row, 2].astype(F32)
        )

    def place_row(place):
        forth = (lax.rem(place, 2) == 1) | (place == 0)
        turn = jnp.where(forth, sigma, -sigma)
        far = jnp.where(forth, 4, 3)
        return turn, far, ring(y + turn * (4 - lax.div(place + 1, 2)))

    def earlier(place):
        return jnp.where(place == 1, 0, jnp.maximum(place - 2, 0))

    def dv_turn(place):
        turn, far, row = place_row(place)
        sends = grad_sent(row, turn, y, far)

        @when(row < y)
        def _():
            vacc[...] = dv_sum(row)

        @when(row > y)
        def _():
            vacc[...] = jnp.zeros_like(vacc)

        @when((place != 0) & (place != 2) & grad_sent(row, turn, ring(y - turn), far))
        def _():
            dv_ring(earlier(place), turn).wait_recv()
            vacc[...] += vfin[earlier(place)].astype(F32)

        @when(sends)
        def _():
            vsum[place] = vacc[...].astype(BF16)
            dv_ring(place, turn).start()

    def back_turn(place, _):
        turn, far, row = place_row(place)

        @when(row <= y)
        def _():
            for b in range(NX):
                rows = slice(b * ROWS, (b + 1) * ROWS)
                for cols in halves:
                    weights = e_ref[row, rows, cols] * stat_l[pl.ds(row * NX + b, 1), cols]
                    grads = weights * (dp_ref[row, rows, cols] - dot_ref[0:1, cols])
                    wb_ref[row, rows, cols] = weights.astype(BF16)
                    ds_ref[row, rows, cols] = grads.astype(BF16)
                dkf[b] = mm(ds_ref[row, rows, :], qs[...]) * SCALE
                dvp[row, b] = mm(wb_ref[row, rows, :], gs[...]).astype(BF16)
            for dx in range(1, NX):
                dv_across(row, dx).start()

        @when(row > y)
        def _():
            dkf[...] = jnp.zeros_like(dkf)

        before = earlier(place)
        takes = (place != 0) & (place != 2) & (place != NY - 1)
        takes = takes & grad_sent(row, turn, ring(y - turn), far)
        sends = (place < NY - 1) & grad_sent(row, turn, y, far)

        def ring_block(b, _):
            @when(takes)
            def _():
                grad_ring(before, b, turn).wait_recv()
                dkf[b] += rbuf[before, b].astype(F32)

            @when(sends)
            def _():
                dkp[place, b] = dkf[b].astype(BF16)
                grad_ring(place, b, turn).start()

            return 0

        lax.fori_loop(0, NX, ring_block, 0)

        @when(place >= 2)
        def _():
            dv_turn(place - 2)

        @when(place == 2)
        def _():
            state_turn()

        return 0

    lax.fori_loop(0, NY, back_turn, 0)
    dv_turn(NY - 2)

    for b in range(NX):
        @when(b != x)
        def _():
            push(lout.at[b], fin.at[b], l3_s.at[b], l3_r.at[b], at(y, b)).wait_recv()

    def light_out(h, _):
        cols = pl.ds(pl.multiple_of(h * DH, DH), DH)
        qh, kh, vh, gh = q_l[:, cols], k_l[:, cols], v_l[:, cols], g_l[:, cols]
        level = lall[:, cols]
        entering = jnp.exp(level) * SCALE
        fading = jnp.exp(level[ROWS - 1 : ROWS, :] - level) * SCALE
        prior = fin[h, 0:DH, :]
        later = fin[h, DH : 2 * DH, :]
        o_l[:, cols] = (intra[0, :, cols] + entering * mm(qh, prior)).astype(BF16)
        dq_l[:, cols] = (intra[1, :, cols] + entering * mm_nt(gh, prior)).astype(BF16)
        dk_l[:, cols] = (intra[2, :, cols] + fading * mm_nt(vh, later)).astype(BF16)
        dv_l[:, cols] = (intra[3, :, cols] + fading * mm(kh, later)).astype(BF16)
        return 0

    lax.fori_loop(0, HEADS, light_out, 0)
    moves = [(o_l, o_hbm), (dq_l, dq_hbm), (dk_l, dk_hbm), (dv_l, dv_hbm)]
    moves += [(o_s, os_hbm), (dq_s, dqs_hbm), (dk_s, dks_hbm), (dv_s, dvs_hbm)]
    stores = [
        pltpu.make_async_copy(src, dst, out_s.at[n]) for n, (src, dst) in enumerate(moves)
    ]
    for store in stores[:4]:
        store.start()

    for dx in range(1, NX):
        key_across(dx, x).wait_send()

    def sent_turn(place, _):
        odd = lax.rem(place, 2) == 1
        turn = jnp.where(odd, sigma, -sigma)
        row = ring(y - turn * (lax.div(place + 1, 2) - 1))

        @when(wanted(row, turn, ring(y + turn), jnp.where(odd, 4, 3)))
        def _():
            for j in range(NX + 1):
                key_ring(place, row, j, turn).wait_send()

        turn_back, far_back, row_back = place_row(place - 1)

        @when(grad_sent(row_back, turn_back, y, far_back))
        def _():
            for j in range(NX):
                grad_ring(place - 1, j, turn_back).wait_send()
            dv_ring(place - 1, turn_back).wait_send()

        return 0

    lax.fori_loop(1, NY, sent_turn, 0)
    for dy in range(1, NY):
        state_along(dy, y).wait_send()
    for b in range(NX):
        @when(b != x)
        def _():
            light_send(b, x).wait_send()
            state_back(b, x).wait_send()
    for row in range(NY):
        @when(row <= y)
        def _():
            for dx in range(1, NX):
                value_across(row, dx, x).wait_send()
                dv_across(row, dx).wait_send()

    def dk_across(dx):
        return push(
            dks.at[col(dx)], kfin.at[dx - 1], kf_s.at[dx - 1], kf_r.at[dx - 1], at(y, col(dx))
        )

    for j in (1, 2, 3, 0):
        b = col(j)
        for place, turn, far in ((NY - 3, sigma, 4), (NY - 2, -sigma, 3)):
            @when(grad_sent(y, turn, ring(y - turn), far))
            def _():
                grad_ring(place, b, turn).wait_recv()
                dkf[b] += rbuf[place, b].astype(F32)
        if j:
            dks[b] = dkf[b].astype(BF16)
            dk_across(j).start()

    def query_turn(row, _):
        out_t[...] += mm_tn(vg[row].reshape(SPAN, DH), wb_ref[row])
        dq_t[...] += mm_tn(kg[row].reshape(SPAN, DH), ds_ref[row])
        return 0

    lax.fori_loop(0, y + 1, query_turn, 0)
    for part in parts:
        o_s[:, part] = out_t[:, part].T.astype(BF16)
        dq_s[:, part] = (dq_t[:, part].T * SCALE).astype(BF16)
    stores[4].start()
    stores[5].start()

    vacc[...] = dv_sum(y)
    for place, turn, far in ((NY - 3, sigma, 4), (NY - 2, -sigma, 3)):
        @when(grad_sent(y, turn, ring(y - turn), far))
        def _():
            dv_ring(place, turn).wait_recv()
            vacc[...] += vfin[place].astype(F32)
    dv_s[...] = vacc[...].astype(BF16)
    stores[7].start()

    for dx in range(1, NX):
        dk_across(dx).wait_recv()
    dk_s[...] = (
        dkf[x] + kfin[0].astype(F32) + kfin[1].astype(F32) + kfin[2].astype(F32)
    ).astype(BF16)
    stores[6].start()

    for dx in range(1, NX):
        dk_across(dx).wait_send()
    for store in stores:
        store.wait()


def copy_out(*refs):
    ins, outs, held, sems = refs[:8], refs[8:16], refs[16:24], refs[24]
    reads = [pltpu.make_async_copy(a, b, sems.at[0, n]) for n, (a, b) in enumerate(zip(ins, held))]
    writes = [
        pltpu.make_async_copy(a, b, sems.at[1, n]) for n, (a, b) in enumerate(zip(held, outs))
    ]
    for read in reads:
        read.start()
    for read, write in zip(reads, writes):
        read.wait()
        write.start()
    for write in writes:
        write.wait()


def shards(q_light, k_light, v_light, g_light, log_decay, q_soft, k_soft, v_soft, g_soft):
    dma = pltpu.SemaphoreType.DMA
    wide = jax.ShapeDtypeStruct((ROWS, WIDE), BF16)
    narrow = jax.ShapeDtypeStruct((ROWS, DH), BF16)
    scratch = [pltpu.VMEM((ROWS, WIDE), BF16)] * 6 + [pltpu.VMEM((ROWS, DH), BF16)] * 2
    scratch += [
        pltpu.VMEM((ROWS, WIDE), BF16),
        pltpu.VMEM((ROWS, WIDE), BF16),
        pltpu.VMEM((ROWS, WIDE), BF16),
        pltpu.VMEM((ROWS, WIDE), BF16),
        pltpu.VMEM((HEADS, ROWS), F32),
        pltpu.VMEM((WIDE, DH), BF16),
        pltpu.VMEM((WIDE, DH), BF16),
        pltpu.VMEM((DH, WIDE), BF16),
        pltpu.VMEM((DH, WIDE), BF16),
        pltpu.VMEM((NY, NX, ROWS, DH), BF16),
        pltpu.VMEM((NY, NX, ROWS, DH), BF16),
        pltpu.VMEM((NY, SPAN, WIDE), F32),
        pltpu.VMEM((NY, SPAN, WIDE), F32),
        pltpu.VMEM((NY * NX, WIDE), F32),
        pltpu.VMEM((NY * NX, WIDE), F32),
        pltpu.VMEM((NY * NX, WIDE), F32),
        pltpu.VMEM((8, WIDE), F32),
        pltpu.VMEM((NY, SPAN, WIDE), BF16),
        pltpu.VMEM((NY, SPAN, WIDE), BF16),
        pltpu.VMEM((DH, WIDE), F32),
        pltpu.VMEM((DH, WIDE), F32),
        pltpu.VMEM((NX, ROWS, DH), F32),
        pltpu.VMEM((NY - 1, NX, ROWS, DH), BF16),
        pltpu.VMEM((NY - 1, NX, ROWS, DH), BF16),
        pltpu.VMEM((NY, NX, ROWS, DH), BF16),
        pltpu.VMEM((NY, NX - 1, ROWS, DH), BF16),
        pltpu.VMEM((NY - 1, ROWS, DH), BF16),
        pltpu.VMEM((NY - 1, ROWS, DH), BF16),
        pltpu.VMEM((ROWS, DH), F32),
        pltpu.VMEM((NX - 1, ROWS, DH), BF16),
        pltpu.VMEM((NX, ROWS, DH), BF16),
        pltpu.VMEM((HEADS, ROWS), F32),
        pltpu.VMEM((ROWS, WIDE), F32),
        pltpu.VMEM((4, ROWS, WIDE), F32),
        pltpu.VMEM((HEADS, 2 * DH + 48, DH), BF16),
        pltpu.VMEM((NX, 2 * DH + 48, DH), BF16),
        pltpu.VMEM((2, DH + 48, DH), BF16),
        pltpu.VMEM((NY, DH + 48, DH), BF16),
        pltpu.VMEM((DH, DH), F32),
        pltpu.VMEM((DH, DH), F32),
        pltpu.VMEM((NX, 2 * DH, DH), BF16),
        pltpu.VMEM((HEADS, 2 * DH, DH), BF16),
        dma((15,)),
        dma((8,)),
        dma((NX - 1,)), dma((NX - 1,)),
        dma((NY - 1, NX + 1)), dma((NY - 1, NX + 1)),
        dma((NY, NX - 1)), dma((NY, NX - 1)),
        dma((NX,)), dma((NX,)),
        dma((NY - 1,)), dma((NY - 1,)),
        dma((NX,)), dma((NX,)),
        dma((NY - 1, NX)), dma((NY - 1, NX)),
        dma((NY, NX - 1)), dma((NY, NX - 1)),
        dma((NY - 1,)), dma((NY - 1,)),
        dma((NX - 1,)), dma((NX - 1,)),
    ]
    hbm = pl.BlockSpec(memory_space=pltpu.HBM)
    room = 62 * 1024 * 1024
    shapes = (wide, wide, wide, wide, wide, wide, narrow, narrow)
    results = pl.pallas_call(
        kernel,
        out_shape=shapes,
        in_specs=[hbm] * 9,
        out_specs=(hbm,) * 8,
        scratch_shapes=scratch,
        compiler_params=pltpu.CompilerParams(
            collective_id=0, has_side_effects=True, vmem_limit_bytes=room
        ),
    )(q_light, k_light, v_light, g_light, log_decay.T, q_soft, k_soft, v_soft, g_soft)
    return pl.pallas_call(
        copy_out,
        out_shape=shapes,
        in_specs=[hbm] * 8,
        out_specs=(hbm,) * 8,
        scratch_shapes=[pltpu.VMEM(shape.shape, BF16) for shape in shapes] + [dma((2, 8))],
        compiler_params=pltpu.CompilerParams(vmem_limit_bytes=room),
    )(*results)


def solution(mesh):
    spec = P(("dp", "ctx"), "tp")
    return jax.shard_map(
        shards, mesh=mesh, in_specs=(spec,) * 9, out_specs=(spec,) * 8, check_vma=False
    )
```
